512 devices in a mesh: ens: 8 (over y), grid: 64 (over x, z, core).
Axes of the slice: x: 4, y: 8, z: 8, core: 2. Of those that a mesh axis runs over, the one named last changes fastest.
Arguments:
- hidden: bfloat16 [8, 65536, 1024], P('ens', 'grid'), may hold values from -6 to 6
- weight: bfloat16 [1024, 100], replicated, may hold values from -0.1875 to 0.1875
- target: float32 [100, 65536], P(None, 'grid'), may hold values from -6 to 6
- area_weight: float32 [65536], P('grid'), may hold values from 0.3 to 3
- var_weight: float32 [100], replicated, may hold values from 0.25 to 4
- edge_owner: int32 [65536, 3], P('grid'), may hold values from 0 to 63, all different within a row; in each aligned block of 1024 rows (0 to 1023, 1024 to 2047, ...) at most 60 rows name the same one
- edge_row: int32 [65536, 3], P('grid'), may hold values from 0 to 127
- edge_weight: float32 [65536, 3], P('grid'), may hold values from 0.05 to 1
Outputs:
- grad_weight: float32 [1024, 100], P('grid')
- latent_gradient: bfloat16 [8, 8192, 1024], P('ens', 'grid')
The draws below stay inside these ranges and needn't reach their ends.
Inputs may be any that keep to these rules, and one draw needn't show every extreme that they name: `edge_owner`: the 3 owners of one grid point differ; among the edges of the 1024 points of one device no owner appears more than 60 times, and some owner appears exactly 60 times.
All inputs are finite; a program needn't handle non-finite values.
Results may differ from the reference program's by a relative error of at most 0.0163.
Values may be sent and summed in bfloat16 or wider, within the bound.
A program may use at most 64 MiB of HBM per device.

```python
import math
import jax
import jax.numpy as jnp
import numpy as np
from jax import lax

LATENT = 1024
VARS = 100
NEIGH = 3
G_DEV = 1024
ENSEMBLE_SIZE = 8
MESH_DEV = 128
CAP = 60
NPTS = 65536
NMESH = 8192
N_GRID = 64


def set_ends(values, rng, smallest, largest):
    place = [jax.random.randint(jax.random.fold_in(rng, axis), (), 0, length) for axis, length in enumerate(values.shape)]
    widest = values.shape.index(max(values.shape))
    beside = place[:widest] + [(place[widest] + 1) % values.shape[widest]] + place[widest + 1:]
    return values.at[tuple(place)].set(smallest).at[tuple(beside)].set(largest)


def block_levels(own_key, extent, pieces, smallest, top_value):
    gain = 1.0
    for axis_at, blocks in pieces:
        heights = jax.random.uniform(jax.random.fold_in(jax.random.fold_in(own_key, 6), axis_at), (blocks,), jnp.float32, smallest / len(pieces), top_value / len(pieces))
        gain = gain * jnp.repeat(jnp.exp(heights), extent[axis_at] // blocks).reshape((-1,) + (1,) * (len(extent) - 1 - axis_at))
    return gain


def deal_out(rng, own, number, rows, count, top, limit, lean):
    order = jax.random.permutation(rng, count)
    packed, usual = load_shares(count, rows * top, limit, lean, True), load_shares(count, rows * top, limit, lean, False)
    places = jnp.arange(count)

    def named(tallies, rotation):
        used = int((tallies > 0).sum())
        fixed = max(1, used // 4)
        shifted = fixed + (places - fixed + rotation * (used - fixed)) % max(1, count - fixed)
        return jnp.zeros((count,), jnp.int32).at[order[jnp.where(places < fixed, places, shifted)]].set(jnp.asarray(tallies, jnp.int32))

    tallies = jnp.where(number % 4 == 0, named(packed, number // 4), named(usual, number - number // 4 - 1))
    mixed = jax.random.permutation(jax.random.fold_in(own, 3), count)
    giver, taker = mixed[0:count // 2 * 2:2], mixed[1:count // 2 * 2:2]
    slack = jnp.minimum(tallies[giver] - 1, limit - tallies[taker]) // 2
    slack = jnp.where((giver == order[0]) | (taker == order[0]) | (tallies[taker] == 0), 0, jnp.maximum(slack, 0))
    shifted = jax.random.randint(jax.random.fold_in(own, 4), (count // 2,), 0, 1 << 20) % (slack + 1)
    tallies = tallies.at[giver].add(-shifted).at[taker].add(shifted)
    members = jnp.searchsorted(jnp.cumsum(tallies), jnp.arange(rows * top), side="right").astype(jnp.int32)
    listing = members.reshape(top, rows).T
    listing = listing[jax.random.permutation(jax.random.fold_in(own, 1), rows)]
    rotation = jax.random.randint(jax.random.fold_in(own, 2), (rows, 1), 0, top)
    return jnp.take_along_axis(listing, (jnp.arange(top)[None, :] + rotation) % top, axis=1)


def load_shares(number_of, total, most, lean, full):
    portions = [(1 << 20) // math.isqrt(rank ** lean) + 1 for rank in range(1, number_of + 1)]
    largest = most if full else min(most, max(-(-total // number_of), total * portions[0] // sum(portions)))
    least = 1 if total - largest >= number_of - 1 else 0
    given, rest = [largest] + [least] * (number_of - 1), total - largest - least * (number_of - 1)
    while rest > 0:
        movable = [i for i in range(1, number_of) if given[i] < largest] or [i for i in range(1, number_of) if given[i] < most]
        mass, budget = sum([portions[i] for i in movable]), rest
        for i in movable:
            more = min(most - given[i], max(1, budget * portions[i] // mass), rest)
            given[i] = given[i] + more
            rest = rest - more
    return np.array(given)


def scatter_about(own_key, extent, width, reach, split=(), kind=jnp.bfloat16):
    array = jax.random.normal(own_key, extent, jnp.float32) * width
    if len(split) > 0:
        array = block_levels(own_key, extent, split, -0.22, 0.18) * array
    return jnp.clip(array, min=-reach, max=reach).astype(kind)


def setup_inputs(seed: int = 0) -> dict:
    streams_of = jax.random.split(jax.random.key(seed), 9)
    hidden = scatter_about(streams_of[0], (ENSEMBLE_SIZE, NPTS, LATENT), 1.0, 6.0, ((0, 8), (1, 64)))
    weight = scatter_about(streams_of[1], (LATENT, VARS), LATENT ** -0.5, 0.1875)
    target = scatter_about(streams_of[2], (VARS, NPTS), 1.0, 6.0, ((1, 64),), jnp.float32)
    area_weight = jnp.clip(jnp.exp(math.log(3.0) - 2.3025851 * jax.random.uniform(streams_of[3], (NPTS,), jnp.float32) ** block_levels(streams_of[3], (NPTS,), ((0, 64),), -0.2, 0.2)), 0.3, 3.0)
    var_weight = jnp.clip(jnp.exp(jax.random.uniform(streams_of[4], (VARS,), jnp.float32, math.log(0.25), math.log(4.0))), 0.25, 4.0)
    edge_owner_keys = jax.random.split(jax.random.fold_in(streams_of[5], 1), NPTS // G_DEV)
    edge_owner_turns = jax.random.permutation(jax.random.fold_in(streams_of[5], 3), NPTS // G_DEV)
    edge_owner = jax.vmap(lambda own, number: deal_out(jax.random.fold_in(streams_of[5], 2), own, number, G_DEV, N_GRID, NEIGH, CAP, 2))(edge_owner_keys, edge_owner_turns).reshape((NPTS, NEIGH))
    edge_row = set_ends(jax.random.randint(streams_of[6], (NPTS, NEIGH), 0, MESH_DEV), jax.random.fold_in(streams_of[6], 1), 0, MESH_DEV - 1).astype(jnp.int32)
    edge_weight = jnp.clip(0.05 + 0.95 * jax.random.uniform(streams_of[7], (NPTS, NEIGH), jnp.float32) ** block_levels(streams_of[7], (NPTS, NEIGH), ((0, 64),), -0.2, 0.2), 0.05, 1.0)
    return {"hidden": hidden, "weight": weight, "target": target, "area_weight": area_weight, "var_weight": var_weight, "edge_owner": edge_owner, "edge_row": edge_row, "edge_weight": edge_weight}


smooth_width = 0.1

def softened_sign(difference):
    return difference * lax.rsqrt(difference * difference + smooth_width * smooth_width)

def score_parts(current_member, prediction_stack, truth_field, member_stack):
    pairwise_total = jnp.zeros_like(current_member)
    for other_member in range(member_stack):
        pairwise_total = pairwise_total + softened_sign(current_member - prediction_stack[other_member])
    return softened_sign(current_member - truth_field) / member_stack - pairwise_total / (member_stack * (member_stack - 1))

def reference(hidden, weight, target, area_weight, var_weight, edge_owner, edge_row, edge_weight):
    weight_wide = weight.astype(jnp.float32)

    def decode_grid(member_rows):
        return jnp.dot(member_rows.astype(jnp.float32), weight_wide, preferred_element_type=jnp.float32).T
    prediction_stack = lax.map(decode_grid, hidden)
    location_scale = area_weight[None, :] * var_weight[:, None]
    mesh_index = (edge_owner * MESH_DEV + edge_row).reshape(-1).astype(jnp.int32)
    weight_turned = weight_wide.T

    def member_reverse(inputs):
        member_rows, member_prediction = inputs
        prediction_gradient = (location_scale * score_parts(member_prediction, prediction_stack, target, ENSEMBLE_SIZE)).astype(jnp.bfloat16)
        gradient_wide = prediction_gradient.astype(jnp.float32)
        weight_term = jnp.dot(member_rows.astype(jnp.float32).T, gradient_wide.T, preferred_element_type=jnp.float32)
        messages = (edge_weight[:, :, None] * gradient_wide.T[:, None, :]).astype(jnp.bfloat16).reshape(-1, VARS)
        mesh_sum = jnp.zeros((NMESH, VARS), jnp.float32).at[mesh_index].add(messages.astype(jnp.float32)).astype(jnp.bfloat16)
        mesh_grad = jnp.dot(mesh_sum.astype(jnp.float32), weight_turned, preferred_element_type=jnp.float32)
        return (weight_term, mesh_grad.astype(jnp.bfloat16))
    weight_pieces, latent_gradient = lax.map(member_reverse, (hidden, prediction_stack))
    normalizer = 1.0 / math.sqrt(float(NPTS * ENSEMBLE_SIZE))
    grad_weight = lax.optimization_barrier(jnp.sum(weight_pieces, axis=0)) * normalizer
    return (grad_weight, latent_gradient)
```

```python
import functools
import math

import jax
import jax.numpy as jnp
from jax import lax
from jax.experimental import pallas as pl
from jax.experimental.pallas import tpu as pltpu
from jax.sharding import PartitionSpec as P

smooth_width = 0.1
LANES = 128
VMEM_LIMIT = 40 * 1024 * 1024


def softened_sign(difference):
    return difference * lax.rsqrt(difference * difference + smooth_width * smooth_width)


def round_up(n, m):
    return (n + m - 1) // m * m


def forecast_kernel(wt_ref, hidden_ref, out_ref):
    out_ref[0] = lax.dot_general(
        wt_ref[...], hidden_ref[...], (((1,), (1,)), ((), ())), preferred_element_type=jnp.float32
    )


def score_block(x, t, scale):
    n = len(x)
    total = [None] * n
    for i in range(n):
        for j in range(i + 1, n):
            a = softened_sign(x[i] - x[j])
            total[i] = a if total[i] is None else total[i] + a
            total[j] = -a if total[j] is None else total[j] - a
    out = []
    for i in range(n):
        raw = softened_sign(x[i] - t) * (1.0 / n) - total[i] * (1.0 / (n * (n - 1)))
        out.append((scale * raw).astype(jnp.bfloat16))
    return out


def score_kernel(x_ref, t_ref, s_ref, g_ref):
    n, rows, _ = x_ref.shape
    for r in range(0, g_ref.shape[1], 16):
        here = min(16, rows - r)
        if here <= 0:
            g_ref[:, r : r + 16, :] = jnp.zeros((n, 16, LANES), jnp.bfloat16)
            continue
        got = score_block(
            [x_ref[m, r : r + here, :] for m in range(n)],
            t_ref[r : r + here, :],
            s_ref[r : r + here, :],
        )
        for m in range(n):
            g_ref[m, r : r + here, :] = got[m]
            if here < 16:
                g_ref[m, r + here : r + 16, :] = jnp.zeros((16 - here, LANES), jnp.bfloat16)


def place_slots(own_ref, row_ref, ew_ref, slot_s, w_s, r_s):
    owners, points = slot_s.shape
    neigh = own_ref.shape[0]
    tri = (
        lax.broadcasted_iota(jnp.int32, (LANES, LANES), 0)
        <= lax.broadcasted_iota(jnp.int32, (LANES, LANES), 1)
    ).astype(jnp.float32).astype(jnp.bfloat16)
    owner_id = lax.broadcasted_iota(jnp.int32, (owners, LANES), 0)
    carry = jnp.zeros((owners, 1), jnp.float32)
    for b in range(0, points, LANES):
        hit = jnp.zeros((owners, LANES), jnp.float32)
        w = jnp.zeros((owners, LANES), jnp.float32)
        row = jnp.zeros((owners, LANES), jnp.float32)
        for k in range(neigh):
            same = own_ref[k : k + 1, b : b + LANES] == owner_id
            hit = jnp.where(same, 1.0, hit)
            w = jnp.where(same, ew_ref[k : k + 1, b : b + LANES], w)
            row = jnp.where(same, row_ref[k : k + 1, b : b + LANES].astype(jnp.float32), row)
        count = carry + jnp.dot(hit.astype(jnp.bfloat16), tri, preferred_element_type=jnp.float32)
        slot_s[:, b : b + LANES] = jnp.where(hit > 0.0, count, 0.0)
        w_s[:, b : b + LANES] = w
        r_s[:, b : b + LANES] = row
        carry = count[:, LANES - 1 : LANES]


def message_kernel(
    variables, slots, group, g_ref, own_ref, row_ref, ew_ref, hidden_ref, out_ref, gw_ref, slot_s, w_s, r_s, gt_s, a_s
):
    owners, points = slot_s.shape
    slabs, grows, _ = g_ref.shape
    place_slots(own_ref, row_ref, ew_ref, slot_s, w_s, r_s)
    pad = jnp.zeros((LANES - grows, LANES), jnp.float32)
    for s in range(slabs):
        block = jnp.concatenate([g_ref[s].astype(jnp.float32), pad], axis=0)
        gt_s[s * LANES : (s + 1) * LANES, :] = block.T.astype(jnp.bfloat16)
    wide = jnp.concatenate([g_ref[s] for s in range(slabs)], axis=1)
    latent = hidden_ref.shape[1]
    for b in range(0, latent, 2 * LANES):
        part = jnp.dot(wide, hidden_ref[:, b : b + 2 * LANES], preferred_element_type=jnp.float32)
        for c in range(0, 2 * LANES, LANES):
            gw_ref[b + c : b + c + LANES, :] = jnp.concatenate([part[:, c : c + LANES], pad], axis=0).T
    want = lax.broadcasted_iota(jnp.int32, (slots, points), 0).astype(jnp.float32) + 1.0
    lane = lax.broadcasted_iota(jnp.int32, (slots, LANES), 1)

    def body(i, _):
        w_col, r_col = [], []
        base = pl.multiple_of(i * group, group)
        slot_g = slot_s[pl.ds(base, group), :]
        w_g = w_s[pl.ds(base, group), :]
        r_g = r_s[pl.ds(base, group), :]
        for j in range(group):
            same = slot_g[j : j + 1, :] == want
            a_s[j * slots : (j + 1) * slots, :] = jnp.where(same, 1.0, 0.0).astype(jnp.bfloat16)
            w_col.append(jnp.sum(jnp.where(same, w_g[j : j + 1, :], 0.0), axis=1, keepdims=True))
            r_col.append(jnp.sum(jnp.where(same, r_g[j : j + 1, :], 0.0), axis=1, keepdims=True))
        picked = jnp.dot(a_s[...], gt_s[...], preferred_element_type=jnp.float32)
        for j in range(group):
            message = picked[j * slots : (j + 1) * slots, :] * w_col[j]
            message = jnp.where(lane == variables, r_col[j], message)
            out_ref[pl.ds(pl.multiple_of((base + j) * slots, 16), slots), :] = message.astype(jnp.bfloat16)
        return 0

    lax.fori_loop(0, owners // group, body, 0)


def mesh_kernel(variables, in_ref, w_ref, out_ref):
    total = in_ref.shape[0]
    mesh_rows = out_ref.shape[0]
    pick = (lax.broadcasted_iota(jnp.int32, (16, LANES), 1) == variables).astype(jnp.float32).astype(jnp.bfloat16)
    acc = jnp.zeros((mesh_rows, LANES), jnp.float32)
    step = min(1024, total)
    ids = lax.broadcasted_iota(jnp.int32, (mesh_rows, step), 0).astype(jnp.float32)
    for b in range(0, total, step):
        block = in_ref[b : b + step, :]
        row = lax.dot_general(pick, block, (((1,), (1,)), ((), ())), preferred_element_type=jnp.float32)
        picker = jnp.where(row[0:1, :] == ids, 1.0, 0.0).astype(jnp.bfloat16)
        acc = acc + jnp.dot(picker, block, preferred_element_type=jnp.float32)
    mesh_sum = acc.astype(jnp.bfloat16)
    out_ref[...] = lax.dot_general(
        mesh_sum, w_ref[...], (((1,), (1,)), ((), ())), preferred_element_type=jnp.float32
    ).astype(jnp.bfloat16)


def per_device(hidden, weight, target, area_weight, var_weight, edge_owner, edge_row, edge_weight):
    rows = hidden[0]
    points, latent = rows.shape
    variables = weight.shape[1]
    neigh = edge_owner.shape[1]
    members = lax.axis_size("ens")
    owners = lax.axis_size("grid")
    mesh_rows = points // 8
    slab = points // members
    assert slab == LANES and variables < LANES
    capacity = max(2, (5 * points * neigh + 4 * owners - 1) // (4 * owners))
    slots = round_up(capacity, 16)
    xrows, grows = round_up(variables, 8), round_up(variables, 16)
    group = min(8, owners)
    params = pltpu.CompilerParams(vmem_limit_bytes=VMEM_LIMIT)
    vmem = pl.BlockSpec(memory_space=pltpu.VMEM)

    wt = jnp.pad(weight.T, ((0, xrows - variables), (0, 0)))
    x = pl.pallas_call(
        forecast_kernel,
        grid=(members,),
        in_specs=[
            pl.BlockSpec((xrows, latent), lambda i: (0, 0)),
            pl.BlockSpec((slab, latent), lambda i: (i, 0)),
        ],
        out_specs=pl.BlockSpec((1, xrows, slab), lambda i: (i, 0, 0)),
        out_shape=jax.ShapeDtypeStruct((members, xrows, slab), jnp.float32),
        compiler_params=params,
    )(wt, rows)
    x = lax.all_to_all(x, "ens", split_axis=0, concat_axis=0, tiled=True)
    first = lax.axis_index("ens") * slab
    truth = jnp.pad(
        lax.dynamic_slice_in_dim(target, first, slab, 1), ((0, xrows - variables), (0, 0))
    )
    area = lax.dynamic_slice_in_dim(area_weight, first, slab, 0)
    scale = area[None, :] * jnp.pad(var_weight, (0, xrows - variables))[:, None]
    g = pl.pallas_call(
        score_kernel,
        in_specs=[vmem] * 3,
        out_specs=vmem,
        out_shape=jax.ShapeDtypeStruct((members, grows, slab), jnp.bfloat16),
        compiler_params=params,
    )(x, truth, scale)
    g = lax.all_to_all(g, "ens", split_axis=0, concat_axis=0, tiled=True)
    outgoing, gw = pl.pallas_call(
        functools.partial(message_kernel, variables, slots, group),
        in_specs=[vmem] * 5,
        out_specs=[vmem] * 2,
        out_shape=[
            jax.ShapeDtypeStruct((owners * slots, LANES), jnp.bfloat16),
            jax.ShapeDtypeStruct((latent, LANES), jnp.float32),
        ],
        scratch_shapes=[
            pltpu.VMEM((owners, points), jnp.float32),
            pltpu.VMEM((owners, points), jnp.float32),
            pltpu.VMEM((owners, points), jnp.float32),
            pltpu.VMEM((points, LANES), jnp.bfloat16),
            pltpu.VMEM((group * slots, points), jnp.bfloat16),
        ],
        compiler_params=params,
    )(g, edge_owner.T, edge_row.T, edge_weight.T, rows)
    incoming = lax.all_to_all(
        outgoing.reshape(owners, slots, LANES), "grid", split_axis=0, concat_axis=0, tiled=True
    )
    share = latent // (owners * members)
    gw = gw.reshape(owners, members, share, LANES).transpose(1, 0, 2, 3)
    gw = jnp.sum(lax.all_to_all(gw, "ens", split_axis=0, concat_axis=0, tiled=True), axis=0)
    gw = jnp.sum(lax.all_to_all(gw, "grid", split_axis=0, concat_axis=0, tiled=True), axis=0)
    normalizer = 1.0 / math.sqrt(float(points * owners * members))
    gw = jnp.broadcast_to((gw * normalizer)[None], (members, share, LANES))
    gw = lax.all_to_all(gw, "ens", split_axis=0, concat_axis=0, tiled=True)
    grad_weight = gw.reshape(members * share, LANES)[:, :variables]
    mesh_grad = pl.pallas_call(
        functools.partial(mesh_kernel, variables),
        in_specs=[vmem] * 2,
        out_specs=vmem,
        out_shape=jax.ShapeDtypeStruct((mesh_rows, latent), jnp.bfloat16),
        compiler_params=params,
    )(incoming.reshape(owners * slots, LANES), jnp.pad(weight, ((0, 0), (0, LANES - variables))))
    return grad_weight, mesh_grad[None]


def solution(mesh):
    return jax.shard_map(
        per_device,
        mesh=mesh,
        in_specs=(
            P("ens", "grid", None),
            P(),
            P(None, "grid"),
            P("grid"),
            P(),
            P("grid", None),
            P("grid", None),
            P("grid", None),
        ),
        out_specs=(P("grid", None), P("ens", "grid", None)),
        check_vma=False,
    )
```

```python
import functools
import math

import jax
import jax.numpy as jnp
from jax import lax
from jax.experimental import pallas as pl
from jax.experimental.pallas import tpu as pltpu
from jax.sharding import PartitionSpec as P

smooth_width = 0.1
LANES = 128
VMEM_LIMIT = 40 * 1024 * 1024


def softened_sign(difference):
    return difference * lax.rsqrt(difference * difference + smooth_width * smooth_width)


def round_up(n, m):
    return (n + m - 1) // m * m


def score_block(x, t, scale):
    n = len(x)
    total = [None] * n
    for i in range(n):
        for j in range(i + 1, n):
            a = softened_sign(x[i] - x[j])
            total[i] = a if total[i] is None else total[i] + a
            total[j] = -a if total[j] is None else total[j] - a
    out = []
    for i in range(n):
        raw = softened_sign(x[i] - t) * (1.0 / n) - total[i] * (1.0 / (n * (n - 1)))
        out.append((scale * raw).astype(jnp.bfloat16))
    return out


def place_slots(own_ref, row_ref, ew_ref, slot_s, w_s, r_s):
    owners, points = slot_s.shape
    neigh = own_ref.shape[0]
    tri = (
        lax.broadcasted_iota(jnp.int32, (LANES, LANES), 0)
        <= lax.broadcasted_iota(jnp.int32, (LANES, LANES), 1)
    ).astype(jnp.float32).astype(jnp.bfloat16)
    owner_id = lax.broadcasted_iota(jnp.int32, (owners, LANES), 0)
    carry = jnp.zeros((owners, 1), jnp.float32)
    for b in range(0, points, LANES):
        hit = jnp.zeros((owners, LANES), jnp.float32)
        w = jnp.zeros((owners, LANES), jnp.float32)
        row = jnp.zeros((owners, LANES), jnp.float32)
        for k in range(neigh):
            same = own_ref[k : k + 1, b : b + LANES] == owner_id
            hit = jnp.where(same, 1.0, hit)
            w = jnp.where(same, ew_ref[k : k + 1, b : b + LANES], w)
            row = jnp.where(same, row_ref[k : k + 1, b : b + LANES].astype(jnp.float32), row)
        count = carry + jnp.dot(hit.astype(jnp.bfloat16), tri, preferred_element_type=jnp.float32)
        slot_s[:, b : b + LANES] = jnp.where(hit > 0.0, count, 0.0)
        w_s[:, b : b + LANES] = w
        r_s[:, b : b + LANES] = row
        carry = count[:, LANES - 1 : LANES]


def bulk_wait(ref, sem):
    pltpu.make_async_copy(ref, ref, sem).wait()


def fused_kernel(
    cfg,
    hidden_hbm, wt_hbm, target_hbm, area_hbm, var_hbm, own_hbm, row_hbm, ew_hbm,
    gw_out, mesh_out,
    hid, wt_raw, target, area, var, own, row, ew,
    wt, w_col, x_send, x_recv, g_send, g_recv,
    slot_s, w_s, r_s, a_s, wb_s, gt_s, out_buf, in_buf,
    gw_s, gw_send, gw_recv, q_s, q_send, q_recv, r_send, r_recv,
    in_sem, x_ss, x_rs, g_ss, g_rs, m_ss, m_rs, w_ss, w_rs, q_ss, q_rs, r_ss, r_rs,
):
    variables, slots, group, share, normalizer = cfg
    members, xrows, slab = x_send.shape
    grows = g_send.shape[1]
    owners, points = slot_s.shape
    latent = hid.shape[1]
    mesh_rows = mesh_out.shape[0]
    e, g = lax.axis_index("ens"), lax.axis_index("grid")

    def send(src, dst, ss, rs, axis, peer, me):
        @pl.when(peer != me)
        def _():
            pltpu.make_async_remote_copy(
                src_ref=src, dst_ref=dst, send_sem=ss, recv_sem=rs,
                device_id={axis: peer}, device_id_type=pl.DeviceIdType.MESH,
            ).start()

        @pl.when(peer == me)
        def _():
            pltpu.make_async_copy(src, dst, rs).start()

    barrier = pltpu.get_barrier_semaphore()

    def greet_ens(i, _):
        pl.semaphore_signal(barrier, inc=1, device_id={"ens": lax.rem(e + i, members)}, device_id_type=pl.DeviceIdType.MESH)
        return 0

    def greet_grid(i, _):
        pl.semaphore_signal(barrier, inc=1, device_id={"grid": lax.rem(g + i, owners)}, device_id_type=pl.DeviceIdType.MESH)
        return 0

    chunk = 2 * slab
    loads = [pltpu.make_async_copy(wt_hbm, wt_raw, in_sem.at[0])]
    for c in range(points // chunk):
        rows = pl.ds(c * chunk, chunk)
        loads.append(pltpu.make_async_copy(hidden_hbm.at[rows], hid.at[rows], in_sem.at[1 + c]))
    n_hid = len(loads)
    loads.append(
        pltpu.make_async_copy(
            target_hbm.at[:, pl.ds(pl.multiple_of(e * slab, slab), slab)], target, in_sem.at[n_hid]
        )
    )
    for i, (s, d) in enumerate(((area_hbm, area), (var_hbm, var), (own_hbm, own), (row_hbm, row), (ew_hbm, ew))):
        loads.append(pltpu.make_async_copy(s, d, in_sem.at[n_hid + 1 + i]))
    for cp in loads:
        cp.start()
    lax.fori_loop(1, members, greet_ens, 0)
    lax.fori_loop(1, owners, greet_grid, 0)

    loads[0].wait()
    whole = variables // 16 * 16
    wt[0:whole, :] = wt_raw[0:whole, :]
    wt[whole : whole + 16, :] = jnp.concatenate(
        [wt_raw[whole:variables, :], jnp.zeros((whole + 16 - variables, latent), jnp.bfloat16)], axis=0
    )
    wt[whole + 16 :, :] = jnp.zeros((LANES - whole - 16, latent), jnp.bfloat16)
    for b in range(0, latent, LANES):
        w_col[b : b + LANES, :] = wt[:, b : b + LANES].astype(jnp.float32).T.astype(jnp.bfloat16)

    for c in range(points // chunk):
        loads[1 + c].wait()
        part = jnp.dot(hid[c * chunk : (c + 1) * chunk, :], w_col[...], preferred_element_type=jnp.float32)
        for s in range(2):
            x_send[2 * c + s] = part[s * slab : (s + 1) * slab, :].T[:xrows, :]
        if c == 0:
            pl.semaphore_wait(barrier, members + owners - 2)
        for s in range(2):
            m = 2 * c + s
            send(x_send.at[m], x_recv.at[e], x_ss, x_rs, "ens", m, e)

    for cp in loads[n_hid:]:
        cp.wait()
    place_slots(own, row, ew, slot_s, w_s, r_s)
    want = lax.broadcasted_iota(jnp.int32, (slots, points), 0).astype(jnp.float32) + 1.0
    lane = lax.broadcasted_iota(jnp.int32, (slots, LANES), 1)

    def one_hot(o, _):
        same = slot_s[pl.ds(o, 1), :] == want
        at = pl.ds(pl.multiple_of(o * slots, slots), slots)
        a_s[at, :] = jnp.where(same, 1.0, 0.0).astype(jnp.bfloat16)
        w = jnp.sum(jnp.where(same, w_s[pl.ds(o, 1), :], 0.0), axis=1, keepdims=True)
        r = jnp.sum(jnp.where(same, r_s[pl.ds(o, 1), :], 0.0), axis=1, keepdims=True)
        wb_s[at, :] = jnp.where(lane == variables, r, w)
        return 0

    lax.fori_loop(0, owners, one_hot, 0)
    vcol = jnp.broadcast_to(
        jnp.concatenate([var[...], jnp.zeros((1, LANES - variables), jnp.float32)], axis=1), (LANES, LANES)
    ).T
    scale = vcol * area[pl.ds(e, 1), :]
    q_s[...] = scale

    bulk_wait(x_recv, x_rs)

    def score(r, rows, trows):
        at = pl.ds(r, rows)
        t = target[pl.ds(r, trows), :]
        if trows < rows:
            t = jnp.concatenate([t, jnp.zeros((rows - trows, slab), jnp.float32)], axis=0)
        got = score_block([x_recv[m, at, :] for m in range(members)], t, q_s[at, :])
        for m in range(members):
            v = got[m]
            if rows < 16:
                v = jnp.concatenate([v, jnp.zeros((16 - rows, slab), jnp.bfloat16)], axis=0)
            g_send[m, pl.ds(r, 16), :] = v

    def score_step(i, _):
        score(pl.multiple_of(i * 16, 16), 16, 16)
        return 0

    lax.fori_loop(0, variables // 16, score_step, 0)
    if variables % 16:
        score(whole, xrows - whole, variables - whole)
    for m in range(members):
        send(g_send.at[m], g_recv.at[e], g_ss, g_rs, "ens", m, e)

    bulk_wait(g_recv, g_rs)
    pad = jnp.zeros((LANES - grows, LANES), jnp.float32)
    lane = lax.broadcasted_iota(jnp.int32, (LANES, LANES), 1)
    for s in range(members):
        block = jnp.concatenate([g_recv[s].astype(jnp.float32), pad], axis=0).T
        gt_s[s * LANES : (s + 1) * LANES, :] = jnp.where(lane == variables, 1.0, block).astype(jnp.bfloat16)
    groups = owners // group
    blocks = m_rs.shape[0]

    def messages(t, _):
        at = lax.rem(g // group + 1 + t, groups)
        rows = pl.ds(pl.multiple_of(at * (group * slots), group * slots), group * slots)
        picked = jnp.dot(a_s[rows, :], gt_s[...], preferred_element_type=jnp.float32)
        out_buf[rows, :] = (picked * wb_s[rows, :]).astype(jnp.bfloat16)
        for j in range(group):
            o = at * group + j
            send(
                out_buf.at[pl.ds(pl.multiple_of(o * slots, slots), slots)],
                in_buf.at[pl.ds(pl.multiple_of(g * slots, slots), slots)],
                m_ss, m_rs.at[g // (owners // blocks)], "grid", o, g,
            )
        return 0

    lax.fori_loop(0, groups, messages, 0)

    wide = jnp.concatenate([g_recv[s] for s in range(members)], axis=1)
    for b in range(0, latent, 2 * LANES):
        part = jnp.dot(wide, hid[:, b : b + 2 * LANES], preferred_element_type=jnp.float32)
        for c in range(0, 2 * LANES, LANES):
            gw_s[b + c : b + c + LANES, :] = jnp.concatenate([part[:, c : c + LANES], pad], axis=0).T
    for m in range(members):
        for i in range(share):
            gw_send[m, pl.ds(i, owners, share), :] = gw_s[pl.ds(share * m + i, owners, share * members), :]
        send(gw_send.at[m], gw_recv.at[e], w_ss, w_rs, "ens", m, e)
    bulk_wait(gw_recv, w_rs)
    total = gw_recv[0]
    for m in range(1, members):
        total = total + gw_recv[m]
    q_s[0 : owners * share, :] = total

    def spread(i, _):
        o = lax.rem(g + i, owners)
        q_send[o] = q_s[pl.ds(o * share, share), :]
        send(q_send.at[o], q_recv.at[g], q_ss, q_rs, "grid", o, g)
        return 0

    lax.fori_loop(0, owners, spread, 0)

    step = in_buf.shape[0] // blocks
    pick = (lax.broadcasted_iota(jnp.int32, (16, LANES), 1) == variables).astype(jnp.float32).astype(jnp.bfloat16)
    ids = lax.broadcasted_iota(jnp.int32, (mesh_rows, step), 0).astype(jnp.float32)
    acc = jnp.zeros((mesh_rows, LANES), jnp.float32)
    for b in range(blocks):
        rows = pl.ds(b * step, step)
        bulk_wait(in_buf.at[rows], m_rs.at[b])
        block = in_buf[rows, :]
        place = lax.dot_general(pick, block, (((1,), (1,)), ((), ())), preferred_element_type=jnp.float32)
        picker = jnp.where(place[0:1, :] == ids, 1.0, 0.0).astype(jnp.bfloat16)
        acc = acc + jnp.dot(picker, block, preferred_element_type=jnp.float32)

    bulk_wait(q_recv, q_rs)
    r_send[...] = jnp.sum(q_recv[...], axis=0) * normalizer
    for m in range(members):
        send(r_send, r_recv.at[e], r_ss, r_rs, "ens", m, e)
    mesh_out[...] = jnp.dot(
        acc.astype(jnp.bfloat16), wt[...], preferred_element_type=jnp.float32
    ).astype(jnp.bfloat16)
    bulk_wait(r_recv, r_rs)
    for m in range(members):
        gw_out[share * m : share * (m + 1), :] = r_recv[m, :, 0:variables]

    bulk_wait(x_send.at[pl.ds(0, members - 1)], x_ss)
    bulk_wait(g_send.at[pl.ds(0, members - 1)], g_ss)
    bulk_wait(out_buf.at[pl.ds(0, (owners - 1) * slots)], m_ss)
    bulk_wait(gw_send.at[pl.ds(0, members - 1)], w_ss)
    bulk_wait(q_send.at[pl.ds(0, owners - 1)], q_ss)
    bulk_wait(r_recv.at[pl.ds(0, members - 1)], r_ss)


def per_device(hidden, weight, target, area_weight, var_weight, edge_owner, edge_row, edge_weight):
    rows = hidden[0]
    points, latent = rows.shape
    variables = weight.shape[1]
    neigh = edge_owner.shape[1]
    members = lax.axis_size("ens")
    owners = lax.axis_size("grid")
    mesh_rows = points // 8
    slab = points // members
    assert slab == LANES and variables < LANES
    capacity = max(2, (5 * points * neigh + 4 * owners - 1) // (4 * owners))
    slots = round_up(capacity, 16)
    xrows, grows = round_up(variables, 8), round_up(variables, 16)
    group = min(8, owners)
    share = latent // (owners * members)
    normalizer = 1.0 / math.sqrt(float(points * owners * members))
    f32, bf16, i32 = jnp.float32, jnp.bfloat16, jnp.int32
    any_space = pl.BlockSpec(memory_space=pl.ANY)
    vmem = pl.BlockSpec(memory_space=pltpu.VMEM)
    dma = pltpu.SemaphoreType.DMA
    grad_weight, mesh_grad = pl.pallas_call(
        functools.partial(fused_kernel, (variables, slots, group, share, normalizer)),
        in_specs=[any_space] * 8,
        out_specs=[vmem] * 2,
        out_shape=[
            jax.ShapeDtypeStruct((members * share, variables), f32),
            jax.ShapeDtypeStruct((mesh_rows, latent), bf16),
        ],
        scratch_shapes=[
            pltpu.VMEM((points, latent), bf16),
            pltpu.VMEM((variables, latent), bf16),
            pltpu.VMEM((variables, slab), f32),
            pltpu.VMEM((points // LANES, LANES), f32),
            pltpu.VMEM((1, variables), f32),
            pltpu.VMEM((neigh, points), i32),
            pltpu.VMEM((neigh, points), i32),
            pltpu.VMEM((neigh, points), f32),
            pltpu.VMEM((LANES, latent), bf16),
            pltpu.VMEM((latent, LANES), bf16),
            pltpu.VMEM((members, xrows, slab), f32),
            pltpu.VMEM((members, xrows, slab), f32),
            pltpu.VMEM((members, grows, slab), bf16),
            pltpu.VMEM((members, grows, slab), bf16),
            pltpu.VMEM((owners, points), f32),
            pltpu.VMEM((owners, points), f32),
            pltpu.VMEM((owners, points), f32),
            pltpu.VMEM((owners * slots, points), bf16),
            pltpu.VMEM((owners * slots, LANES), f32),
            pltpu.VMEM((points, LANES), bf16),
            pltpu.VMEM((owners * slots, LANES), bf16),
            pltpu.VMEM((owners * slots, LANES), bf16),
            pltpu.VMEM((latent, LANES), f32),
            pltpu.VMEM((members, owners * share, LANES), f32),
            pltpu.VMEM((members, owners * share, LANES), f32),
            pltpu.VMEM((max(LANES, owners * share), LANES), f32),
            pltpu.VMEM((owners, share, LANES), f32),
            pltpu.VMEM((owners, share, LANES), f32),
            pltpu.VMEM((share, LANES), f32),
            pltpu.VMEM((members, share, LANES), f32),
            dma((7 + points // (2 * slab),)),
            dma(()), dma(()), dma(()), dma(()), dma(()), dma((min(4, owners),)),
            dma(()), dma(()), dma(()), dma(()), dma(()), dma(()),
        ],
        compiler_params=pltpu.CompilerParams(
            collective_id=0, has_side_effects=True, vmem_limit_bytes=VMEM_LIMIT
        ),
    )(
        rows, weight.T, target, area_weight.reshape(points // LANES, LANES), var_weight.reshape(1, variables),
        edge_owner.T, edge_row.T, edge_weight.T,
    )
    return grad_weight, mesh_grad[None]


def solution(mesh):
    return jax.shard_map(
        per_device,
        mesh=mesh,
        in_specs=(
            P("ens", "grid", None),
            P(),
            P(None, "grid"),
            P("grid"),
            P(),
            P("grid", None),
            P("grid", None),
            P("grid", None),
        ),
        out_specs=(P("grid", None), P("ens", "grid", None)),
        check_vma=False,
    )
```

```python
import functools
import math

import jax
import jax.numpy as jnp
from jax import lax
from jax.experimental import pallas as pl
from jax.experimental.pallas import tpu as pltpu
from jax.sharding import PartitionSpec as P

smooth_width = 0.1
LANES = 128
VMEM_LIMIT = 62 * 1024 * 1024


def softened_sign(difference):
    return difference * lax.rsqrt(difference * difference + smooth_width * smooth_width)


def round_up(n, m):
    return (n + m - 1) // m * m


def score_block(x, t, scale):
    n = len(x)
    total = [None] * n
    for i in range(n):
        for j in range(i + 1, n):
            a = softened_sign(x[i] - x[j])
            total[i] = a if total[i] is None else total[i] + a
            total[j] = -a if total[j] is None else total[j] - a
    out = []
    for i in range(n):
        raw = softened_sign(x[i] - t) * (1.0 / n) - total[i] * (1.0 / (n * (n - 1)))
        out.append((scale * raw).astype(jnp.bfloat16))
    return out


def grid_shape(owners):
    return (owners // 16, 8, 2) if owners >= 16 else (owners // 4, 2, 2)


def place_slots(own_ref, row_ref, ew_ref, slot_s, w_s, r_s):
    owners, points = slot_s.shape
    neigh = own_ref.shape[0]
    tri = (
        lax.broadcasted_iota(jnp.int32, (LANES, LANES), 0)
        <= lax.broadcasted_iota(jnp.int32, (LANES, LANES), 1)
    ).astype(jnp.float32).astype(jnp.bfloat16)
    nx, nz, nc = grid_shape(owners)
    at = lax.broadcasted_iota(jnp.int32, (owners, LANES), 0)
    z_id = lax.shift_right_logical(at, int(math.log2(nx * nc)))
    x_id = jnp.bitwise_and(lax.shift_right_logical(at, int(math.log2(nc))), nx - 1)
    owner_id = (x_id * nz + z_id) * nc + jnp.bitwise_and(at, nc - 1)
    carry = jnp.zeros((owners, 1), jnp.float32)
    for b in range(0, points, LANES):
        hit = jnp.zeros((owners, LANES), jnp.float32)
        w = jnp.zeros((owners, LANES), jnp.float32)
        row = jnp.zeros((owners, LANES), jnp.float32)
        for k in range(neigh):
            same = own_ref[k : k + 1, b : b + LANES] == owner_id
            hit = jnp.where(same, 1.0, hit)
            w = jnp.where(same, ew_ref[k : k + 1, b : b + LANES], w)
            row = jnp.where(same, row_ref[k : k + 1, b : b + LANES].astype(jnp.float32), row)
        count = carry + jnp.dot(hit.astype(jnp.bfloat16), tri, preferred_element_type=jnp.float32)
        slot_s[:, b : b + LANES] = jnp.where(hit > 0.0, count, 0.0)
        w_s[:, b : b + LANES] = w
        r_s[:, b : b + LANES] = row
        carry = count[:, LANES - 1 : LANES]


def bulk_wait(ref, sem):
    pltpu.make_async_copy(ref, ref, sem).wait()


def fused_kernel(
    cfg,
    hidden_hbm, wt_hbm, target_hbm, area_hbm, var_hbm, own_hbm, row_hbm, ew_hbm,
    gw_out, mesh_out,
    hid, wt_raw, target, area, var, own, row, ew,
    wt, w_col, x_send, x_recv, g_send, g_recv,
    slot_s, w_s, r_s, a_s, wb_s, gt_s, out_buf, in_buf,
    d_send, d_recv, gw_s, gw_send, gw_recv, q_s, q_recv, p_send, p_recv, r_send, r_recv,
    in_sem, x_ss, x_rs, g_ss, g_rs, m_ss, m_rs, d_ss, d_rs, w_ss, w_rs, q_ss, q_rs, p_ss, p_rs, r_ss, r_rs,
):
    variables, slots, share, normalizer = cfg
    members, xrows, slab = x_send.shape
    grows = g_send.shape[1]
    owners, points = slot_s.shape
    latent = hid.shape[1]
    mesh_rows = mesh_out.shape[0]
    e, g = lax.axis_index("ens"), lax.axis_index("grid")
    nx, nz, nc = grid_shape(owners)
    nu = nx * nc
    z, u = lax.rem(g // nc, nz), (g // (nz * nc)) * nc + lax.rem(g, nc)

    def plane_peer(i):
        return ((i // nc) * nz + z) * nc + lax.rem(i, nc)

    def column_peer(i):
        return ((u // nc) * nz + i) * nc + lax.rem(u, nc)

    def send(src, dst, ss, rs, axis, peer, me):
        @pl.when(peer != me)
        def _():
            pltpu.make_async_remote_copy(
                src_ref=src, dst_ref=dst, send_sem=ss, recv_sem=rs,
                device_id={axis: peer}, device_id_type=pl.DeviceIdType.MESH,
            ).start()

        @pl.when(peer == me)
        def _():
            pltpu.make_async_copy(src, dst, rs).start()

    barrier = pltpu.get_barrier_semaphore()

    def greet_ens(i, _):
        pl.semaphore_signal(barrier, inc=1, device_id={"ens": lax.rem(e + i, members)}, device_id_type=pl.DeviceIdType.MESH)
        return 0

    def greet_plane(i, _):
        pl.semaphore_signal(barrier, inc=1, device_id={"grid": plane_peer(lax.rem(u + i, nu))}, device_id_type=pl.DeviceIdType.MESH)
        return 0

    def greet_column(i, _):
        pl.semaphore_signal(barrier, inc=1, device_id={"grid": column_peer(lax.rem(z + i, nz))}, device_id_type=pl.DeviceIdType.MESH)
        return 0

    chunk = 2 * slab
    loads = [pltpu.make_async_copy(wt_hbm, wt_raw, in_sem.at[0])]
    for c in range(points // chunk):
        rows = pl.ds(c * chunk, chunk)
        loads.append(pltpu.make_async_copy(hidden_hbm.at[rows], hid.at[rows], in_sem.at[1 + c]))
    n_hid = len(loads)
    loads.append(
        pltpu.make_async_copy(
            target_hbm.at[:, pl.ds(pl.multiple_of(e * slab, slab), slab)], target, in_sem.at[n_hid]
        )
    )
    for i, (s, d) in enumerate(((area_hbm, area), (var_hbm, var), (own_hbm, own), (row_hbm, row), (ew_hbm, ew))):
        loads.append(pltpu.make_async_copy(s, d, in_sem.at[n_hid + 1 + i]))
    for cp in loads:
        cp.start()
    lax.fori_loop(1, members, greet_ens, 0)
    lax.fori_loop(1, nu, greet_plane, 0)
    lax.fori_loop(1, nz, greet_column, 0)

    loads[0].wait()
    whole = variables // 16 * 16
    wt[0:whole, :] = wt_raw[0:whole, :]
    wt[whole : whole + 16, :] = jnp.concatenate(
        [wt_raw[whole:variables, :], jnp.zeros((whole + 16 - variables, latent), jnp.bfloat16)], axis=0
    )
    wt[whole + 16 :, :] = jnp.zeros((LANES - whole - 16, latent), jnp.bfloat16)
    for b in range(0, latent, LANES):
        w_col[b : b + LANES, :] = wt[:, b : b + LANES].astype(jnp.float32).T.astype(jnp.bfloat16)

    for c in range(points // chunk):
        loads[1 + c].wait()
        part = jnp.dot(hid[c * chunk : (c + 1) * chunk, :], w_col[...], preferred_element_type=jnp.float32)
        for s in range(2):
            x_send[2 * c + s] = part[s * slab : (s + 1) * slab, :].T[:xrows, :]
        if c == 0:
            pl.semaphore_wait(barrier, members + nu + nz - 3)
        for s in range(2):
            m = 2 * c + s
            send(x_send.at[m], x_recv.at[e], x_ss, x_rs, "ens", m, e)

    for cp in loads[n_hid:]:
        cp.wait()
    place_slots(own, row, ew, slot_s, w_s, r_s)
    want = lax.broadcasted_iota(jnp.int32, (slots, points), 0).astype(jnp.float32) + 1.0
    lane = lax.broadcasted_iota(jnp.int32, (slots, LANES), 1)

    def one_hot(o, _):
        same = slot_s[pl.ds(o, 1), :] == want
        at = pl.ds(pl.multiple_of(o * slots, slots), slots)
        a_s[at, :] = jnp.where(same, 1.0, 0.0).astype(jnp.bfloat16)
        w = jnp.sum(jnp.where(same, w_s[pl.ds(o, 1), :], 0.0), axis=1, keepdims=True)
        r = jnp.sum(jnp.where(same, r_s[pl.ds(o, 1), :], 0.0), axis=1, keepdims=True)
        wb_s[at, :] = jnp.where(lane == variables, r, w)
        return 0

    lax.fori_loop(0, owners, one_hot, 0)
    vcol = jnp.broadcast_to(
        jnp.concatenate([var[...], jnp.zeros((1, LANES - variables), jnp.float32)], axis=1), (LANES, LANES)
    ).T
    scale = vcol * area[pl.ds(e, 1), :]
    q_s[0:LANES, :] = scale

    bulk_wait(x_recv, x_rs)

    def score(r, rows, trows):
        at = pl.ds(r, rows)
        t = target[pl.ds(r, trows), :]
        if trows < rows:
            t = jnp.concatenate([t, jnp.zeros((rows - trows, slab), jnp.float32)], axis=0)
        got = score_block([x_recv[m, at, :] for m in range(members)], t, q_s[at, :])
        for m in range(members):
            v = got[m]
            if rows < 16:
                v = jnp.concatenate([v, jnp.zeros((16 - rows, slab), jnp.bfloat16)], axis=0)
            g_send[m, pl.ds(r, 16), :] = v

    def score_step(i, _):
        score(pl.multiple_of(i * 16, 16), 16, 16)
        return 0

    lax.fori_loop(0, variables // 16, score_step, 0)
    if variables % 16:
        score(whole, xrows - whole, variables - whole)
    for m in range(members):
        send(g_send.at[m], g_recv.at[e], g_ss, g_rs, "ens", m, e)

    bulk_wait(g_recv, g_rs)
    pad = jnp.zeros((LANES - grows, LANES), jnp.float32)
    lane = lax.broadcasted_iota(jnp.int32, (LANES, LANES), 1)
    for s in range(members):
        block = jnp.concatenate([g_recv[s].astype(jnp.float32), pad], axis=0).T
        gt_s[s * LANES : (s + 1) * LANES, :] = jnp.where(lane == variables, 1.0, block).astype(jnp.bfloat16)
    step = nu * slots

    def messages(t, _):
        at = lax.rem(z + 1 + t, nz)
        rows = pl.ds(pl.multiple_of(at * step, step), step)
        picked = jnp.dot(a_s[rows, :], gt_s[...], preferred_element_type=jnp.float32)
        out_buf[rows, :] = (picked * wb_s[rows, :]).astype(jnp.bfloat16)
        for j in range(nu):
            send(
                out_buf.at[pl.ds(pl.multiple_of(at * step + j * slots, slots), slots)],
                in_buf.at[pl.ds(pl.multiple_of(at * step + u * slots, slots), slots)],
                m_ss, m_rs.at[at], "grid", plane_peer(j), g,
            )
        return 0

    lax.fori_loop(0, nz, messages, 0)

    wide = jnp.concatenate([g_recv[s] for s in range(members)], axis=1)
    for b in range(0, latent, 2 * LANES):
        part = jnp.dot(wide, hid[:, b : b + 2 * LANES], preferred_element_type=jnp.float32)
        for c in range(0, 2 * LANES, LANES):
            gw_s[b + c : b + c + LANES, :] = jnp.concatenate([part[:, c : c + LANES], pad], axis=0).T
    run = nz * share
    for m in range(members):
        for v in range(nu):
            for i in range(share):
                first = ((v // nc) * nz * nc + v % nc) * members * share + share * m + i
                gw_send[m, pl.ds(v * run + i, nz, share), :] = gw_s[pl.ds(first, nz, nc * members * share), :]
        send(gw_send.at[m], gw_recv.at[e], w_ss, w_rs, "ens", m, e)

    pick = (lax.broadcasted_iota(jnp.int32, (16, LANES), 1) == variables).astype(jnp.float32).astype(jnp.bfloat16)
    ids = lax.broadcasted_iota(jnp.int32, (mesh_rows, step), 0).astype(jnp.float32)

    def mesh_part(t, _):
        at = lax.rem(z + 1 + t, nz)
        rows = pl.ds(pl.multiple_of(at * step, step), step)
        bulk_wait(in_buf.at[rows], m_rs.at[at])
        block = in_buf[rows, :]
        place = lax.dot_general(pick, block, (((1,), (1,)), ((), ())), preferred_element_type=jnp.float32)
        picker = jnp.where(place[0:1, :] == ids, 1.0, 0.0).astype(jnp.bfloat16)
        d_send[at] = jnp.dot(picker, block, preferred_element_type=jnp.float32).astype(jnp.bfloat16)
        send(d_send.at[at], d_recv.at[z], d_ss, d_rs, "grid", column_peer(at), g)
        return 0

    lax.fori_loop(0, nz // 2, mesh_part, 0)

    bulk_wait(gw_recv, w_rs)
    total = gw_recv[0]
    for m in range(1, members):
        total = total + gw_recv[m]
    q_s[0 : owners * share, :] = total
    for j in range(nu):
        send(q_s.at[pl.ds(j * run, run)], q_recv.at[u], q_ss, q_rs, "grid", plane_peer(j), g)

    lax.fori_loop(nz // 2, nz - 1, mesh_part, 0)

    bulk_wait(q_recv, q_rs)
    total = q_recv[0]
    for j in range(1, nu):
        total = total + q_recv[j]
    for j in range(nz):
        p_send[j] = total[j * share : (j + 1) * share, :]
    for j in range(nz):
        send(p_send.at[j], p_recv.at[z], p_ss, p_rs, "grid", column_peer(j), g)

    lax.fori_loop(nz - 1, nz, mesh_part, 0)

    bulk_wait(p_recv, p_rs)
    r_send[...] = jnp.sum(p_recv[...], axis=0) * normalizer
    for m in range(members):
        send(r_send, r_recv.at[e], r_ss, r_rs, "ens", m, e)
    bulk_wait(d_recv, d_rs)
    acc = d_recv[0].astype(jnp.float32)
    for j in range(1, nz):
        acc = acc + d_recv[j].astype(jnp.float32)
    mesh_out[...] = jnp.dot(
        acc.astype(jnp.bfloat16), wt[...], preferred_element_type=jnp.float32
    ).astype(jnp.bfloat16)
    bulk_wait(r_recv, r_rs)
    for m in range(members):
        gw_out[share * m : share * (m + 1), :] = r_recv[m, :, 0:variables]

    bulk_wait(x_send.at[pl.ds(0, members - 1)], x_ss)
    bulk_wait(g_send.at[pl.ds(0, members - 1)], g_ss)
    bulk_wait(out_buf.at[pl.ds(0, (nu - 1) * nz * slots)], m_ss)
    bulk_wait(d_send.at[pl.ds(0, nz - 1)], d_ss)
    bulk_wait(gw_send.at[pl.ds(0, members - 1)], w_ss)
    bulk_wait(q_recv.at[pl.ds(0, nu - 1)], q_ss)
    bulk_wait(p_send.at[pl.ds(0, nz - 1)], p_ss)
    bulk_wait(r_recv.at[pl.ds(0, members - 1)], r_ss)


def per_device(hidden, weight, target, area_weight, var_weight, edge_owner, edge_row, edge_weight):
    rows = hidden[0]
    points, latent = rows.shape
    variables = weight.shape[1]
    neigh = edge_owner.shape[1]
    members = lax.axis_size("ens")
    owners = lax.axis_size("grid")
    mesh_rows = points // 8
    slab = points // members
    assert slab == LANES and variables < LANES
    capacity = max(2, (5 * points * neigh + 4 * owners - 1) // (4 * owners))
    slots = round_up(capacity, 16)
    xrows, grows = round_up(variables, 8), round_up(variables, 16)
    nx, nz, nc = grid_shape(owners)
    nu = nx * nc
    share = latent // (owners * members)
    normalizer = 1.0 / math.sqrt(float(points * owners * members))
    f32, bf16, i32 = jnp.float32, jnp.bfloat16, jnp.int32
    hbm = pl.BlockSpec(memory_space=pltpu.HBM)
    vmem = pl.BlockSpec(memory_space=pltpu.VMEM)
    dma = pltpu.SemaphoreType.DMA
    grad_weight, mesh_grad = pl.pallas_call(
        functools.partial(fused_kernel, (variables, slots, share, normalizer)),
        in_specs=[hbm] * 8,
        out_specs=[vmem] * 2,
        out_shape=[
            jax.ShapeDtypeStruct((members * share, variables), f32),
            jax.ShapeDtypeStruct((mesh_rows, latent), bf16),
        ],
        scratch_shapes=[
            pltpu.VMEM((points, latent), bf16),
            pltpu.VMEM((variables, latent), bf16),
            pltpu.VMEM((variables, slab), f32),
            pltpu.VMEM((points // LANES, LANES), f32),
            pltpu.VMEM((1, variables), f32),
            pltpu.VMEM((neigh, points), i32),
            pltpu.VMEM((neigh, points), i32),
            pltpu.VMEM((neigh, points), f32),
            pltpu.VMEM((LANES, latent), bf16),
            pltpu.VMEM((latent, LANES), bf16),
            pltpu.VMEM((members, xrows, slab), f32),
            pltpu.VMEM((members, xrows, slab), f32),
            pltpu.VMEM((members, grows, slab), bf16),
            pltpu.VMEM((members, grows, slab), bf16),
            pltpu.VMEM((owners, points), f32),
            pltpu.VMEM((owners, points), f32),
            pltpu.VMEM((owners, points), f32),
            pltpu.VMEM((owners * slots, points), bf16),
            pltpu.VMEM((owners * slots, LANES), f32),
            pltpu.VMEM((points, LANES), bf16),
            pltpu.VMEM((owners * slots, LANES), bf16),
            pltpu.VMEM((owners * slots, LANES), bf16),
            pltpu.VMEM((nz, mesh_rows, LANES), bf16),
            pltpu.VMEM((nz, mesh_rows, LANES), bf16),
            pltpu.VMEM((latent, LANES), f32),
            pltpu.VMEM((members, owners * share, LANES), f32),
            pltpu.VMEM((members, owners * share, LANES), f32),
            pltpu.VMEM((max(LANES, owners * share), LANES), f32),
            pltpu.VMEM((nu, nz * share, LANES), f32),
            pltpu.VMEM((nz, share, LANES), f32),
            pltpu.VMEM((nz, share, LANES), f32),
            pltpu.VMEM((share, LANES), f32),
            pltpu.VMEM((members, share, LANES), f32),
            dma((7 + points // (2 * slab),)),
            dma(()), dma(()), dma(()), dma(()), dma(()), dma((nz,)), dma(()), dma(()),
            dma(()), dma(()), dma(()), dma(()), dma(()), dma(()), dma(()), dma(()),
        ],
        compiler_params=pltpu.CompilerParams(
            collective_id=0, has_side_effects=True, vmem_limit_bytes=VMEM_LIMIT
        ),
    )(
        rows, weight.T, target, area_weight.reshape(points // LANES, LANES), var_weight.reshape(1, variables),
        edge_owner.T, edge_row.T, edge_weight.T,
    )
    return grad_weight, mesh_grad[None]


def solution(mesh):
    return jax.shard_map(
        per_device,
        mesh=mesh,
        in_specs=(
            P("ens", "grid", None),
            P(),
            P(None, "grid"),
            P("grid"),
            P(),
            P("grid", None),
            P("grid", None),
            P("grid", None),
        ),
        out_specs=(P("grid", None), P("ens", "grid", None)),
        check_vma=False,
    )
```

```python
import functools
import math

import jax
import jax.numpy as jnp
from jax import lax
from jax.experimental import pallas as pl
from jax.experimental.pallas import tpu as pltpu
from jax.sharding import PartitionSpec as P

smooth_width = 0.1
LANES = 128
VMEM_LIMIT = 62 * 1024 * 1024


def softened_sign(difference):
    return difference * lax.rsqrt(difference * difference + smooth_width * smooth_width)


def round_up(n, m):
    return (n + m - 1) // m * m


def score_block(x, t, scale):
    n = len(x)
    total = [None] * n
    for i in range(n):
        for j in range(i + 1, n):
            a = softened_sign(x[i] - x[j])
            total[i] = a if total[i] is None else total[i] + a
            total[j] = -a if total[j] is None else total[j] - a
    out = []
    for i in range(n):
        raw = softened_sign(x[i] - t) * (1.0 / n) - total[i] * (1.0 / (n * (n - 1)))
        out.append((scale * raw).astype(jnp.bfloat16))
    return out


def grid_shape(owners):
    return (owners // 16, 8, 2) if owners >= 16 else (owners // 4, 2, 2)


def place_slots(own_ref, row_ref, ew_ref, slot_s, w_s, r_s):
    owners, points = slot_s.shape
    neigh = own_ref.shape[0]
    tri = (
        lax.broadcasted_iota(jnp.int32, (LANES, LANES), 0)
        <= lax.broadcasted_iota(jnp.int32, (LANES, LANES), 1)
    ).astype(jnp.float32).astype(jnp.bfloat16)
    nx, nz, nc = grid_shape(owners)
    at = lax.broadcasted_iota(jnp.int32, (owners, LANES), 0)
    z_id = lax.shift_right_logical(at, int(math.log2(nx * nc)))
    x_id = jnp.bitwise_and(lax.shift_right_logical(at, int(math.log2(nc))), nx - 1)
    owner_id = (x_id * nz + z_id) * nc + jnp.bitwise_and(at, nc - 1)
    carry = jnp.zeros((owners, 1), jnp.float32)
    for b in range(0, points, LANES):
        hit = jnp.zeros((owners, LANES), jnp.float32)
        w = jnp.zeros((owners, LANES), jnp.float32)
        row = jnp.zeros((owners, LANES), jnp.float32)
        for k in range(neigh):
            same = own_ref[k : k + 1, b : b + LANES] == owner_id
            hit = jnp.where(same, 1.0, hit)
            w = jnp.where(same, ew_ref[k : k + 1, b : b + LANES], w)
            row = jnp.where(same, row_ref[k : k + 1, b : b + LANES].astype(jnp.float32), row)
        count = carry + jnp.dot(hit.astype(jnp.bfloat16), tri, preferred_element_type=jnp.float32)
        slot_s[:, b : b + LANES] = jnp.where(hit > 0.0, count, 0.0)
        w_s[:, b : b + LANES] = w
        r_s[:, b : b + LANES] = row
        carry = count[:, LANES - 1 : LANES]


def bulk_wait(ref, sem):
    pltpu.make_async_copy(ref, ref, sem).wait()


def fused_kernel(
    cfg,
    hidden_hbm, wt_hbm, target_hbm, area_hbm, var_hbm, own_hbm, row_hbm, ew_hbm,
    gw_out, mesh_out,
    hid, wt_raw, target, area, var, own, row, ew,
    wt, w_col, x_send, x_recv, g_send, g_recv,
    slot_s, w_s, r_s, a_s, wb_s, gt_s, out_buf, in_buf,
    d_send, d_recv, gw_s, half_s, half_recv, y_send, y_recv, q_s, q_recv, p_send, p_recv, r_send, r_recv,
    in_sem, x_ss, x_rs, g_ss, g_rs, m_ss, m_rs, d_ss, d_rs, h_ss, h_rs, y_ss, y_rs, q_ss, q_rs, p_ss, p_rs, r_ss, r_rs,
):
    variables, slots, share, normalizer = cfg
    members, xrows, slab = x_send.shape
    grows = g_send.shape[1]
    owners, points = slot_s.shape
    latent = hid.shape[1]
    mesh_rows = d_send.shape[1]
    e, g = lax.axis_index("ens"), lax.axis_index("grid")
    nx, nz, nc = grid_shape(owners)
    nu = nx * nc
    z, core = lax.rem(g // nc, nz), lax.rem(g, nc)
    x_at = g // (nz * nc)
    u = x_at * nc + core

    def plane_peer(i):
        return ((i // nc) * nz + z) * nc + lax.rem(i, nc)

    def column_peer(i):
        return ((u // nc) * nz + i) * nc + lax.rem(u, nc)

    def send(src, dst, ss, rs, axis, peer, me):
        @pl.when(peer != me)
        def _():
            pltpu.make_async_remote_copy(
                src_ref=src, dst_ref=dst, send_sem=ss, recv_sem=rs,
                device_id={axis: peer}, device_id_type=pl.DeviceIdType.MESH,
            ).start()

        @pl.when(peer == me)
        def _():
            pltpu.make_async_copy(src, dst, rs).start()

    barrier = pltpu.get_barrier_semaphore()

    def greet_ens(i, _):
        pl.semaphore_signal(barrier, inc=1, device_id={"ens": lax.rem(e + i, members)}, device_id_type=pl.DeviceIdType.MESH)
        return 0

    def greet_plane(i, _):
        pl.semaphore_signal(barrier, inc=1, device_id={"grid": plane_peer(lax.rem(u + i, nu))}, device_id_type=pl.DeviceIdType.MESH)
        return 0

    def greet_column(i, _):
        pl.semaphore_signal(barrier, inc=1, device_id={"grid": column_peer(lax.rem(z + i, nz))}, device_id_type=pl.DeviceIdType.MESH)
        return 0

    chunk = 2 * slab
    loads = [pltpu.make_async_copy(wt_hbm, wt_raw, in_sem.at[0])]
    for c in range(points // chunk):
        rows = pl.ds(c * chunk, chunk)
        loads.append(pltpu.make_async_copy(hidden_hbm.at[rows], hid.at[rows], in_sem.at[1 + c]))
    n_hid = len(loads)
    loads.append(
        pltpu.make_async_copy(
            target_hbm.at[:, pl.ds(pl.multiple_of(e * slab, slab), slab)], target, in_sem.at[n_hid]
        )
    )
    for i, (s, d) in enumerate(((area_hbm, area), (var_hbm, var), (own_hbm, own), (row_hbm, row), (ew_hbm, ew))):
        loads.append(pltpu.make_async_copy(s, d, in_sem.at[n_hid + 1 + i]))
    for cp in loads:
        cp.start()
    lax.fori_loop(1, members, greet_ens, 0)
    lax.fori_loop(1, nu, greet_plane, 0)
    lax.fori_loop(1, nz, greet_column, 0)

    loads[0].wait()
    whole = variables // 16 * 16
    wt[0:whole, :] = wt_raw[0:whole, :]
    wt[whole : whole + 16, :] = jnp.concatenate(
        [wt_raw[whole:variables, :], jnp.zeros((whole + 16 - variables, latent), jnp.bfloat16)], axis=0
    )
    wt[whole + 16 :, :] = jnp.zeros((LANES - whole - 16, latent), jnp.bfloat16)
    for b in range(0, latent, LANES):
        w_col[b : b + LANES, :] = wt[:, b : b + LANES].astype(jnp.float32).T.astype(jnp.bfloat16)

    for c in range(points // chunk):
        loads[1 + c].wait()
        part = jnp.dot(hid[c * chunk : (c + 1) * chunk, :], w_col[...], preferred_element_type=jnp.float32)
        for s in range(2):
            x_send[2 * c + s] = part[s * slab : (s + 1) * slab, :].T[:xrows, :]
        if c == 0:
            pl.semaphore_wait(barrier, members + nu + nz - 3)
        for s in range(2):
            m = 2 * c + s
            send(x_send.at[m], x_recv.at[e], x_ss, x_rs, "ens", m, e)

    for cp in loads[n_hid:]:
        cp.wait()
    place_slots(own, row, ew, slot_s, w_s, r_s)
    want = lax.broadcasted_iota(jnp.int32, (slots, points), 0).astype(jnp.float32) + 1.0
    lane = lax.broadcasted_iota(jnp.int32, (slots, LANES), 1)

    def one_hot(o, _):
        same = slot_s[pl.ds(o, 1), :] == want
        at = pl.ds(pl.multiple_of(o * slots, slots), slots)
        a_s[at, :] = jnp.where(same, 1.0, 0.0).astype(jnp.bfloat16)
        w = jnp.sum(jnp.where(same, w_s[pl.ds(o, 1), :], 0.0), axis=1, keepdims=True)
        r = jnp.sum(jnp.where(same, r_s[pl.ds(o, 1), :], 0.0), axis=1, keepdims=True)
        wb_s[at, :] = jnp.where(lane == variables, r, w)
        return 0

    lax.fori_loop(0, owners, one_hot, 0)
    vcol = jnp.broadcast_to(
        jnp.concatenate([var[...], jnp.zeros((1, LANES - variables), jnp.float32)], axis=1), (LANES, LANES)
    ).T
    scale = vcol * area[pl.ds(e, 1), :]
    q_s[0:LANES, :] = scale

    bulk_wait(x_recv, x_rs)

    def score(r, rows, trows):
        at = pl.ds(r, rows)
        t = target[pl.ds(r, trows), :]
        if trows < rows:
            t = jnp.concatenate([t, jnp.zeros((rows - trows, slab), jnp.float32)], axis=0)
        got = score_block([x_recv[m, at, :] for m in range(members)], t, q_s[at, :])
        for m in range(members):
            v = got[m]
            if rows < 16:
                v = jnp.concatenate([v, jnp.zeros((16 - rows, slab), jnp.bfloat16)], axis=0)
            g_send[m, pl.ds(r, 16), :] = v

    def score_step(i, _):
        score(pl.multiple_of(i * 16, 16), 16, 16)
        return 0

    lax.fori_loop(0, variables // 16, score_step, 0)
    if variables % 16:
        score(whole, xrows - whole, variables - whole)
    for m in range(members):
        send(g_send.at[m], g_recv.at[e], g_ss, g_rs, "ens", m, e)

    bulk_wait(g_recv, g_rs)
    pad = jnp.zeros((LANES - grows, LANES), jnp.float32)
    lane = lax.broadcasted_iota(jnp.int32, (LANES, LANES), 1)
    for s in range(members):
        block = jnp.concatenate([g_recv[s].astype(jnp.float32), pad], axis=0).T
        gt_s[s * LANES : (s + 1) * LANES, :] = jnp.where(lane == variables, 1.0, block).astype(jnp.bfloat16)
    step = nu * slots

    def messages(t, _):
        at = lax.rem(z + 1 + t, nz)
        rows = pl.ds(pl.multiple_of(at * step, step), step)
        picked = jnp.dot(a_s[rows, :], gt_s[...], preferred_element_type=jnp.float32)
        out_buf[rows, :] = (picked * wb_s[rows, :]).astype(jnp.bfloat16)
        for j in range(nu):
            send(
                out_buf.at[pl.ds(pl.multiple_of(at * step + j * slots, slots), slots)],
                in_buf.at[pl.ds(pl.multiple_of(at * step + u * slots, slots), slots)],
                m_ss, m_rs.at[at], "grid", plane_peer(j), g,
            )
        return 0

    lax.fori_loop(0, nz // 4, messages, 0)

    wide = jnp.concatenate([g_recv[s] for s in range(members)], axis=1)
    for b in range(0, latent, 2 * LANES):
        part = jnp.dot(wide, hid[:, b : b + 2 * LANES], preferred_element_type=jnp.float32)
        for c in range(0, 2 * LANES, LANES):
            gw_s[b + c : b + c + LANES, :] = jnp.concatenate([part[:, c : c + LANES], pad], axis=0).T
    run = nz * share
    per_member = nx * run
    for c in range(nc):
        for m in range(members):
            for v in range(nx):
                for i in range(share):
                    first = (v * nz * nc + c) * members * share + share * m + i
                    half_s[c, pl.ds(m * per_member + v * run + i, nz, share), :] = gw_s[
                        pl.ds(first, nz, nc * members * share), :
                    ]
    half = pltpu.make_async_remote_copy(
        src_ref=half_s.at[1 - core], dst_ref=half_recv, send_sem=h_ss, recv_sem=h_rs,
        device_id={"grid": g + 1 - 2 * core}, device_id_type=pl.DeviceIdType.MESH,
    )
    half.start()

    lax.fori_loop(nz // 4, nz // 2, messages, 0)

    half.wait_recv()
    for m in range(members):
        rows = pl.ds(m * per_member, per_member)
        y_send[m] = half_s[core, rows, :] + half_recv[rows, :]
    for m in range(members):
        send(y_send.at[m], y_recv.at[e], y_ss, y_rs, "ens", m, e)

    lax.fori_loop(nz // 2, nz, messages, 0)

    pick = (lax.broadcasted_iota(jnp.int32, (16, LANES), 1) == variables).astype(jnp.float32).astype(jnp.bfloat16)
    ids = lax.broadcasted_iota(jnp.int32, (mesh_rows, step), 0).astype(jnp.float32)

    def mesh_part(t, _):
        at = lax.rem(z + 1 + t, nz)
        rows = pl.ds(pl.multiple_of(at * step, step), step)
        bulk_wait(in_buf.at[rows], m_rs.at[at])
        block = in_buf[rows, :]
        place = lax.dot_general(pick, block, (((1,), (1,)), ((), ())), preferred_element_type=jnp.float32)
        picker = jnp.where(place[0:1, :] == ids, 1.0, 0.0).astype(jnp.bfloat16)
        d_send[at] = jnp.dot(picker, block, preferred_element_type=jnp.float32).astype(jnp.bfloat16)
        send(d_send.at[at], d_recv.at[z], d_ss, d_rs, "grid", column_peer(at), g)
        return 0

    lax.fori_loop(0, nz - 2, mesh_part, 0)

    bulk_wait(y_recv, y_rs)
    total = y_recv[0]
    for m in range(1, members):
        total = total + y_recv[m]
    q_s[0:per_member, :] = total
    for j in range(nx):
        send(q_s.at[pl.ds(j * run, run)], q_recv.at[x_at], q_ss, q_rs, "grid", plane_peer(j * nc + core), g)

    lax.fori_loop(nz - 2, nz - 1, mesh_part, 0)

    bulk_wait(q_recv, q_rs)
    total = q_recv[0]
    for j in range(1, nx):
        total = total + q_recv[j]
    for j in range(nz):
        p_send[j] = total[j * share : (j + 1) * share, :]
    for j in range(nz):
        send(p_send.at[j], p_recv.at[z], p_ss, p_rs, "grid", column_peer(j), g)

    lax.fori_loop(nz - 1, nz, mesh_part, 0)

    bulk_wait(p_recv, p_rs)
    r_send[...] = jnp.sum(p_recv[...], axis=0) * normalizer
    for m in range(members):
        send(r_send, r_recv.at[e], r_ss, r_rs, "ens", m, e)
    bulk_wait(d_recv, d_rs)
    acc = d_recv[0].astype(jnp.float32)
    for j in range(1, nz):
        acc = acc + d_recv[j].astype(jnp.float32)
    mesh_out[...] = acc.astype(jnp.bfloat16)
    bulk_wait(r_recv, r_rs)
    for m in range(members):
        gw_out[share * m : share * (m + 1), :] = r_recv[m]

    bulk_wait(x_send.at[pl.ds(0, members - 1)], x_ss)
    bulk_wait(g_send.at[pl.ds(0, members - 1)], g_ss)
    bulk_wait(out_buf.at[pl.ds(0, (nu - 1) * nz * slots)], m_ss)
    bulk_wait(d_send.at[pl.ds(0, nz - 1)], d_ss)
    half.wait_send()
    bulk_wait(y_send.at[pl.ds(0, members - 1)], y_ss)
    bulk_wait(q_recv.at[pl.ds(0, nx - 1)], q_ss)
    bulk_wait(p_send.at[pl.ds(0, nz - 1)], p_ss)
    bulk_wait(r_recv.at[pl.ds(0, members - 1)], r_ss)


def finish_kernel(gw_ref, mesh_ref, wt_ref, gw_out, mesh_out):
    variables, latent = wt_ref.shape
    gw_out[...] = gw_ref[:, 0:variables]
    whole = variables // 16 * 16
    wide = jnp.concatenate(
        [wt_ref[whole:variables, :], jnp.zeros((whole + 16 - variables, latent), jnp.bfloat16)], axis=0
    )
    total = jnp.dot(mesh_ref[:, 0:whole], wt_ref[0:whole, :], preferred_element_type=jnp.float32)
    total = total + jnp.dot(mesh_ref[:, whole : whole + 16], wide, preferred_element_type=jnp.float32)
    mesh_out[...] = total.astype(jnp.bfloat16)


def per_device(hidden, weight, target, area_weight, var_weight, edge_owner, edge_row, edge_weight):
    rows = hidden[0]
    points, latent = rows.shape
    variables = weight.shape[1]
    neigh = edge_owner.shape[1]
    members = lax.axis_size("ens")
    owners = lax.axis_size("grid")
    mesh_rows = points // 8
    slab = points // members
    assert slab == LANES and variables < LANES
    capacity = max(2, (5 * points * neigh + 4 * owners - 1) // (4 * owners))
    slots = round_up(capacity, 16)
    xrows, grows = round_up(variables, 8), round_up(variables, 16)
    nx, nz, nc = grid_shape(owners)
    nu = nx * nc
    share = latent // (owners * members)
    normalizer = 1.0 / math.sqrt(float(points * owners * members))
    f32, bf16, i32 = jnp.float32, jnp.bfloat16, jnp.int32
    hbm = pl.BlockSpec(memory_space=pltpu.HBM)
    vmem = pl.BlockSpec(memory_space=pltpu.VMEM)
    dma = pltpu.SemaphoreType.DMA
    wt = weight.T
    gw, mesh_sum = pl.pallas_call(
        functools.partial(fused_kernel, (variables, slots, share, normalizer)),
        in_specs=[hbm] * 8,
        out_specs=[vmem] * 2,
        out_shape=[
            jax.ShapeDtypeStruct((members * share, LANES), f32),
            jax.ShapeDtypeStruct((mesh_rows, LANES), bf16),
        ],
        scratch_shapes=[
            pltpu.VMEM((points, latent), bf16),
            pltpu.VMEM((variables, latent), bf16),
            pltpu.VMEM((variables, slab), f32),
            pltpu.VMEM((points // LANES, LANES), f32),
            pltpu.VMEM((1, variables), f32),
            pltpu.VMEM((neigh, points), i32),
            pltpu.VMEM((neigh, points), i32),
            pltpu.VMEM((neigh, points), f32),
            pltpu.VMEM((LANES, latent), bf16),
            pltpu.VMEM((latent, LANES), bf16),
            pltpu.VMEM((members, xrows, slab), f32),
            pltpu.VMEM((members, xrows, slab), f32),
            pltpu.VMEM((members, grows, slab), bf16),
            pltpu.VMEM((members, grows, slab), bf16),
            pltpu.VMEM((owners, points), f32),
            pltpu.VMEM((owners, points), f32),
            pltpu.VMEM((owners, points), f32),
            pltpu.VMEM((owners * slots, points), bf16),
            pltpu.VMEM((owners * slots, LANES), f32),
            pltpu.VMEM((points, LANES), bf16),
            pltpu.VMEM((owners * slots, LANES), bf16),
            pltpu.VMEM((owners * slots, LANES), bf16),
            pltpu.VMEM((nz, mesh_rows, LANES), bf16),
            pltpu.VMEM((nz, mesh_rows, LANES), bf16),
            pltpu.VMEM((latent, LANES), f32),
            pltpu.VMEM((nc, latent // nc, LANES), f32),
            pltpu.VMEM((latent // nc, LANES), f32),
            pltpu.VMEM((members, nx * nz * share, LANES), f32),
            pltpu.VMEM((members, nx * nz * share, LANES), f32),
            pltpu.VMEM((max(LANES, owners * share), LANES), f32),
            pltpu.VMEM((nx, nz * share, LANES), f32),
            pltpu.VMEM((nz, share, LANES), f32),
            pltpu.VMEM((nz, share, LANES), f32),
            pltpu.VMEM((share, LANES), f32),
            pltpu.VMEM((members, share, LANES), f32),
            dma((7 + points // (2 * slab),)),
            dma(()), dma(()), dma(()), dma(()), dma(()), dma((nz,)), dma(()), dma(()),
            dma(()), dma(()), dma(()), dma(()), dma(()), dma(()), dma(()), dma(()), dma(()), dma(()),
        ],
        compiler_params=pltpu.CompilerParams(
            collective_id=0, has_side_effects=True, vmem_limit_bytes=VMEM_LIMIT
        ),
    )(
        rows, wt, target, area_weight.reshape(points // LANES, LANES), var_weight.reshape(1, variables),
        edge_owner.T, edge_row.T, edge_weight.T,
    )
    grad_weight, mesh_grad = pl.pallas_call(
        finish_kernel,
        in_specs=[vmem] * 3,
        out_specs=[vmem] * 2,
        out_shape=[
            jax.ShapeDtypeStruct((members * share, variables), f32),
            jax.ShapeDtypeStruct((mesh_rows, latent), bf16),
        ],
        compiler_params=pltpu.CompilerParams(vmem_limit_bytes=VMEM_LIMIT),
    )(gw, mesh_sum, wt)
    return grad_weight, mesh_grad[None]


def solution(mesh):
    return jax.shard_map(
        per_device,
        mesh=mesh,
        in_specs=(
            P("ens", "grid", None),
            P(),
            P(None, "grid"),
            P("grid"),
            P(),
            P("grid", None),
            P("grid", None),
            P("grid", None),
        ),
        out_specs=(P("grid", None), P("ens", "grid", None)),
        check_vma=False,
    )
```

```python
import functools
import math

import jax
import jax.numpy as jnp
from jax import lax
from jax.experimental import pallas as pl
from jax.experimental.pallas import tpu as pltpu
from jax.sharding import PartitionSpec as P

smooth_width = 0.1
LANES = 128
STEPS = 32000.0
VMEM_LIMIT = 62 * 1024 * 1024


def softened_sign(difference):
    return difference * lax.rsqrt(difference * difference + smooth_width * smooth_width)


def round_up(n, m):
    return (n + m - 1) // m * m


def score_block(x, t, scale):
    n = len(x)
    total = [None] * n
    for i in range(n):
        for j in range(i + 1, n):
            a = softened_sign(x[i] - x[j])
            total[i] = a if total[i] is None else total[i] + a
            total[j] = -a if total[j] is None else total[j] - a
    out = []
    for i in range(n):
        raw = softened_sign(x[i] - t) * (1.0 / n) - total[i] * (1.0 / (n * (n - 1)))
        out.append((scale * raw).astype(jnp.bfloat16))
    return out


def grid_shape(owners):
    return (owners // 16, 8, 2) if owners >= 16 else (owners // 4, 2, 2)


def place_slots(own_ref, row_ref, ew_ref, slot_s, w_s, r_s):
    owners, points = slot_s.shape
    neigh = own_ref.shape[0]
    tri = (
        lax.broadcasted_iota(jnp.int32, (LANES, LANES), 0)
        <= lax.broadcasted_iota(jnp.int32, (LANES, LANES), 1)
    ).astype(jnp.float32).astype(jnp.bfloat16)
    nx, nz, nc = grid_shape(owners)
    at = lax.broadcasted_iota(jnp.int32, (owners, LANES), 0)
    z_id = lax.shift_right_logical(at, int(math.log2(nx * nc)))
    x_id = jnp.bitwise_and(lax.shift_right_logical(at, int(math.log2(nc))), nx - 1)
    owner_id = (x_id * nz + z_id) * nc + jnp.bitwise_and(at, nc - 1)
    carry = jnp.zeros((owners, 1), jnp.float32)
    for b in range(0, points, LANES):
        hit = jnp.zeros((owners, LANES), jnp.float32)
        w = jnp.zeros((owners, LANES), jnp.float32)
        row = jnp.zeros((owners, LANES), jnp.float32)
        for k in range(neigh):
            same = own_ref[k : k + 1, b : b + LANES] == owner_id
            hit = jnp.where(same, 1.0, hit)
            w = jnp.where(same, ew_ref[k : k + 1, b : b + LANES], w)
            row = jnp.where(same, row_ref[k : k + 1, b : b + LANES].astype(jnp.float32), row)
        count = carry + jnp.dot(hit.astype(jnp.bfloat16), tri, preferred_element_type=jnp.float32)
        slot_s[:, b : b + LANES] = jnp.where(hit > 0.0, count, 0.0)
        w_s[:, b : b + LANES] = w
        r_s[:, b : b + LANES] = row
        carry = count[:, LANES - 1 : LANES]


def far_first(n):
    return sorted(range(n), key=lambda o: -min(o, n - o))


def bulk_wait(ref, sem):
    pltpu.make_async_copy(ref, ref, sem).wait()


def fused_kernel(
    cfg,
    hidden_hbm, wt_hbm, target_hbm, area_hbm, var_hbm, own_hbm, row_hbm, ew_hbm,
    gw_out, mesh_out,
    hid, wt_raw, target, area, var, own, row, ew,
    wt, w_col, x_send, x_recv, unit_s, g_send, g_recv,
    slot_s, w_s, r_s, a_s, wb_s, gt_s, out_buf, in_buf,
    d_send, d_recv, gw_s, half_s, half_recv, y_send, y_recv, q_s, q_recv, p_send, p_recv, r_send, r_recv,
    in_sem, x_ss, x_rs, g_ss, g_rs, m_ss, m_rs, d_ss, d_rs, h_ss, h_rs, y_ss, y_rs, q_ss, q_rs, p_ss, p_rs, r_ss, r_rs,
):
    variables, slots, share, normalizer = cfg
    members, grows, slab = g_send.shape
    owners, points = slot_s.shape
    latent = hid.shape[1]
    mesh_rows = d_send.shape[1]
    e, g = lax.axis_index("ens"), lax.axis_index("grid")
    nx, nz, nc = grid_shape(owners)
    nu = nx * nc
    z, core = lax.rem(g // nc, nz), lax.rem(g, nc)
    x_at = g // (nz * nc)
    u = x_at * nc + core

    def plane_peer(i):
        return ((i // nc) * nz + z) * nc + lax.rem(i, nc)

    def column_peer(i):
        return ((u // nc) * nz + i) * nc + lax.rem(u, nc)

    def send(src, dst, ss, rs, axis, peer, me):
        @pl.when(peer != me)
        def _():
            pltpu.make_async_remote_copy(
                src_ref=src, dst_ref=dst, send_sem=ss, recv_sem=rs,
                device_id={axis: peer}, device_id_type=pl.DeviceIdType.MESH,
            ).start()

        @pl.when(peer == me)
        def _():
            pltpu.make_async_copy(src, dst, rs).start()

    barrier = pltpu.get_barrier_semaphore()

    def greet_ens(i, _):
        pl.semaphore_signal(barrier, inc=1, device_id={"ens": lax.rem(e + i, members)}, device_id_type=pl.DeviceIdType.MESH)
        return 0

    def greet_plane(i, _):
        pl.semaphore_signal(barrier, inc=1, device_id={"grid": plane_peer(lax.rem(u + i, nu))}, device_id_type=pl.DeviceIdType.MESH)
        return 0

    def greet_column(i, _):
        pl.semaphore_signal(barrier, inc=1, device_id={"grid": column_peer(lax.rem(z + i, nz))}, device_id_type=pl.DeviceIdType.MESH)
        return 0

    chunk = 2 * slab
    loads = [pltpu.make_async_copy(wt_hbm, wt_raw, in_sem.at[0])]
    chunks = points // chunk
    order = [lax.rem(e // 2 + o, chunks) for o in far_first(chunks)]
    for c in order:
        rows = pl.ds(pl.multiple_of(c * chunk, chunk), chunk)
        loads.append(pltpu.make_async_copy(hidden_hbm.at[rows], hid.at[rows], in_sem.at[1 + c]))
    n_hid = len(loads)
    loads.append(
        pltpu.make_async_copy(
            target_hbm.at[:, pl.ds(pl.multiple_of(e * slab, slab), slab)], target, in_sem.at[n_hid]
        )
    )
    for i, (s, d) in enumerate(((area_hbm, area), (var_hbm, var), (own_hbm, own), (row_hbm, row), (ew_hbm, ew))):
        loads.append(pltpu.make_async_copy(s, d, in_sem.at[n_hid + 1 + i]))
    for cp in loads:
        cp.start()
    lax.fori_loop(1, members, greet_ens, 0)
    lax.fori_loop(1, nu, greet_plane, 0)
    lax.fori_loop(1, nz, greet_column, 0)

    loads[0].wait()
    whole = variables // 16 * 16
    wt[0:whole, :] = wt_raw[0:whole, :]
    wt[whole : whole + 16, :] = jnp.concatenate(
        [wt_raw[whole:variables, :], jnp.zeros((whole + 16 - variables, latent), jnp.bfloat16)], axis=0
    )
    wt[whole + 16 :, :] = jnp.zeros((LANES - whole - 16, latent), jnp.bfloat16)
    for b in range(0, latent, LANES):
        w_col[b : b + LANES, :] = wt[:, b : b + LANES].astype(jnp.float32).T.astype(jnp.bfloat16)

    tail_row = lax.broadcasted_iota(jnp.int32, (8, slab), 0)
    zero_rows = jnp.zeros((8, slab), jnp.int32)
    for t, c in enumerate(order):
        loads[1 + t].wait()
        rows = pl.ds(pl.multiple_of(c * chunk, chunk), chunk)
        part = jnp.dot(hid[rows, :], w_col[...], preferred_element_type=jnp.float32)
        for s in range(2):
            m = 2 * c + s
            block = part[s * slab : (s + 1) * slab, :].T[: whole + 8, :]
            top = jnp.max(jnp.abs(block), axis=0, keepdims=True)
            power = jnp.ceil(jnp.log2(jnp.maximum(top, 1e-30)))
            code = jnp.floor(block * (jnp.exp2(-power) * STEPS) + 0.5).astype(jnp.int32)
            tail = jnp.where(tail_row == variables - whole, power.astype(jnp.int32), code[whole:, :])
            x_send[m, 0:whole, :] = code[0:whole, :].astype(jnp.int16)
            x_send[m, whole : whole + 16, :] = jnp.concatenate([tail, zero_rows], axis=0).astype(jnp.int16)
        if t == 0:
            pl.semaphore_wait(barrier, members + nu + nz - 3)
        for s in range(2):
            m = 2 * c + s
            send(x_send.at[m], x_recv.at[e], x_ss, x_rs, "ens", m, e)

    for cp in loads[n_hid:]:
        cp.wait()
    place_slots(own, row, ew, slot_s, w_s, r_s)
    want = lax.broadcasted_iota(jnp.int32, (slots, points), 0).astype(jnp.float32) + 1.0
    lane = lax.broadcasted_iota(jnp.int32, (slots, LANES), 1)

    def one_hot(o, _):
        same = slot_s[pl.ds(o, 1), :] == want
        at = pl.ds(pl.multiple_of(o * slots, slots), slots)
        a_s[at, :] = jnp.where(same, 1.0, 0.0).astype(jnp.bfloat16)
        w = jnp.sum(jnp.where(same, w_s[pl.ds(o, 1), :], 0.0), axis=1, keepdims=True)
        r = jnp.sum(jnp.where(same, r_s[pl.ds(o, 1), :], 0.0), axis=1, keepdims=True)
        wb_s[at, :] = jnp.where(lane == variables, r, w)
        return 0

    lax.fori_loop(0, owners, one_hot, 0)
    vcol = jnp.broadcast_to(
        jnp.concatenate([var[...], jnp.zeros((1, LANES - variables), jnp.float32)], axis=1), (LANES, LANES)
    ).T
    scale = vcol * area[pl.ds(e, 1), :]
    q_s[0:LANES, :] = scale

    bulk_wait(x_recv, x_rs)

    def wide_block(m, at):
        return x_recv[m, at, :].astype(jnp.int32).astype(jnp.float32)

    for m in range(members):
        power = wide_block(m, pl.ds(whole, 16))[variables - whole : variables - whole + 1, :]
        unit_s[m] = jnp.broadcast_to(jnp.exp2(power) * (1.0 / STEPS), (16, slab))

    def score(r, t):
        at = pl.ds(r, 16)
        got = score_block([wide_block(m, at) * unit_s[m] for m in range(members)], t, q_s[at, :])
        for m in range(members):
            g_send[m, at, :] = got[m]

    def score_step(i, _):
        r = pl.multiple_of(i * 16, 16)
        score(r, target[pl.ds(r, 16), :])
        return 0

    lax.fori_loop(0, variables // 16, score_step, 0)
    score(
        whole,
        jnp.concatenate(
            [target[whole:variables, :], jnp.zeros((whole + 16 - variables, slab), jnp.float32)], axis=0
        ),
    )
    for o in far_first(members):
        m = lax.rem(e + o, members)
        send(g_send.at[m], g_recv.at[e], g_ss, g_rs, "ens", m, e)

    bulk_wait(g_recv, g_rs)
    pad = jnp.zeros((LANES - grows, LANES), jnp.float32)
    lane = lax.broadcasted_iota(jnp.int32, (LANES, LANES), 1)
    for s in range(members):
        block = jnp.concatenate([g_recv[s].astype(jnp.float32), pad], axis=0).T
        gt_s[s * LANES : (s + 1) * LANES, :] = jnp.where(lane == variables, 1.0, block).astype(jnp.bfloat16)
    step = nu * slots
    both = min(2, nz)
    groups = nz // both

    def messages(t, _):
        at = lax.rem(z // both + 1 + t, groups)
        rows = pl.ds(pl.multiple_of(at * (both * step), both * step), both * step)
        picked = jnp.dot(a_s[rows, :], gt_s[...], preferred_element_type=jnp.float32)
        zs = pl.ds(at * both, both)
        out_buf[zs] = (picked * wb_s[rows, :]).astype(jnp.bfloat16).reshape(both, nu, slots, LANES)
        for o in far_first(nx):
            for c in range(nc):
                j = lax.rem(x_at + o, nx) * nc + lax.rem(core + 1 + c, nc)
                send(out_buf.at[zs, j], in_buf.at[zs, u], m_ss, m_rs.at[at], "grid", plane_peer(j), g)
        return 0

    lax.fori_loop(0, 1, messages, 0)

    wide = jnp.concatenate([g_recv[s] for s in range(members)], axis=1)
    for b in range(0, latent, 2 * LANES):
        part = jnp.dot(wide, hid[:, b : b + 2 * LANES], preferred_element_type=jnp.float32)
        for c in range(0, 2 * LANES, LANES):
            gw_s[b + c : b + c + LANES, :] = jnp.concatenate([part[:, c : c + LANES], pad], axis=0).T
    run = nz * share
    per_member = nx * run
    for c in range(nc):
        for m in range(members):
            for v in range(nx):
                for i in range(share):
                    first = (v * nz * nc + c) * members * share + share * m + i
                    half_s[c, pl.ds(m * per_member + v * run + i, nz, share), :] = gw_s[
                        pl.ds(first, nz, nc * members * share), :
                    ]
    half = pltpu.make_async_remote_copy(
        src_ref=half_s.at[1 - core], dst_ref=half_recv, send_sem=h_ss, recv_sem=h_rs,
        device_id={"grid": g + 1 - 2 * core}, device_id_type=pl.DeviceIdType.MESH,
    )
    half.start()

    lax.fori_loop(1, max(1, groups // 2), messages, 0)

    half.wait_recv()
    for m in range(members):
        rows = pl.ds(m * per_member, per_member)
        y_send[m] = half_s[core, rows, :] + half_recv[rows, :]
    for o in far_first(members):
        m = lax.rem(e + o, members)
        send(y_send.at[m], y_recv.at[e], y_ss, y_rs, "ens", m, e)

    lax.fori_loop(max(1, groups // 2), groups, messages, 0)

    pick = (lax.broadcasted_iota(jnp.int32, (16, LANES), 1) == variables).astype(jnp.float32).astype(jnp.bfloat16)
    ids = lax.broadcasted_iota(jnp.int32, (mesh_rows, step), 0).astype(jnp.float32)

    def mesh_part(t, _):
        at = lax.rem(z // both + 1 + t, groups)
        zs = pl.ds(at * both, both)
        bulk_wait(in_buf.at[zs], m_rs.at[at])
        for i in range(both):
            zi = at * both + i
            block = in_buf[zi].reshape(step, LANES)
            place = lax.dot_general(pick, block, (((1,), (1,)), ((), ())), preferred_element_type=jnp.float32)
            picker = jnp.where(place[0:1, :] == ids, 1.0, 0.0).astype(jnp.bfloat16)
            d_send[zi] = jnp.dot(picker, block, preferred_element_type=jnp.float32).astype(jnp.bfloat16)
            send(d_send.at[zi], d_recv.at[z], d_ss, d_rs, "grid", column_peer(zi), g)
        return 0

    lax.fori_loop(0, groups // 2, mesh_part, 0)

    bulk_wait(y_recv, y_rs)
    total = y_recv[0]
    for m in range(1, members):
        total = total + y_recv[m]
    q_s[0:per_member, :] = total
    for j in range(nx):
        send(q_s.at[pl.ds(j * run, run)], q_recv.at[x_at], q_ss, q_rs, "grid", plane_peer(j * nc + core), g)

    lax.fori_loop(groups // 2, groups - 1, mesh_part, 0)

    bulk_wait(q_recv, q_rs)
    total = q_recv[0]
    for j in range(1, nx):
        total = total + q_recv[j]
    for j in range(nz):
        p_send[j] = total[j * share : (j + 1) * share, :]
    for j in range(nz):
        send(p_send.at[j], p_recv.at[z], p_ss, p_rs, "grid", column_peer(j), g)

    lax.fori_loop(groups - 1, groups, mesh_part, 0)

    bulk_wait(p_recv, p_rs)
    r_send[...] = jnp.sum(p_recv[...], axis=0) * normalizer
    for m in range(members):
        send(r_send, r_recv.at[e], r_ss, r_rs, "ens", m, e)
    bulk_wait(d_recv, d_rs)
    acc = d_recv[0].astype(jnp.float32)
    for j in range(1, nz):
        acc = acc + d_recv[j].astype(jnp.float32)
    mesh_out[...] = acc.astype(jnp.bfloat16)
    bulk_wait(r_recv, r_rs)
    for m in range(members):
        gw_out[share * m : share * (m + 1), :] = r_recv[m]

    bulk_wait(x_send.at[pl.ds(0, members - 1)], x_ss)
    bulk_wait(g_send.at[pl.ds(0, members - 1)], g_ss)
    bulk_wait(out_buf.at[:, pl.ds(0, nu - 1)], m_ss)
    bulk_wait(d_send.at[pl.ds(0, nz - 1)], d_ss)
    half.wait_send()
    bulk_wait(y_send.at[pl.ds(0, members - 1)], y_ss)
    bulk_wait(q_recv.at[pl.ds(0, nx - 1)], q_ss)
    bulk_wait(p_send.at[pl.ds(0, nz - 1)], p_ss)
    bulk_wait(r_recv.at[pl.ds(0, members - 1)], r_ss)


def finish_kernel(gw_ref, mesh_ref, wt_ref, gw_out, mesh_out):
    variables, latent = wt_ref.shape
    gw_out[...] = gw_ref[:, 0:variables]
    whole = variables // 16 * 16
    wide = jnp.concatenate(
        [wt_ref[whole:variables, :], jnp.zeros((whole + 16 - variables, latent), jnp.bfloat16)], axis=0
    )
    total = jnp.dot(mesh_ref[:, 0:whole], wt_ref[0:whole, :], preferred_element_type=jnp.float32)
    total = total + jnp.dot(mesh_ref[:, whole : whole + 16], wide, preferred_element_type=jnp.float32)
    mesh_out[...] = total.astype(jnp.bfloat16)


def per_device(hidden, weight, target, area_weight, var_weight, edge_owner, edge_row, edge_weight):
    rows = hidden[0]
    points, latent = rows.shape
    variables = weight.shape[1]
    neigh = edge_owner.shape[1]
    members = lax.axis_size("ens")
    owners = lax.axis_size("grid")
    mesh_rows = points // 8
    slab = points // members
    assert slab == LANES and variables < LANES
    capacity = max(2, (5 * points * neigh + 4 * owners - 1) // (4 * owners))
    slots = round_up(capacity, 16)
    grows = round_up(variables, 16)
    assert variables % 16 in range(1, 8)
    nx, nz, nc = grid_shape(owners)
    nu = nx * nc
    share = latent // (owners * members)
    normalizer = 1.0 / math.sqrt(float(points * owners * members))
    f32, bf16, i32 = jnp.float32, jnp.bfloat16, jnp.int32
    hbm = pl.BlockSpec(memory_space=pltpu.HBM)
    vmem = pl.BlockSpec(memory_space=pltpu.VMEM)
    dma = pltpu.SemaphoreType.DMA
    wt = weight.T
    gw, mesh_sum = pl.pallas_call(
        functools.partial(fused_kernel, (variables, slots, share, normalizer)),
        in_specs=[hbm] * 8,
        out_specs=[vmem] * 2,
        out_shape=[
            jax.ShapeDtypeStruct((members * share, LANES), f32),
            jax.ShapeDtypeStruct((mesh_rows, LANES), bf16),
        ],
        scratch_shapes=[
            pltpu.VMEM((points, latent), bf16),
            pltpu.VMEM((variables, latent), bf16),
            pltpu.VMEM((variables, slab), f32),
            pltpu.VMEM((points // LANES, LANES), f32),
            pltpu.VMEM((1, variables), f32),
            pltpu.VMEM((neigh, points), i32),
            pltpu.VMEM((neigh, points), i32),
            pltpu.VMEM((neigh, points), f32),
            pltpu.VMEM((LANES, latent), bf16),
            pltpu.VMEM((latent, LANES), bf16),
            pltpu.VMEM((members, grows, slab), jnp.int16),
            pltpu.VMEM((members, grows, slab), jnp.int16),
            pltpu.VMEM((members, 16, slab), f32),
            pltpu.VMEM((members, grows, slab), bf16),
            pltpu.VMEM((members, grows, slab), bf16),
            pltpu.VMEM((owners, points), f32),
            pltpu.VMEM((owners, points), f32),
            pltpu.VMEM((owners, points), f32),
            pltpu.VMEM((owners * slots, points), bf16),
            pltpu.VMEM((owners * slots, LANES), f32),
            pltpu.VMEM((points, LANES), bf16),
            pltpu.VMEM((nz, nu, slots, LANES), bf16),
            pltpu.VMEM((nz, nu, slots, LANES), bf16),
            pltpu.VMEM((nz, mesh_rows, LANES), bf16),
            pltpu.VMEM((nz, mesh_rows, LANES), bf16),
            pltpu.VMEM((latent, LANES), f32),
            pltpu.VMEM((nc, latent // nc, LANES), f32),
            pltpu.VMEM((latent // nc, LANES), f32),
            pltpu.VMEM((members, nx * nz * share, LANES), f32),
            pltpu.VMEM((members, nx * nz * share, LANES), f32),
            pltpu.VMEM((max(LANES, owners * share), LANES), f32),
            pltpu.VMEM((nx, nz * share, LANES), f32),
            pltpu.VMEM((nz, share, LANES), f32),
            pltpu.VMEM((nz, share, LANES), f32),
            pltpu.VMEM((share, LANES), f32),
            pltpu.VMEM((members, share, LANES), f32),
            dma((7 + points // (2 * slab),)),
            dma(()), dma(()), dma(()), dma(()), dma(()), dma((nz,)), dma(()), dma(()),
            dma(()), dma(()), dma(()), dma(()), dma(()), dma(()), dma(()), dma(()), dma(()), dma(()),
        ],
        compiler_params=pltpu.CompilerParams(
            collective_id=0, has_side_effects=True, vmem_limit_bytes=VMEM_LIMIT
        ),
    )(
        rows, wt, target, area_weight.reshape(points // LANES, LANES), var_weight.reshape(1, variables),
        edge_owner.T, edge_row.T, edge_weight.T,
    )
    grad_weight, mesh_grad = pl.pallas_call(
        finish_kernel,
        in_specs=[vmem] * 3,
        out_specs=[vmem] * 2,
        out_shape=[
            jax.ShapeDtypeStruct((members * share, variables), f32),
            jax.ShapeDtypeStruct((mesh_rows, latent), bf16),
        ],
        compiler_params=pltpu.CompilerParams(vmem_limit_bytes=VMEM_LIMIT),
    )(gw, mesh_sum, wt)
    return grad_weight, mesh_grad[None]


def solution(mesh):
    return jax.shard_map(
        per_device,
        mesh=mesh,
        in_specs=(
            P("ens", "grid", None),
            P(),
            P(None, "grid"),
            P("grid"),
            P(),
            P("grid", None),
            P("grid", None),
            P("grid", None),
        ),
        out_specs=(P("grid", None), P("ens", "grid", None)),
        check_vma=False,
    )
```

```python
import functools
import math

import jax
import jax.numpy as jnp
from jax import lax
from jax.experimental import pallas as pl
from jax.experimental.pallas import tpu as pltpu
from jax.sharding import PartitionSpec as P

smooth_width = 0.1
LANES = 128
STEPS = 32000.0
VMEM_LIMIT = 62 * 1024 * 1024


def softened_sign(difference):
    return difference * lax.rsqrt(difference * difference + smooth_width * smooth_width)


def round_up(n, m):
    return (n + m - 1) // m * m


def score_block(x, t, scale):
    n = len(x)
    total = [None] * n
    for i in range(n):
        for j in range(i + 1, n):
            a = softened_sign(x[i] - x[j])
            total[i] = a if total[i] is None else total[i] + a
            total[j] = -a if total[j] is None else total[j] - a
    out = []
    for i in range(n):
        raw = softened_sign(x[i] - t) * (1.0 / n) - total[i] * (1.0 / (n * (n - 1)))
        out.append((scale * raw).astype(jnp.bfloat16))
    return out


def grid_shape(owners):
    return (owners // 16, 8, 2) if owners >= 16 else (owners // 4, 2, 2)


def place_slots(own_ref, row_ref, ew_ref, slot_s, x_s):
    owners, points = slot_s.shape
    neigh = own_ref.shape[0]
    tri = (
        lax.broadcasted_iota(jnp.int32, (LANES, LANES), 0)
        <= lax.broadcasted_iota(jnp.int32, (LANES, LANES), 1)
    ).astype(jnp.float32).astype(jnp.bfloat16)
    nx, nz, nc = grid_shape(owners)
    at = lax.broadcasted_iota(jnp.int32, (owners, LANES), 0)
    z_id = lax.shift_right_logical(at, int(math.log2(nx * nc)))
    x_id = jnp.bitwise_and(lax.shift_right_logical(at, int(math.log2(nc))), nx - 1)
    owner_id = (x_id * nz + z_id) * nc + jnp.bitwise_and(at, nc - 1)
    line = lax.broadcasted_iota(jnp.int32, (16, LANES), 0)
    blank = jnp.zeros((LANES - 16, LANES), jnp.float32)
    carry = jnp.zeros((owners, 1), jnp.float32)
    for b in range(0, points, LANES):
        hit = jnp.zeros((owners, LANES), jnp.float32)
        vals = jnp.zeros((16, LANES), jnp.float32)
        owns = jnp.zeros((16, LANES), jnp.float32)
        for k in range(neigh):
            own = own_ref[k : k + 1, b : b + LANES]
            hit = jnp.where(own == owner_id, 1.0, hit)
            rest = ew_ref[k : k + 1, b : b + LANES]
            for i in range(3):
                piece = rest.astype(jnp.bfloat16).astype(jnp.float32)
                vals = jnp.where(line == 4 * k + i, piece, vals)
                rest = rest - piece
            vals = jnp.where(line == 4 * k + 3, row_ref[k : k + 1, b : b + LANES].astype(jnp.float32), vals)
            owns = jnp.where((line >= 4 * k) & (line < 4 * k + 4), own.astype(jnp.float32), owns)
        count = carry + jnp.dot(hit.astype(jnp.bfloat16), tri, preferred_element_type=jnp.float32)
        slot_s[:, b : b + LANES] = jnp.where(hit > 0.0, count, 0.0)
        carry = count[:, LANES - 1 : LANES]
        x_s[b : b + LANES, 0:LANES] = jnp.concatenate([vals, blank], axis=0).T.astype(jnp.bfloat16)
        x_s[b : b + LANES, LANES:] = jnp.concatenate([owns, blank], axis=0).T.astype(jnp.bfloat16)


def far_first(n):
    return sorted(range(n), key=lambda o: -min(o, n - o))


def bulk_wait(ref, sem):
    pltpu.make_async_copy(ref, ref, sem).wait()


def fused_kernel(
    cfg,
    hidden_hbm, wt_hbm, target_hbm, area_hbm, var_hbm, own_hbm, row_hbm, ew_hbm,
    gw_out, mesh_out,
    hid, wt_raw, target, area, var, own, row, ew,
    wt, w_col, x_send, x_recv, unit_s, g_send, g_recv,
    slot_s, x_s, a_s, sel_s, wb_s, gt_s, out_buf, in_buf,
    d_send, d_recv, gw_s, half_recv, y_send, y_recv, q_s, gq_s, q_recv, p_send, p_recv, r_send, r_recv,
    in_sem, x_ss, x_rs, g_ss, g_rs, m_ss, m_rs, d_ss, d_rs, h_ss, h_rs, y_ss, y_rs, q_ss, q_rs, p_ss, p_rs, r_ss, r_rs,
):
    variables, slots, share, normalizer = cfg
    members, grows, slab = g_send.shape
    owners, points = slot_s.shape
    latent = hid.shape[1]
    mesh_rows = d_send.shape[1]
    e, g = lax.axis_index("ens"), lax.axis_index("grid")
    nx, nz, nc = grid_shape(owners)
    nu = nx * nc
    z, core = lax.rem(g // nc, nz), lax.rem(g, nc)
    x_at = g // (nz * nc)
    u = x_at * nc + core

    def plane_peer(i):
        return ((i // nc) * nz + z) * nc + lax.rem(i, nc)

    def column_peer(i):
        return ((u // nc) * nz + i) * nc + lax.rem(u, nc)

    def send(src, dst, ss, rs, axis, peer, me):
        @pl.when(peer != me)
        def _():
            pltpu.make_async_remote_copy(
                src_ref=src, dst_ref=dst, send_sem=ss, recv_sem=rs,
                device_id={axis: peer}, device_id_type=pl.DeviceIdType.MESH,
            ).start()

        @pl.when(peer == me)
        def _():
            pltpu.make_async_copy(src, dst, rs).start()

    barrier = pltpu.get_barrier_semaphore()

    def greet_ens(i, _):
        pl.semaphore_signal(barrier, inc=1, device_id={"ens": lax.rem(e + i, members)}, device_id_type=pl.DeviceIdType.MESH)
        return 0

    def greet_plane(i, _):
        pl.semaphore_signal(barrier, inc=1, device_id={"grid": plane_peer(lax.rem(u + i, nu))}, device_id_type=pl.DeviceIdType.MESH)
        return 0

    def greet_column(i, _):
        pl.semaphore_signal(barrier, inc=1, device_id={"grid": column_peer(lax.rem(z + i, nz))}, device_id_type=pl.DeviceIdType.MESH)
        return 0

    chunk = 2 * slab
    loads = [pltpu.make_async_copy(wt_hbm, wt_raw, in_sem.at[0])]
    chunks = points // chunk
    order = [lax.rem(e // 2 + o, chunks) for o in far_first(chunks)]
    for c in order:
        rows = pl.ds(pl.multiple_of(c * chunk, chunk), chunk)
        loads.append(pltpu.make_async_copy(hidden_hbm.at[rows], hid.at[rows], in_sem.at[1 + c]))
    n_hid = len(loads)
    loads.append(
        pltpu.make_async_copy(
            target_hbm.at[:, pl.ds(pl.multiple_of(e * slab, slab), slab)], target, in_sem.at[n_hid]
        )
    )
    for i, (s, d) in enumerate(((area_hbm, area), (var_hbm, var), (own_hbm, own), (row_hbm, row), (ew_hbm, ew))):
        loads.append(pltpu.make_async_copy(s, d, in_sem.at[n_hid + 1 + i]))
    for cp in loads:
        cp.start()
    lax.fori_loop(1, members, greet_ens, 0)
    lax.fori_loop(1, nu, greet_plane, 0)
    lax.fori_loop(1, nz, greet_column, 0)

    loads[0].wait()
    whole = variables // 16 * 16
    wt[0:whole, :] = wt_raw[0:whole, :]
    wt[whole : whole + 16, :] = jnp.concatenate(
        [wt_raw[whole:variables, :], jnp.zeros((whole + 16 - variables, latent), jnp.bfloat16)], axis=0
    )
    wt[whole + 16 :, :] = jnp.zeros((LANES - whole - 16, latent), jnp.bfloat16)
    for b in range(0, latent, LANES):
        w_col[b : b + LANES, :] = wt[:, b : b + LANES].astype(jnp.float32).T.astype(jnp.bfloat16)

    tail_row = lax.broadcasted_iota(jnp.int32, (8, slab), 0)
    zero_rows = jnp.zeros((8, slab), jnp.int32)
    for t, c in enumerate(order):
        loads[1 + t].wait()
        rows = pl.ds(pl.multiple_of(c * chunk, chunk), chunk)
        part = jnp.dot(hid[rows, :], w_col[...], preferred_element_type=jnp.float32)
        for s in range(2):
            m = 2 * c + s
            block = part[s * slab : (s + 1) * slab, :].T[: whole + 8, :]
            top = jnp.max(jnp.abs(block), axis=0, keepdims=True)
            power = jnp.ceil(jnp.log2(jnp.maximum(top, 1e-30)))
            code = jnp.floor(block * (jnp.exp2(-power) * STEPS) + 0.5).astype(jnp.int32)
            tail = jnp.where(tail_row == variables - whole, power.astype(jnp.int32), code[whole:, :])
            x_send[m, 0:whole, :] = code[0:whole, :].astype(jnp.int16)
            x_send[m, whole : whole + 16, :] = jnp.concatenate([tail, zero_rows], axis=0).astype(jnp.int16)
        if t == 0:
            pl.semaphore_wait(barrier, members + nu + nz - 3)
        for s in range(2):
            m = 2 * c + s
            send(x_send.at[m], x_recv.at[e], x_ss, x_rs, "ens", m, e)

    for cp in loads[n_hid:]:
        cp.wait()
    place_slots(own, row, ew, slot_s, x_s)
    step = nu * slots
    both = min(2, nz)
    groups = nz // both
    want = lax.broadcasted_iota(jnp.int32, (slots, LANES), 0).astype(jnp.float32) + 1.0
    line = lax.broadcasted_iota(jnp.int32, (LANES, LANES), 0)
    lane = lax.broadcasted_iota(jnp.int32, (LANES, LANES), 1)
    spread = jnp.where((lax.rem(line, 4) == 3) == (lane == variables), 1.0, 0.0).astype(jnp.bfloat16)

    def one_hot(t, _):
        at = lax.rem(z // both + 1 + t, groups)
        base = pl.multiple_of(at * (both * nu), both * nu)
        slot_g = slot_s[pl.ds(base, both * nu), :]
        first = at * (both * step)
        for j in range(both * nu):
            rows = pl.ds(pl.multiple_of(first + j * slots, slots), slots)
            for b in range(0, points, LANES):
                same = slot_g[j : j + 1, b : b + LANES] == want
                a_s[rows, b : b + LANES] = jnp.where(same, 1.0, 0.0).astype(jnp.bfloat16)
        rows = pl.ds(pl.multiple_of(first, both * step), both * step)
        ext = jnp.dot(a_s[rows, :], x_s[...], preferred_element_type=jnp.float32)
        for j in range(both * nu):
            owner = (((j % nu) // nc) * nz + at * both + j // nu) * nc + j % nc
            part = ext[j * slots : (j + 1) * slots, :]
            mine = part[:, LANES:] == owner.astype(jnp.float32)
            sel_s[j * slots : (j + 1) * slots, :] = jnp.where(mine, part[:, 0:LANES], 0.0).astype(jnp.bfloat16)
        wb_s[rows, :] = jnp.dot(sel_s[...], spread, preferred_element_type=jnp.float32)
        return 0

    early = (groups + 1) // 2
    lax.fori_loop(0, early, one_hot, 0)
    vcol = jnp.broadcast_to(
        jnp.concatenate([var[...], jnp.zeros((1, LANES - variables), jnp.float32)], axis=1), (LANES, LANES)
    ).T
    scale = vcol * area[pl.ds(e, 1), :]
    q_s[0:LANES, :] = scale

    bulk_wait(x_recv, x_rs)

    def wide_block(m, at):
        return x_recv[m, at, :].astype(jnp.int32).astype(jnp.float32)

    for m in range(members):
        power = wide_block(m, pl.ds(whole, 16))[variables - whole : variables - whole + 1, :]
        unit_s[m] = jnp.broadcast_to(jnp.exp2(power) * (1.0 / STEPS), (16, slab))

    def score(r, t):
        at = pl.ds(r, 16)
        got = score_block([wide_block(m, at) * unit_s[m] for m in range(members)], t, q_s[at, :])
        for m in range(members):
            g_send[m, at, :] = got[m]

    def score_step(i, _):
        r = pl.multiple_of(i * 16, 16)
        score(r, target[pl.ds(r, 16), :])
        return 0

    lax.fori_loop(0, variables // 16, score_step, 0)
    score(
        whole,
        jnp.concatenate(
            [target[whole:variables, :], jnp.zeros((whole + 16 - variables, slab), jnp.float32)], axis=0
        ),
    )
    for o in far_first(members):
        m = lax.rem(e + o, members)
        send(g_send.at[m], g_recv.at[e], g_ss, g_rs, "ens", m, e)

    lax.fori_loop(early, groups, one_hot, 0)

    bulk_wait(g_recv, g_rs)
    pad = jnp.zeros((LANES - grows, LANES), jnp.float32)
    for s in range(members):
        block = jnp.concatenate([g_recv[s].astype(jnp.float32), pad], axis=0).T
        gt_s[s * LANES : (s + 1) * LANES, :] = jnp.where(lane == variables, 1.0, block).astype(jnp.bfloat16)
    def messages(t, _):
        at = lax.rem(z // both + 1 + t, groups)
        rows = pl.ds(pl.multiple_of(at * (both * step), both * step), both * step)
        picked = jnp.dot(a_s[rows, :], gt_s[...], preferred_element_type=jnp.float32)
        zs = pl.ds(at * both, both)
        out_buf[zs] = (picked * wb_s[rows, :]).astype(jnp.bfloat16).reshape(both, nu, slots, LANES)
        for o in far_first(nx):
            for c in range(nc):
                j = lax.rem(x_at + o, nx) * nc + lax.rem(core + 1 + c, nc)
                send(out_buf.at[zs, j], in_buf.at[zs, u], m_ss, m_rs.at[at], "grid", plane_peer(j), g)
        return 0

    lax.fori_loop(0, 1, messages, 0)

    wide = jnp.concatenate([g_recv[s] for s in range(members)], axis=1)
    for b in range(0, latent, 2 * LANES):
        part = jnp.dot(wide, hid[:, b : b + 2 * LANES], preferred_element_type=jnp.float32)
        for c in range(0, 2 * LANES, LANES):
            block = jnp.concatenate([part[:, c : c + LANES], pad], axis=0).T
            pairs = LANES // (nc * members * share)
            gw_s[(b + c) // LANES * pairs : ((b + c) // LANES + 1) * pairs] = block.reshape(
                pairs, nc, members * share, LANES
            )
    half = pltpu.make_async_remote_copy(
        src_ref=gw_s.at[:, 1 - core], dst_ref=half_recv, send_sem=h_ss, recv_sem=h_rs,
        device_id={"grid": g + 1 - 2 * core}, device_id_type=pl.DeviceIdType.MESH,
    )
    half.start()

    lax.fori_loop(1, max(1, groups // 2), messages, 0)

    half.wait_recv()
    total = gw_s[:, core] + half_recv[...]
    for m in range(members):
        y_send[m] = total[:, m * share : (m + 1) * share, :]
    for o in far_first(members):
        m = lax.rem(e + o, members)
        send(y_send.at[m], y_recv.at[e], y_ss, y_rs, "ens", m, e)

    lax.fori_loop(max(1, groups // 2), groups, messages, 0)

    pick = (lax.broadcasted_iota(jnp.int32, (16, LANES), 1) == variables).astype(jnp.float32).astype(jnp.bfloat16)
    ids = lax.broadcasted_iota(jnp.int32, (mesh_rows, step), 0).astype(jnp.float32)

    def mesh_part(t, _):
        at = lax.rem(z // both + 1 + t, groups)
        zs = pl.ds(at * both, both)
        bulk_wait(in_buf.at[zs], m_rs.at[at])
        for i in range(both):
            zi = at * both + i
            block = in_buf[zi].reshape(step, LANES)
            place = lax.dot_general(pick, block, (((1,), (1,)), ((), ())), preferred_element_type=jnp.float32)
            picker = jnp.where(place[0:1, :] == ids, 1.0, 0.0).astype(jnp.bfloat16)
            d_send[zi] = jnp.dot(picker, block, preferred_element_type=jnp.float32).astype(jnp.bfloat16)
            send(d_send.at[zi], d_recv.at[z], d_ss, d_rs, "grid", column_peer(zi), g)
        return 0

    lax.fori_loop(0, groups // 2, mesh_part, 0)

    bulk_wait(y_recv, y_rs)
    total = y_recv[0]
    for m in range(1, members):
        total = total + y_recv[m]
    gq_s[...] = total.reshape(nx, nz, share, LANES)
    for j in range(nx):
        send(gq_s.at[j], q_recv.at[x_at], q_ss, q_rs, "grid", plane_peer(j * nc + core), g)

    lax.fori_loop(groups // 2, groups - 1, mesh_part, 0)

    bulk_wait(q_recv, q_rs)
    total = q_recv[0]
    for j in range(1, nx):
        total = total + q_recv[j]
    p_send[...] = total
    for j in range(nz):
        send(p_send.at[j], p_recv.at[z], p_ss, p_rs, "grid", column_peer(j), g)

    lax.fori_loop(groups - 1, groups, mesh_part, 0)

    bulk_wait(p_recv, p_rs)
    r_send[...] = jnp.sum(p_recv[...], axis=0) * normalizer
    for m in range(members):
        send(r_send, r_recv.at[e], r_ss, r_rs, "ens", m, e)
    bulk_wait(d_recv, d_rs)
    acc = d_recv[0].astype(jnp.float32)
    for j in range(1, nz):
        acc = acc + d_recv[j].astype(jnp.float32)
    mesh_out[...] = acc.astype(jnp.bfloat16)
    bulk_wait(r_recv, r_rs)
    for m in range(members):
        gw_out[share * m : share * (m + 1), :] = r_recv[m]

    bulk_wait(x_send.at[pl.ds(0, members - 1)], x_ss)
    bulk_wait(g_send.at[pl.ds(0, members - 1)], g_ss)
    bulk_wait(out_buf.at[:, pl.ds(0, nu - 1)], m_ss)
    bulk_wait(d_send.at[pl.ds(0, nz - 1)], d_ss)
    half.wait_send()
    bulk_wait(y_send.at[pl.ds(0, members - 1)], y_ss)
    bulk_wait(q_recv.at[pl.ds(0, nx - 1)], q_ss)
    bulk_wait(p_send.at[pl.ds(0, nz - 1)], p_ss)
    bulk_wait(r_recv.at[pl.ds(0, members - 1)], r_ss)


def finish_kernel(gw_ref, mesh_ref, wt_ref, gw_out, mesh_out):
    variables, latent = wt_ref.shape
    gw_out[...] = gw_ref[:, 0:variables]
    whole = variables // 16 * 16
    wide = jnp.concatenate(
        [wt_ref[whole:variables, :], jnp.zeros((whole + 16 - variables, latent), jnp.bfloat16)], axis=0
    )
    total = jnp.dot(mesh_ref[:, 0:whole], wt_ref[0:whole, :], preferred_element_type=jnp.float32)
    total = total + jnp.dot(mesh_ref[:, whole : whole + 16], wide, preferred_element_type=jnp.float32)
    mesh_out[...] = total.astype(jnp.bfloat16)


def per_device(hidden, weight, target, area_weight, var_weight, edge_owner, edge_row, edge_weight):
    rows = hidden[0]
    points, latent = rows.shape
    variables = weight.shape[1]
    neigh = edge_owner.shape[1]
    members = lax.axis_size("ens")
    owners = lax.axis_size("grid")
    mesh_rows = points // 8
    slab = points // members
    assert slab == LANES and variables < LANES
    capacity = max(2, (5 * points * neigh + 4 * owners - 1) // (4 * owners))
    slots = round_up(capacity, 16)
    grows = round_up(variables, 16)
    assert variables % 16 in range(1, 8)
    nx, nz, nc = grid_shape(owners)
    nu = nx * nc
    share = latent // (owners * members)
    normalizer = 1.0 / math.sqrt(float(points * owners * members))
    f32, bf16, i32 = jnp.float32, jnp.bfloat16, jnp.int32
    hbm = pl.BlockSpec(memory_space=pltpu.HBM)
    vmem = pl.BlockSpec(memory_space=pltpu.VMEM)
    dma = pltpu.SemaphoreType.DMA
    wt = weight.T
    gw, mesh_sum = pl.pallas_call(
        functools.partial(fused_kernel, (variables, slots, share, normalizer)),
        in_specs=[hbm] * 8,
        out_specs=[vmem] * 2,
        out_shape=[
            jax.ShapeDtypeStruct((members * share, LANES), f32),
            jax.ShapeDtypeStruct((mesh_rows, LANES), bf16),
        ],
        scratch_shapes=[
            pltpu.VMEM((points, latent), bf16),
            pltpu.VMEM((variables, latent), bf16),
            pltpu.VMEM((variables, slab), f32),
            pltpu.VMEM((points // LANES, LANES), f32),
            pltpu.VMEM((1, variables), f32),
            pltpu.VMEM((neigh, points), i32),
            pltpu.VMEM((neigh, points), i32),
            pltpu.VMEM((neigh, points), f32),
            pltpu.VMEM((LANES, latent), bf16),
            pltpu.VMEM((latent, LANES), bf16),
            pltpu.VMEM((members, grows, slab), jnp.int16),
            pltpu.VMEM((members, grows, slab), jnp.int16),
            pltpu.VMEM((members, 16, slab), f32),
            pltpu.VMEM((members, grows, slab), bf16),
            pltpu.VMEM((members, grows, slab), bf16),
            pltpu.VMEM((owners, points), f32),
            pltpu.VMEM((points, 2 * LANES), bf16),
            pltpu.VMEM((owners * slots, points), bf16),
            pltpu.VMEM((min(2, nz) * nu * slots, LANES), bf16),
            pltpu.VMEM((owners * slots, LANES), f32),
            pltpu.VMEM((points, LANES), bf16),
            pltpu.VMEM((nz, nu, slots, LANES), bf16),
            pltpu.VMEM((nz, nu, slots, LANES), bf16),
            pltpu.VMEM((nz, mesh_rows, LANES), bf16),
            pltpu.VMEM((nz, mesh_rows, LANES), bf16),
            pltpu.VMEM((nx * nz, nc, members * share, LANES), f32),
            pltpu.VMEM((nx * nz, members * share, LANES), f32),
            pltpu.VMEM((members, nx * nz, share, LANES), f32),
            pltpu.VMEM((members, nx * nz, share, LANES), f32),
            pltpu.VMEM((LANES, LANES), f32),
            pltpu.VMEM((nx, nz, share, LANES), f32),
            pltpu.VMEM((nx, nz, share, LANES), f32),
            pltpu.VMEM((nz, share, LANES), f32),
            pltpu.VMEM((nz, share, LANES), f32),
            pltpu.VMEM((share, LANES), f32),
            pltpu.VMEM((members, share, LANES), f32),
            dma((7 + points // (2 * slab),)),
            dma(()), dma(()), dma(()), dma(()), dma(()), dma((nz,)), dma(()), dma(()),
            dma(()), dma(()), dma(()), dma(()), dma(()), dma(()), dma(()), dma(()), dma(()), dma(()),
        ],
        compiler_params=pltpu.CompilerParams(
            collective_id=0, has_side_effects=True, vmem_limit_bytes=VMEM_LIMIT
        ),
    )(
        rows, wt, target, area_weight.reshape(points // LANES, LANES), var_weight.reshape(1, variables),
        edge_owner.T, edge_row.T, edge_weight.T,
    )
    grad_weight, mesh_grad = pl.pallas_call(
        finish_kernel,
        in_specs=[vmem] * 3,
        out_specs=[vmem] * 2,
        out_shape=[
            jax.ShapeDtypeStruct((members * share, variables), f32),
            jax.ShapeDtypeStruct((mesh_rows, latent), bf16),
        ],
        compiler_params=pltpu.CompilerParams(vmem_limit_bytes=VMEM_LIMIT),
    )(gw, mesh_sum, wt)
    return grad_weight, mesh_grad[None]


def solution(mesh):
    return jax.shard_map(
        per_device,
        mesh=mesh,
        in_specs=(
            P("ens", "grid", None),
            P(),
            P(None, "grid"),
            P("grid"),
            P(),
            P("grid", None),
            P("grid", None),
            P("grid", None),
        ),
        out_specs=(P("grid", None), P("ens", "grid", None)),
        check_vma=False,
    )
```

```python
import functools
import math

import jax
import jax.numpy as jnp
from jax import lax
from jax.experimental import pallas as pl
from jax.experimental.pallas import tpu as pltpu
from jax.sharding import PartitionSpec as P

smooth_width = 0.1
LANES = 128
STEPS = 32000.0
VMEM_LIMIT = 62 * 1024 * 1024


def softened_sign(difference):
    return difference * lax.rsqrt(difference * difference + smooth_width * smooth_width)


def round_up(n, m):
    return (n + m - 1) // m * m


def score_block(x, t, scale):
    n = len(x)
    total = [None] * n
    for i in range(n):
        for j in range(i + 1, n):
            a = softened_sign(x[i] - x[j])
            total[i] = a if total[i] is None else total[i] + a
            total[j] = -a if total[j] is None else total[j] - a
    out = []
    for i in range(n):
        raw = softened_sign(x[i] - t) * (1.0 / n) - total[i] * (1.0 / (n * (n - 1)))
        out.append((scale * raw).astype(jnp.bfloat16))
    return out


def grid_shape(owners):
    return (owners // 16, 8, 2) if owners >= 16 else (owners // 4, 2, 2)


def place_slots(own_ref, row_ref, ew_ref, slot_s, x_s):
    owners, points = slot_s.shape
    neigh = own_ref.shape[0]
    tri = (
        lax.broadcasted_iota(jnp.int32, (LANES, LANES), 0)
        <= lax.broadcasted_iota(jnp.int32, (LANES, LANES), 1)
    ).astype(jnp.float32).astype(jnp.bfloat16)
    nx, nz, nc = grid_shape(owners)
    at = lax.broadcasted_iota(jnp.int32, (owners, LANES), 0)
    z_id = lax.shift_right_logical(at, int(math.log2(nx * nc)))
    x_id = jnp.bitwise_and(lax.shift_right_logical(at, int(math.log2(nc))), nx - 1)
    owner_id = (x_id * nz + z_id) * nc + jnp.bitwise_and(at, nc - 1)
    line = lax.broadcasted_iota(jnp.int32, (16, LANES), 0)
    blank = jnp.zeros((LANES - 16, LANES), jnp.float32)
    carry = jnp.zeros((owners, 1), jnp.float32)
    for b in range(0, points, LANES):
        hit = jnp.zeros((owners, LANES), jnp.float32)
        vals = jnp.zeros((16, LANES), jnp.float32)
        owns = jnp.zeros((16, LANES), jnp.float32)
        for k in range(neigh):
            own = own_ref[k : k + 1, b : b + LANES]
            hit = jnp.where(own == owner_id, 1.0, hit)
            rest = ew_ref[k : k + 1, b : b + LANES]
            for i in range(3):
                piece = rest.astype(jnp.bfloat16).astype(jnp.float32)
                vals = jnp.where(line == 4 * k + i, piece, vals)
                rest = rest - piece
            vals = jnp.where(line == 4 * k + 3, row_ref[k : k + 1, b : b + LANES].astype(jnp.float32), vals)
            owns = jnp.where((line >= 4 * k) & (line < 4 * k + 4), own.astype(jnp.float32), owns)
        count = carry + jnp.dot(hit.astype(jnp.bfloat16), tri, preferred_element_type=jnp.float32)
        slot_s[:, b : b + LANES] = jnp.where(hit > 0.0, count, 0.0)
        carry = count[:, LANES - 1 : LANES]
        x_s[b : b + LANES, 0:LANES] = jnp.concatenate([vals, blank], axis=0).T.astype(jnp.bfloat16)
        x_s[b : b + LANES, LANES:] = jnp.concatenate([owns, blank], axis=0).T.astype(jnp.bfloat16)


def far_first(n):
    return sorted(range(n), key=lambda o: -min(o, n - o))


def bulk_wait(ref, sem):
    pltpu.make_async_copy(ref, ref, sem).wait()


def fused_kernel(
    cfg,
    hidden_hbm, wt_hbm, target_hbm, area_hbm, var_hbm, own_hbm, row_hbm, ew_hbm,
    gw_out, mesh_out,
    hid, wt_raw, target, area, var, own, row, ew,
    wt, w_col, x_send, x_recv, unit_s, g_send, g_recv,
    slot_s, x_s, a_s, sel_s, wb_s, gt_s, out_buf, in_buf,
    d_send, d_recv, gw_s, half_recv, y_send, y_recv, q_s, gq_s, q_recv, p_send, p_recv, r_send, r_recv,
    in_sem, x_ss, x_rs, g_ss, g_rs, m_ss, m_rs, d_ss, d_rs, h_ss, h_rs, y_ss, y_rs, q_ss, q_rs, p_ss, p_rs, r_ss, r_rs,
):
    variables, slots, share, normalizer = cfg
    members, grows, slab = g_send.shape
    owners, points = slot_s.shape
    latent = hid.shape[1]
    mesh_rows = d_send.shape[1]
    e, g = lax.axis_index("ens"), lax.axis_index("grid")
    nx, nz, nc = grid_shape(owners)
    nu = nx * nc
    z, core = lax.rem(g // nc, nz), lax.rem(g, nc)
    x_at = g // (nz * nc)
    u = x_at * nc + core

    def plane_peer(i):
        return ((i // nc) * nz + z) * nc + lax.rem(i, nc)

    def column_peer(i):
        return ((u // nc) * nz + i) * nc + lax.rem(u, nc)

    def send(src, dst, ss, rs, axis, peer, me):
        @pl.when(peer != me)
        def _():
            pltpu.make_async_remote_copy(
                src_ref=src, dst_ref=dst, send_sem=ss, recv_sem=rs,
                device_id={axis: peer}, device_id_type=pl.DeviceIdType.MESH,
            ).start()

        @pl.when(peer == me)
        def _():
            pltpu.make_async_copy(src, dst, rs).start()

    barrier = pltpu.get_barrier_semaphore()

    def greet_ens(i, _):
        pl.semaphore_signal(barrier, inc=1, device_id={"ens": lax.rem(e + i, members)}, device_id_type=pl.DeviceIdType.MESH)
        return 0

    def greet_plane(i, _):
        pl.semaphore_signal(barrier, inc=1, device_id={"grid": plane_peer(lax.rem(u + i, nu))}, device_id_type=pl.DeviceIdType.MESH)
        return 0

    def greet_column(i, _):
        pl.semaphore_signal(barrier, inc=1, device_id={"grid": column_peer(lax.rem(z + i, nz))}, device_id_type=pl.DeviceIdType.MESH)
        return 0

    chunk = 2 * slab
    loads = [pltpu.make_async_copy(wt_hbm, wt_raw, in_sem.at[0])]
    chunks = points // chunk
    order = [lax.rem(e // 2 + o, chunks) for o in far_first(chunks)]
    for c in order:
        rows = pl.ds(pl.multiple_of(c * chunk, chunk), chunk)
        loads.append(pltpu.make_async_copy(hidden_hbm.at[rows], hid.at[rows], in_sem.at[1 + c]))
    n_hid = len(loads)
    loads.append(
        pltpu.make_async_copy(
            target_hbm.at[:, pl.ds(pl.multiple_of(e * slab, slab), slab)], target, in_sem.at[n_hid]
        )
    )
    for i, (s, d) in enumerate(((area_hbm, area), (var_hbm, var), (own_hbm, own), (row_hbm, row), (ew_hbm, ew))):
        loads.append(pltpu.make_async_copy(s, d, in_sem.at[n_hid + 1 + i]))
    for cp in loads:
        cp.start()
    lax.fori_loop(1, members, greet_ens, 0)
    lax.fori_loop(1, nu, greet_plane, 0)
    lax.fori_loop(1, nz, greet_column, 0)

    loads[0].wait()
    whole = variables // 16 * 16
    wt[0:whole, :] = wt_raw[0:whole, :]
    wt[whole : whole + 16, :] = jnp.concatenate(
        [wt_raw[whole:variables, :], jnp.zeros((whole + 16 - variables, latent), jnp.bfloat16)], axis=0
    )
    wt[whole + 16 :, :] = jnp.zeros((LANES - whole - 16, latent), jnp.bfloat16)
    for b in range(0, latent, LANES):
        w_col[b : b + LANES, :] = wt[:, b : b + LANES].astype(jnp.float32).T.astype(jnp.bfloat16)

    tail_row = lax.broadcasted_iota(jnp.int32, (8, slab), 0)
    zero_rows = jnp.zeros((8, slab), jnp.int32)
    for t, c in enumerate(order):
        loads[1 + t].wait()
        rows = pl.ds(pl.multiple_of(c * chunk, chunk), chunk)
        part = jnp.dot(hid[rows, :], w_col[...], preferred_element_type=jnp.float32)
        for s in range(2):
            m = 2 * c + s
            block = part[s * slab : (s + 1) * slab, :].T[: whole + 8, :]
            top = jnp.max(jnp.abs(block), axis=0, keepdims=True)
            power = jnp.ceil(jnp.log2(jnp.maximum(top, 1e-30)))
            code = jnp.floor(block * (jnp.exp2(-power) * STEPS) + 0.5).astype(jnp.int32)
            tail = jnp.where(tail_row == variables - whole, power.astype(jnp.int32), code[whole:, :])
            x_send[m, 0:whole, :] = code[0:whole, :].astype(jnp.int16)
            x_send[m, whole : whole + 16, :] = jnp.concatenate([tail, zero_rows], axis=0).astype(jnp.int16)
        if t == 0:
            pl.semaphore_wait(barrier, members + nu + nz - 3)
        for s in range(2):
            m = 2 * c + s
            send(x_send.at[m], x_recv.at[e], x_ss, x_rs, "ens", m, e)

    for cp in loads[n_hid:]:
        cp.wait()
    place_slots(own, row, ew, slot_s, x_s)
    step = nu * slots
    both = min(2, nz)
    groups = nz // both
    want = lax.broadcasted_iota(jnp.int32, (slots, LANES), 0).astype(jnp.float32) + 1.0
    line = lax.broadcasted_iota(jnp.int32, (LANES, LANES), 0)
    lane = lax.broadcasted_iota(jnp.int32, (LANES, LANES), 1)
    spread = jnp.where((lax.rem(line, 4) == 3) == (lane == variables), 1.0, 0.0).astype(jnp.bfloat16)

    def one_hot(t, _):
        at = lax.rem(z // both + 1 + t, groups)
        base = pl.multiple_of(at * (both * nu), both * nu)
        slot_g = slot_s[pl.ds(base, both * nu), :]
        first = at * (both * step)
        for j in range(both * nu):
            rows = pl.ds(pl.multiple_of(first + j * slots, slots), slots)
            for b in range(0, points, LANES):
                same = slot_g[j : j + 1, b : b + LANES] == want
                a_s[rows, b : b + LANES] = jnp.where(same, 1.0, 0.0).astype(jnp.bfloat16)
        rows = pl.ds(pl.multiple_of(first, both * step), both * step)
        ext = jnp.dot(a_s[rows, :], x_s[...], preferred_element_type=jnp.float32)
        for j in range(both * nu):
            owner = (((j % nu) // nc) * nz + at * both + j // nu) * nc + j % nc
            part = ext[j * slots : (j + 1) * slots, :]
            mine = part[:, LANES:] == owner.astype(jnp.float32)
            sel_s[j * slots : (j + 1) * slots, :] = jnp.where(mine, part[:, 0:LANES], 0.0).astype(jnp.bfloat16)
        wb_s[rows, :] = jnp.dot(sel_s[...], spread, preferred_element_type=jnp.float32)
        return 0

    lax.fori_loop(0, 1, one_hot, 0)
    vcol = jnp.broadcast_to(
        jnp.concatenate([var[...], jnp.zeros((1, LANES - variables), jnp.float32)], axis=1), (LANES, LANES)
    ).T
    scale = vcol * area[pl.ds(e, 1), :]
    q_s[0:LANES, :] = scale

    bulk_wait(x_recv, x_rs)

    def wide_block(m, at):
        return x_recv[m, at, :].astype(jnp.int32).astype(jnp.float32)

    for m in range(members):
        power = wide_block(m, pl.ds(whole, 16))[variables - whole : variables - whole + 1, :]
        unit_s[m] = jnp.broadcast_to(jnp.exp2(power) * (1.0 / STEPS), (16, slab))

    def score(r, t):
        at = pl.ds(r, 16)
        got = score_block([wide_block(m, at) * unit_s[m] for m in range(members)], t, q_s[at, :])
        for m in range(members):
            g_send[m, at, :] = got[m]

    def score_step(i, _):
        r = pl.multiple_of(i * 16, 16)
        score(r, target[pl.ds(r, 16), :])
        return 0

    lax.fori_loop(0, variables // 16, score_step, 0)
    score(
        whole,
        jnp.concatenate(
            [target[whole:variables, :], jnp.zeros((whole + 16 - variables, slab), jnp.float32)], axis=0
        ),
    )
    for o in far_first(members):
        m = lax.rem(e + o, members)
        send(g_send.at[m], g_recv.at[e], g_ss, g_rs, "ens", m, e)

    early = max(1, groups // 2)
    lax.fori_loop(1, early, one_hot, 0)

    bulk_wait(g_recv, g_rs)
    pad = jnp.zeros((LANES - grows, LANES), jnp.float32)
    for s in range(members):
        block = jnp.concatenate([g_recv[s].astype(jnp.float32), pad], axis=0).T
        gt_s[s * LANES : (s + 1) * LANES, :] = jnp.where(lane == variables, 1.0, block).astype(jnp.bfloat16)
    def messages(t, _):
        at = lax.rem(z // both + 1 + t, groups)
        rows = pl.ds(pl.multiple_of(at * (both * step), both * step), both * step)
        picked = jnp.dot(a_s[rows, :], gt_s[...], preferred_element_type=jnp.float32)
        zs = pl.ds(at * both, both)
        out_buf[zs] = (picked * wb_s[rows, :]).astype(jnp.bfloat16).reshape(both, nu, slots, LANES)
        for o in far_first(nx):
            for c in range(nc):
                j = lax.rem(x_at + o, nx) * nc + lax.rem(core + 1 + c, nc)
                send(out_buf.at[zs, j], in_buf.at[zs, u], m_ss, m_rs.at[at], "grid", plane_peer(j), g)
        return 0

    lax.fori_loop(0, early, messages, 0)

    wide = jnp.concatenate([g_recv[s] for s in range(members)], axis=1)
    for b in range(0, latent, 2 * LANES):
        part = jnp.dot(wide, hid[:, b : b + 2 * LANES], preferred_element_type=jnp.float32)
        for c in range(0, 2 * LANES, LANES):
            block = jnp.concatenate([part[:, c : c + LANES], pad], axis=0).T
            pairs = LANES // (nc * members * share)
            gw_s[(b + c) // LANES * pairs : ((b + c) // LANES + 1) * pairs] = block.reshape(
                pairs, nc, members * share, LANES
            )
    half = pltpu.make_async_remote_copy(
        src_ref=gw_s.at[:, 1 - core], dst_ref=half_recv, send_sem=h_ss, recv_sem=h_rs,
        device_id={"grid": g + 1 - 2 * core}, device_id_type=pl.DeviceIdType.MESH,
    )
    half.start()

    def late_messages(t, _):
        one_hot(t, 0)
        return messages(t, 0)

    middle = (early + groups) // 2
    lax.fori_loop(early, middle, late_messages, 0)

    half.wait_recv()
    total = gw_s[:, core] + half_recv[...]
    for m in range(members):
        y_send[m] = total[:, m * share : (m + 1) * share, :]
    for o in far_first(members):
        m = lax.rem(e + o, members)
        send(y_send.at[m], y_recv.at[e], y_ss, y_rs, "ens", m, e)

    lax.fori_loop(middle, groups, late_messages, 0)

    pick = (lax.broadcasted_iota(jnp.int32, (16, LANES), 1) == variables).astype(jnp.float32).astype(jnp.bfloat16)
    ids = lax.broadcasted_iota(jnp.int32, (mesh_rows, step), 0).astype(jnp.float32)

    def mesh_part(t, _):
        at = lax.rem(z // both + 1 + t, groups)
        zs = pl.ds(at * both, both)
        bulk_wait(in_buf.at[zs], m_rs.at[at])
        for i in range(both):
            zi = at * both + i
            block = in_buf[zi].reshape(step, LANES)
            place = lax.dot_general(pick, block, (((1,), (1,)), ((), ())), preferred_element_type=jnp.float32)
            picker = jnp.where(place[0:1, :] == ids, 1.0, 0.0).astype(jnp.bfloat16)
            d_send[zi] = jnp.dot(picker, block, preferred_element_type=jnp.float32).astype(jnp.bfloat16)
            send(d_send.at[zi], d_recv.at[z], d_ss, d_rs, "grid", column_peer(zi), g)
        return 0

    lax.fori_loop(0, groups // 2, mesh_part, 0)

    bulk_wait(y_recv, y_rs)
    total = y_recv[0]
    for m in range(1, members):
        total = total + y_recv[m]
    gq_s[...] = total.reshape(nx, nz, share, LANES)
    for j in range(nx):
        send(gq_s.at[j], q_recv.at[x_at], q_ss, q_rs, "grid", plane_peer(j * nc + core), g)

    lax.fori_loop(groups // 2, groups - 1, mesh_part, 0)

    bulk_wait(q_recv, q_rs)
    total = q_recv[0]
    for j in range(1, nx):
        total = total + q_recv[j]
    p_send[...] = total
    for j in range(nz):
        send(p_send.at[j], p_recv.at[z], p_ss, p_rs, "grid", column_peer(j), g)

    lax.fori_loop(groups - 1, groups, mesh_part, 0)

    bulk_wait(p_recv, p_rs)
    r_send[...] = jnp.sum(p_recv[...], axis=0) * normalizer
    for m in range(members):
        send(r_send, r_recv.at[e], r_ss, r_rs, "ens", m, e)
    bulk_wait(d_recv, d_rs)
    acc = d_recv[0].astype(jnp.float32)
    for j in range(1, nz):
        acc = acc + d_recv[j].astype(jnp.float32)
    mesh_out[...] = acc.astype(jnp.bfloat16)
    bulk_wait(r_recv, r_rs)
    for m in range(members):
        gw_out[share * m : share * (m + 1), :] = r_recv[m]

    bulk_wait(x_send.at[pl.ds(0, members - 1)], x_ss)
    bulk_wait(g_send.at[pl.ds(0, members - 1)], g_ss)
    bulk_wait(out_buf.at[:, pl.ds(0, nu - 1)], m_ss)
    bulk_wait(d_send.at[pl.ds(0, nz - 1)], d_ss)
    half.wait_send()
    bulk_wait(y_send.at[pl.ds(0, members - 1)], y_ss)
    bulk_wait(q_recv.at[pl.ds(0, nx - 1)], q_ss)
    bulk_wait(p_send.at[pl.ds(0, nz - 1)], p_ss)
    bulk_wait(r_recv.at[pl.ds(0, members - 1)], r_ss)


def finish_kernel(gw_ref, mesh_ref, wt_ref, gw_out, mesh_out):
    variables, latent = wt_ref.shape
    gw_out[...] = gw_ref[:, 0:variables]
    whole = variables // 16 * 16
    wide = jnp.concatenate(
        [wt_ref[whole:variables, :], jnp.zeros((whole + 16 - variables, latent), jnp.bfloat16)], axis=0
    )
    total = jnp.dot(mesh_ref[:, 0:whole], wt_ref[0:whole, :], preferred_element_type=jnp.float32)
    total = total + jnp.dot(mesh_ref[:, whole : whole + 16], wide, preferred_element_type=jnp.float32)
    mesh_out[...] = total.astype(jnp.bfloat16)


def per_device(hidden, weight, target, area_weight, var_weight, edge_owner, edge_row, edge_weight):
    rows = hidden[0]
    points, latent = rows.shape
    variables = weight.shape[1]
    neigh = edge_owner.shape[1]
    members = lax.axis_size("ens")
    owners = lax.axis_size("grid")
    mesh_rows = points // 8
    slab = points // members
    assert slab == LANES and variables < LANES
    capacity = max(2, (5 * points * neigh + 4 * owners - 1) // (4 * owners))
    slots = round_up(capacity, 16)
    grows = round_up(variables, 16)
    assert variables % 16 in range(1, 8)
    nx, nz, nc = grid_shape(owners)
    nu = nx * nc
    share = latent // (owners * members)
    normalizer = 1.0 / math.sqrt(float(points * owners * members))
    f32, bf16, i32 = jnp.float32, jnp.bfloat16, jnp.int32
    hbm = pl.BlockSpec(memory_space=pltpu.HBM)
    vmem = pl.BlockSpec(memory_space=pltpu.VMEM)
    dma = pltpu.SemaphoreType.DMA
    wt = weight.T
    gw, mesh_sum = pl.pallas_call(
        functools.partial(fused_kernel, (variables, slots, share, normalizer)),
        in_specs=[hbm] * 8,
        out_specs=[vmem] * 2,
        out_shape=[
            jax.ShapeDtypeStruct((members * share, LANES), f32),
            jax.ShapeDtypeStruct((mesh_rows, LANES), bf16),
        ],
        scratch_shapes=[
            pltpu.VMEM((points, latent), bf16),
            pltpu.VMEM((variables, latent), bf16),
            pltpu.VMEM((variables, slab), f32),
            pltpu.VMEM((points // LANES, LANES), f32),
            pltpu.VMEM((1, variables), f32),
            pltpu.VMEM((neigh, points), i32),
            pltpu.VMEM((neigh, points), i32),
            pltpu.VMEM((neigh, points), f32),
            pltpu.VMEM((LANES, latent), bf16),
            pltpu.VMEM((latent, LANES), bf16),
            pltpu.VMEM((members, grows, slab), jnp.int16),
            pltpu.VMEM((members, grows, slab), jnp.int16),
            pltpu.VMEM((members, 16, slab), f32),
            pltpu.VMEM((members, grows, slab), bf16),
            pltpu.VMEM((members, grows, slab), bf16),
            pltpu.VMEM((owners, points), f32),
            pltpu.VMEM((points, 2 * LANES), bf16),
            pltpu.VMEM((owners * slots, points), bf16),
            pltpu.VMEM((min(2, nz) * nu * slots, LANES), bf16),
            pltpu.VMEM((owners * slots, LANES), f32),
            pltpu.VMEM((points, LANES), bf16),
            pltpu.VMEM((nz, nu, slots, LANES), bf16),
            pltpu.VMEM((nz, nu, slots, LANES), bf16),
            pltpu.VMEM((nz, mesh_rows, LANES), bf16),
            pltpu.VMEM((nz, mesh_rows, LANES), bf16),
            pltpu.VMEM((nx * nz, nc, members * share, LANES), f32),
            pltpu.VMEM((nx * nz, members * share, LANES), f32),
            pltpu.VMEM((members, nx * nz, share, LANES), f32),
            pltpu.VMEM((members, nx * nz, share, LANES), f32),
            pltpu.VMEM((LANES, LANES), f32),
            pltpu.VMEM((nx, nz, share, LANES), f32),
            pltpu.VMEM((nx, nz, share, LANES), f32),
            pltpu.VMEM((nz, share, LANES), f32),
            pltpu.VMEM((nz, share, LANES), f32),
            pltpu.VMEM((share, LANES), f32),
            pltpu.VMEM((members, share, LANES), f32),
            dma((7 + points // (2 * slab),)),
            dma(()), dma(()), dma(()), dma(()), dma(()), dma((nz,)), dma(()), dma(()),
            dma(()), dma(()), dma(()), dma(()), dma(()), dma(()), dma(()), dma(()), dma(()), dma(()),
        ],
        compiler_params=pltpu.CompilerParams(
            collective_id=0, has_side_effects=True, vmem_limit_bytes=VMEM_LIMIT
        ),
    )(
        rows, wt, target, area_weight.reshape(points // LANES, LANES), var_weight.reshape(1, variables),
        edge_owner.T, edge_row.T, edge_weight.T,
    )
    grad_weight, mesh_grad = pl.pallas_call(
        finish_kernel,
        in_specs=[vmem] * 3,
        out_specs=[vmem] * 2,
        out_shape=[
            jax.ShapeDtypeStruct((members * share, variables), f32),
            jax.ShapeDtypeStruct((mesh_rows, latent), bf16),
        ],
        compiler_params=pltpu.CompilerParams(vmem_limit_bytes=VMEM_LIMIT),
    )(gw, mesh_sum, wt)
    return grad_weight, mesh_grad[None]


def solution(mesh):
    return jax.shard_map(
        per_device,
        mesh=mesh,
        in_specs=(
            P("ens", "grid", None),
            P(),
            P(None, "grid"),
            P("grid"),
            P(),
            P("grid", None),
            P("grid", None),
            P("grid", None),
        ),
        out_specs=(P("grid", None), P("ens", "grid", None)),
        check_vma=False,
    )
```

```python
import functools
import math

import jax
import jax.numpy as jnp
import numpy as np
from jax import lax
from jax.experimental import pallas as pl
from jax.experimental.pallas import tpu as pltpu
from jax.sharding import PartitionSpec as P

smooth_width = 0.1
LANES = 128
STEPS = 32000.0
VMEM_LIMIT = 62 * 1024 * 1024


def softened_sign(difference):
    return difference * lax.rsqrt(difference * difference + smooth_width * smooth_width)


def round_up(n, m):
    return (n + m - 1) // m * m


def score_block(x, t, scale):
    n = len(x)
    total = [None] * n
    for i in range(n):
        for j in range(i + 1, n):
            a = softened_sign(x[i] - x[j])
            total[i] = a if total[i] is None else total[i] + a
            total[j] = -a if total[j] is None else total[j] - a
    out = []
    for i in range(n):
        raw = softened_sign(x[i] - t) * (1.0 / n) - total[i] * (1.0 / (n * (n - 1)))
        out.append((scale * raw).astype(jnp.bfloat16))
    return out


def grid_shape(owners):
    return (owners // 16, 8, 2) if owners >= 16 else (owners // 4, 2, 2)


def place_slots(own_ref, row_ref, ew_ref, slot_s, x_s):
    owners, points = slot_s.shape
    neigh = own_ref.shape[0]
    tri = (
        lax.broadcasted_iota(jnp.int32, (LANES, LANES), 0)
        <= lax.broadcasted_iota(jnp.int32, (LANES, LANES), 1)
    ).astype(jnp.float32).astype(jnp.bfloat16)
    nx, nz, nc = grid_shape(owners)
    at = lax.broadcasted_iota(jnp.int32, (owners, LANES), 0)
    z_id = lax.shift_right_logical(at, int(math.log2(nx * nc)))
    x_id = jnp.bitwise_and(lax.shift_right_logical(at, int(math.log2(nc))), nx - 1)
    owner_id = (x_id * nz + z_id) * nc + jnp.bitwise_and(at, nc - 1)
    line = lax.broadcasted_iota(jnp.int32, (16, LANES), 0)
    blank = jnp.zeros((LANES - 16, LANES), jnp.float32)
    carry = jnp.zeros((owners, 1), jnp.float32)
    for b in range(0, points, LANES):
        hit = jnp.zeros((owners, LANES), jnp.float32)
        vals = jnp.zeros((16, LANES), jnp.float32)
        owns = jnp.zeros((16, LANES), jnp.float32)
        for k in range(neigh):
            own = own_ref[k : k + 1, b : b + LANES]
            hit = jnp.where(own == owner_id, 1.0, hit)
            rest = ew_ref[k : k + 1, b : b + LANES]
            for i in range(3):
                piece = rest.astype(jnp.bfloat16).astype(jnp.float32)
                vals = jnp.where(line == 4 * k + i, piece, vals)
                rest = rest - piece
            vals = jnp.where(line == 4 * k + 3, row_ref[k : k + 1, b : b + LANES].astype(jnp.float32), vals)
            owns = jnp.where((line >= 4 * k) & (line < 4 * k + 4), own.astype(jnp.float32), owns)
        count = carry + jnp.dot(hit.astype(jnp.bfloat16), tri, preferred_element_type=jnp.float32)
        slot_s[:, b : b + LANES] = jnp.where(hit > 0.0, count, 0.0)
        carry = count[:, LANES - 1 : LANES]
        x_s[b : b + LANES, 0:LANES] = jnp.concatenate([vals, blank], axis=0).T.astype(jnp.bfloat16)
        x_s[b : b + LANES, LANES:] = jnp.concatenate([owns, blank], axis=0).T.astype(jnp.bfloat16)


def packing(variables, slots, capacity, nu):
    used = variables + 1
    width = LANES - used
    pieces = -(-used // width)
    keep = round_up(-(-capacity * pieces // (pieces + 1)), 16)
    late, hosts = slots - keep, keep // pieces
    assert capacity - keep <= hosts and late <= LANES
    shift = np.zeros((LANES, pieces * LANES), np.float32)
    for v in range(used):
        shift[v, v // width * LANES + used + v % width] = 1
    grow = np.zeros((nu * keep, pieces * nu * late), np.float32)
    order = np.zeros((pieces * nu * hosts, nu * keep), np.float32)
    for o in range(nu):
        for i in range(hosts):
            for q in range(pieces):
                if i < late:
                    grow[o * keep + pieces * i + q, (q * nu + o) * late + i] = 1
                order[(q * nu + o) * hosts + i, o * keep + pieces * i + q] = 1
    return keep, pieces, [a.astype(jnp.bfloat16) for a in (shift, grow, order, shift.T.copy())]


def far_first(n):
    return sorted(range(n), key=lambda o: -min(o, n - o))


def bulk_wait(ref, sem):
    pltpu.make_async_copy(ref, ref, sem).wait()


def fused_kernel(
    cfg,
    hidden_hbm, wt_hbm, target_hbm, area_hbm, var_hbm, own_hbm, row_hbm, ew_hbm, plans_hbm,
    gw_out, mesh_out,
    hid, wt_raw, target, area, var, own, row, ew, shift_s, grow_s, order_s, back_s,
    wt, w_col, x_send, x_recv, unit_s, g_send, g_recv,
    slot_s, x_s, a_s, sel_s, wb_s, gt_s, out_buf, in_buf,
    d_send, d_recv, gw_s, half_recv, y_send, y_recv, q_s, gq_s, q_recv, p_send, p_recv, r_send, r_recv,
    in_sem, x_ss, x_rs, g_ss, g_rs, m_ss, m_rs, d_ss, d_rs, h_ss, h_rs, y_ss, y_rs, q_ss, q_rs, p_ss, p_rs, r_ss, r_rs,
):
    variables, slots, share, normalizer, pieces = cfg
    keep = out_buf.shape[2]
    late = slots - keep
    members, grows, slab = g_send.shape
    owners, points = slot_s.shape
    latent = hid.shape[1]
    mesh_rows = d_send.shape[1]
    e, g = lax.axis_index("ens"), lax.axis_index("grid")
    nx, nz, nc = grid_shape(owners)
    nu = nx * nc
    z, core = lax.rem(g // nc, nz), lax.rem(g, nc)
    x_at = g // (nz * nc)
    u = x_at * nc + core

    def plane_peer(i):
        return ((i // nc) * nz + z) * nc + lax.rem(i, nc)

    def column_peer(i):
        return ((u // nc) * nz + i) * nc + lax.rem(u, nc)

    def send(src, dst, ss, rs, axis, peer, me):
        @pl.when(peer != me)
        def _():
            pltpu.make_async_remote_copy(
                src_ref=src, dst_ref=dst, send_sem=ss, recv_sem=rs,
                device_id={axis: peer}, device_id_type=pl.DeviceIdType.MESH,
            ).start()

        @pl.when(peer == me)
        def _():
            pltpu.make_async_copy(src, dst, rs).start()

    barrier = pltpu.get_barrier_semaphore()

    def greet_ens(i, _):
        pl.semaphore_signal(barrier, inc=1, device_id={"ens": lax.rem(e + i, members)}, device_id_type=pl.DeviceIdType.MESH)
        return 0

    def greet_plane(i, _):
        pl.semaphore_signal(barrier, inc=1, device_id={"grid": plane_peer(lax.rem(u + i, nu))}, device_id_type=pl.DeviceIdType.MESH)
        return 0

    def greet_column(i, _):
        pl.semaphore_signal(barrier, inc=1, device_id={"grid": column_peer(lax.rem(z + i, nz))}, device_id_type=pl.DeviceIdType.MESH)
        return 0

    chunk = 2 * slab
    loads = [pltpu.make_async_copy(wt_hbm, wt_raw, in_sem.at[0])]
    chunks = points // chunk
    order = [lax.rem(e // 2 + o, chunks) for o in far_first(chunks)]
    for c in order:
        rows = pl.ds(pl.multiple_of(c * chunk, chunk), chunk)
        loads.append(pltpu.make_async_copy(hidden_hbm.at[rows], hid.at[rows], in_sem.at[1 + c]))
    n_hid = len(loads)
    loads.append(
        pltpu.make_async_copy(
            target_hbm.at[:, pl.ds(pl.multiple_of(e * slab, slab), slab)], target, in_sem.at[n_hid]
        )
    )
    for i, (s, d) in enumerate(((area_hbm, area), (var_hbm, var), (own_hbm, own), (row_hbm, row), (ew_hbm, ew))):
        loads.append(pltpu.make_async_copy(s, d, in_sem.at[n_hid + 1 + i]))
    start = 0
    for ref in (shift_s, grow_s, order_s, back_s):
        for b in range(0, ref.shape[1], LANES):
            rows = pl.ds(start, ref.shape[0])
            loads.append(
                pltpu.make_async_copy(plans_hbm.at[rows], ref.at[:, pl.ds(b, LANES)], in_sem.at[len(loads)])
            )
            start += ref.shape[0]
    for cp in loads:
        cp.start()
    lax.fori_loop(1, members, greet_ens, 0)
    lax.fori_loop(1, nu, greet_plane, 0)
    lax.fori_loop(1, nz, greet_column, 0)

    loads[0].wait()
    whole = variables // 16 * 16
    wt[0:whole, :] = wt_raw[0:whole, :]
    wt[whole : whole + 16, :] = jnp.concatenate(
        [wt_raw[whole:variables, :], jnp.zeros((whole + 16 - variables, latent), jnp.bfloat16)], axis=0
    )
    wt[whole + 16 :, :] = jnp.zeros((LANES - whole - 16, latent), jnp.bfloat16)
    for b in range(0, latent, LANES):
        w_col[b : b + LANES, :] = wt[:, b : b + LANES].astype(jnp.float32).T.astype(jnp.bfloat16)

    tail_row = lax.broadcasted_iota(jnp.int32, (8, slab), 0)
    zero_rows = jnp.zeros((8, slab), jnp.int32)
    for t, c in enumerate(order):
        loads[1 + t].wait()
        rows = pl.ds(pl.multiple_of(c * chunk, chunk), chunk)
        part = jnp.dot(hid[rows, :], w_col[...], preferred_element_type=jnp.float32)
        for s in range(2):
            m = 2 * c + s
            block = part[s * slab : (s + 1) * slab, :].T[: whole + 8, :]
            top = jnp.max(jnp.abs(block), axis=0, keepdims=True)
            power = jnp.ceil(jnp.log2(jnp.maximum(top, 1e-30)))
            code = jnp.floor(block * (jnp.exp2(-power) * STEPS) + 0.5).astype(jnp.int32)
            tail = jnp.where(tail_row == variables - whole, power.astype(jnp.int32), code[whole:, :])
            x_send[m, 0:whole, :] = code[0:whole, :].astype(jnp.int16)
            x_send[m, whole : whole + 16, :] = jnp.concatenate([tail, zero_rows], axis=0).astype(jnp.int16)
        if t == 0:
            pl.semaphore_wait(barrier, members + nu + nz - 3)
        for s in range(2):
            m = 2 * c + s
            send(x_send.at[m], x_recv.at[e], x_ss, x_rs, "ens", m, e)

    for cp in loads[n_hid:]:
        cp.wait()
    place_slots(own, row, ew, slot_s, x_s)
    step = nu * slots
    both = min(2, nz)
    groups = nz // both
    want = lax.broadcasted_iota(jnp.int32, (slots, LANES), 0).astype(jnp.float32) + 1.0
    line = lax.broadcasted_iota(jnp.int32, (LANES, LANES), 0)
    lane = lax.broadcasted_iota(jnp.int32, (LANES, LANES), 1)
    spread = jnp.where((lax.rem(line, 4) == 3) == (lane == variables), 1.0, 0.0).astype(jnp.bfloat16)

    def one_hot(t, _):
        at = lax.rem(z // both + 1 + t, groups)
        base = pl.multiple_of(at * (both * nu), both * nu)
        slot_g = slot_s[pl.ds(base, both * nu), :]
        first = at * (both * step)
        for j in range(both * nu):
            rows = pl.ds(pl.multiple_of(first + j * slots, slots), slots)
            for b in range(0, points, LANES):
                same = slot_g[j : j + 1, b : b + LANES] == want
                a_s[rows, b : b + LANES] = jnp.where(same, 1.0, 0.0).astype(jnp.bfloat16)
        rows = pl.ds(pl.multiple_of(first, both * step), both * step)
        ext = jnp.dot(a_s[rows, :], x_s[...], preferred_element_type=jnp.float32)
        for j in range(both * nu):
            owner = (((j % nu) // nc) * nz + at * both + j // nu) * nc + j % nc
            part = ext[j * slots : (j + 1) * slots, :]
            mine = part[:, LANES:] == owner.astype(jnp.float32)
            sel_s[j * slots : (j + 1) * slots, :] = jnp.where(mine, part[:, 0:LANES], 0.0).astype(jnp.bfloat16)
        wb_s[rows, :] = jnp.dot(sel_s[...], spread, preferred_element_type=jnp.float32)
        return 0

    lax.fori_loop(0, 1, one_hot, 0)
    vcol = jnp.broadcast_to(
        jnp.concatenate([var[...], jnp.zeros((1, LANES - variables), jnp.float32)], axis=1), (LANES, LANES)
    ).T
    scale = vcol * area[pl.ds(e, 1), :]
    q_s[0:LANES, :] = scale

    bulk_wait(x_recv, x_rs)

    def wide_block(m, at):
        return x_recv[m, at, :].astype(jnp.int32).astype(jnp.float32)

    for m in range(members):
        power = wide_block(m, pl.ds(whole, 16))[variables - whole : variables - whole + 1, :]
        unit_s[m] = jnp.broadcast_to(jnp.exp2(power) * (1.0 / STEPS), (16, slab))

    def score(r, t):
        at = pl.ds(r, 16)
        got = score_block([wide_block(m, at) * unit_s[m] for m in range(members)], t, q_s[at, :])
        for m in range(members):
            g_send[m, at, :] = got[m]

    def score_step(i, _):
        r = pl.multiple_of(i * 16, 16)
        score(r, target[pl.ds(r, 16), :])
        return 0

    lax.fori_loop(0, variables // 16, score_step, 0)
    score(
        whole,
        jnp.concatenate(
            [target[whole:variables, :], jnp.zeros((whole + 16 - variables, slab), jnp.float32)], axis=0
        ),
    )
    for o in far_first(members):
        m = lax.rem(e + o, members)
        send(g_send.at[m], g_recv.at[e], g_ss, g_rs, "ens", m, e)

    early = max(1, groups // 2)
    lax.fori_loop(1, early, one_hot, 0)

    bulk_wait(g_recv, g_rs)
    pad = jnp.zeros((LANES - grows, LANES), jnp.float32)
    for s in range(members):
        block = jnp.concatenate([g_recv[s].astype(jnp.float32), pad], axis=0).T
        gt_s[s * LANES : (s + 1) * LANES, :] = jnp.where(lane == variables, 1.0, block).astype(jnp.bfloat16)
    def messages(t, _):
        at = lax.rem(z // both + 1 + t, groups)
        rows = pl.ds(pl.multiple_of(at * (both * step), both * step), both * step)
        picked = jnp.dot(a_s[rows, :], gt_s[...], preferred_element_type=jnp.float32)
        zs = pl.ds(at * both, both)
        message = picked * wb_s[rows, :]
        for i in range(both):
            at_o = [i * step + o * slots for o in range(nu)]
            head = jnp.concatenate([message[k : k + keep, :] for k in at_o], axis=0)
            rest = jnp.concatenate([message[k + keep : k + slots, :] for k in at_o], axis=0).astype(jnp.bfloat16)
            moved = jnp.dot(rest, shift_s[...], preferred_element_type=jnp.float32).astype(jnp.bfloat16)
            moved = jnp.concatenate([moved[:, q * LANES : (q + 1) * LANES] for q in range(pieces)], axis=0)
            moved = jnp.dot(grow_s[...], moved, preferred_element_type=jnp.float32)
            out_buf[at * both + i] = (head + moved).astype(jnp.bfloat16).reshape(nu, keep, LANES)
        for o in far_first(nx):
            for c in range(nc):
                j = lax.rem(x_at + o, nx) * nc + lax.rem(core + 1 + c, nc)
                send(out_buf.at[zs, j], in_buf.at[zs, u], m_ss, m_rs.at[at], "grid", plane_peer(j), g)
        return 0

    lax.fori_loop(0, 1, messages, 0)

    wide = jnp.concatenate([g_recv[s] for s in range(members)], axis=1)
    for b in range(0, latent, 2 * LANES):
        part = jnp.dot(wide, hid[:, b : b + 2 * LANES], preferred_element_type=jnp.float32)
        for c in range(0, 2 * LANES, LANES):
            block = jnp.concatenate([part[:, c : c + LANES], pad], axis=0).T
            pairs = LANES // (nc * members * share)
            gw_s[(b + c) // LANES * pairs : ((b + c) // LANES + 1) * pairs] = block.reshape(
                pairs, nc, members * share, LANES
            )
    half = pltpu.make_async_remote_copy(
        src_ref=gw_s.at[:, 1 - core], dst_ref=half_recv, send_sem=h_ss, recv_sem=h_rs,
        device_id={"grid": g + 1 - 2 * core}, device_id_type=pl.DeviceIdType.MESH,
    )
    half.start()

    def late_messages(t, _):
        one_hot(t, 0)
        return messages(t, 0)

    lax.fori_loop(1, early, messages, 0)

    half.wait_recv()
    total = gw_s[:, core] + half_recv[...]
    for m in range(members):
        y_send[m] = total[:, m * share : (m + 1) * share, :]
    for o in far_first(members):
        m = lax.rem(e + o, members)
        send(y_send.at[m], y_recv.at[e], y_ss, y_rs, "ens", m, e)

    lax.fori_loop(early, groups, late_messages, 0)

    pick = (lax.broadcasted_iota(jnp.int32, (16, LANES), 1) == variables).astype(jnp.float32).astype(jnp.bfloat16)
    wide_step = round_up(nu * keep + nu * keep // pieces + 1, LANES)
    ids = lax.broadcasted_iota(jnp.int32, (mesh_rows, wide_step), 0).astype(jnp.float32)

    def mesh_part(t, _):
        at = lax.rem(z // both + 1 + t, groups)
        zs = pl.ds(at * both, both)
        bulk_wait(in_buf.at[zs], m_rs.at[at])
        for i in range(both):
            zi = at * both + i
            head = in_buf[zi].reshape(nu * keep, LANES)
            moved = jnp.dot(order_s[...], head, preferred_element_type=jnp.float32).astype(jnp.bfloat16)
            hosts = nu * keep // pieces
            moved = jnp.concatenate([moved[q * hosts : (q + 1) * hosts, :] for q in range(pieces)], axis=1)
            moved = jnp.dot(moved, back_s[...], preferred_element_type=jnp.float32).astype(jnp.bfloat16)
            empty = jnp.zeros((wide_step - nu * keep - hosts, LANES), jnp.bfloat16)
            block = jnp.concatenate([head, moved, empty], axis=0)
            place = lax.dot_general(pick, block, (((1,), (1,)), ((), ())), preferred_element_type=jnp.float32)
            picker = jnp.where(place[0:1, :] == ids, 1.0, 0.0).astype(jnp.bfloat16)
            d_send[zi] = jnp.dot(picker, block, preferred_element_type=jnp.float32).astype(jnp.bfloat16)
            send(d_send.at[zi], d_recv.at[z], d_ss, d_rs, "grid", column_peer(zi), g)
        return 0

    lax.fori_loop(0, groups // 2, mesh_part, 0)

    bulk_wait(y_recv, y_rs)
    total = y_recv[0]
    for m in range(1, members):
        total = total + y_recv[m]
    gq_s[...] = total.reshape(nx, nz, share, LANES)
    for j in range(nx):
        send(gq_s.at[j], q_recv.at[x_at], q_ss, q_rs, "grid", plane_peer(j * nc + core), g)

    lax.fori_loop(groups // 2, groups - 1, mesh_part, 0)

    bulk_wait(q_recv, q_rs)
    total = q_recv[0]
    for j in range(1, nx):
        total = total + q_recv[j]
    p_send[...] = total
    for j in range(nz):
        send(p_send.at[j], p_recv.at[z], p_ss, p_rs, "grid", column_peer(j), g)

    lax.fori_loop(groups - 1, groups, mesh_part, 0)

    bulk_wait(p_recv, p_rs)
    r_send[...] = jnp.sum(p_recv[...], axis=0) * normalizer
    for m in range(members):
        send(r_send, r_recv.at[e], r_ss, r_rs, "ens", m, e)
    bulk_wait(d_recv, d_rs)
    acc = d_recv[0].astype(jnp.float32)
    for j in range(1, nz):
        acc = acc + d_recv[j].astype(jnp.float32)
    mesh_out[...] = acc.astype(jnp.bfloat16)
    bulk_wait(r_recv, r_rs)
    for m in range(members):
        gw_out[share * m : share * (m + 1), :] = r_recv[m]

    bulk_wait(x_send.at[pl.ds(0, members - 1)], x_ss)
    bulk_wait(g_send.at[pl.ds(0, members - 1)], g_ss)
    bulk_wait(out_buf.at[:, pl.ds(0, nu - 1)], m_ss)
    bulk_wait(d_send.at[pl.ds(0, nz - 1)], d_ss)
    half.wait_send()
    bulk_wait(y_send.at[pl.ds(0, members - 1)], y_ss)
    bulk_wait(q_recv.at[pl.ds(0, nx - 1)], q_ss)
    bulk_wait(p_send.at[pl.ds(0, nz - 1)], p_ss)
    bulk_wait(r_recv.at[pl.ds(0, members - 1)], r_ss)


def finish_kernel(gw_ref, mesh_ref, wt_ref, gw_out, mesh_out):
    variables, latent = wt_ref.shape
    gw_out[...] = gw_ref[:, 0:variables]
    whole = variables // 16 * 16
    wide = jnp.concatenate(
        [wt_ref[whole:variables, :], jnp.zeros((whole + 16 - variables, latent), jnp.bfloat16)], axis=0
    )
    total = jnp.dot(mesh_ref[:, 0:whole], wt_ref[0:whole, :], preferred_element_type=jnp.float32)
    total = total + jnp.dot(mesh_ref[:, whole : whole + 16], wide, preferred_element_type=jnp.float32)
    mesh_out[...] = total.astype(jnp.bfloat16)


def per_device(hidden, weight, target, area_weight, var_weight, edge_owner, edge_row, edge_weight):
    rows = hidden[0]
    points, latent = rows.shape
    variables = weight.shape[1]
    neigh = edge_owner.shape[1]
    members = lax.axis_size("ens")
    owners = lax.axis_size("grid")
    mesh_rows = points // 8
    slab = points // members
    assert slab == LANES and variables < LANES
    capacity = max(2, (5 * points * neigh + 4 * owners - 1) // (4 * owners))
    slots = round_up(capacity, 16)
    grows = round_up(variables, 16)
    assert variables % 16 in range(1, 8)
    nx, nz, nc = grid_shape(owners)
    nu = nx * nc
    share = latent // (owners * members)
    keep, pieces, plans = packing(variables, slots, capacity, nu)
    packed = np.concatenate([a[:, b : b + LANES] for a in plans for b in range(0, a.shape[1], LANES)], axis=0)
    normalizer = 1.0 / math.sqrt(float(points * owners * members))
    f32, bf16, i32 = jnp.float32, jnp.bfloat16, jnp.int32
    hbm = pl.BlockSpec(memory_space=pltpu.HBM)
    vmem = pl.BlockSpec(memory_space=pltpu.VMEM)
    dma = pltpu.SemaphoreType.DMA
    wt = weight.T
    gw, mesh_sum = pl.pallas_call(
        functools.partial(fused_kernel, (variables, slots, share, normalizer, pieces)),
        in_specs=[hbm] * 9,
        out_specs=[vmem] * 2,
        out_shape=[
            jax.ShapeDtypeStruct((members * share, LANES), f32),
            jax.ShapeDtypeStruct((mesh_rows, LANES), bf16),
        ],
        scratch_shapes=[
            pltpu.VMEM((points, latent), bf16),
            pltpu.VMEM((variables, latent), bf16),
            pltpu.VMEM((variables, slab), f32),
            pltpu.VMEM((points // LANES, LANES), f32),
            pltpu.VMEM((1, variables), f32),
            pltpu.VMEM((neigh, points), i32),
            pltpu.VMEM((neigh, points), i32),
            pltpu.VMEM((neigh, points), f32),
            *[pltpu.VMEM(a.shape, bf16) for a in plans],
            pltpu.VMEM((LANES, latent), bf16),
            pltpu.VMEM((latent, LANES), bf16),
            pltpu.VMEM((members, grows, slab), jnp.int16),
            pltpu.VMEM((members, grows, slab), jnp.int16),
            pltpu.VMEM((members, 16, slab), f32),
            pltpu.VMEM((members, grows, slab), bf16),
            pltpu.VMEM((members, grows, slab), bf16),
            pltpu.VMEM((owners, points), f32),
            pltpu.VMEM((points, 2 * LANES), bf16),
            pltpu.VMEM((owners * slots, points), bf16),
            pltpu.VMEM((min(2, nz) * nu * slots, LANES), bf16),
            pltpu.VMEM((owners * slots, LANES), f32),
            pltpu.VMEM((points, LANES), bf16),
            pltpu.VMEM((nz, nu, keep, LANES), bf16),
            pltpu.VMEM((nz, nu, keep, LANES), bf16),
            pltpu.VMEM((nz, mesh_rows, LANES), bf16),
            pltpu.VMEM((nz, mesh_rows, LANES), bf16),
            pltpu.VMEM((nx * nz, nc, members * share, LANES), f32),
            pltpu.VMEM((nx * nz, members * share, LANES), f32),
            pltpu.VMEM((members, nx * nz, share, LANES), f32),
            pltpu.VMEM((members, nx * nz, share, LANES), f32),
            pltpu.VMEM((LANES, LANES), f32),
            pltpu.VMEM((nx, nz, share, LANES), f32),
            pltpu.VMEM((nx, nz, share, LANES), f32),
            pltpu.VMEM((nz, share, LANES), f32),
            pltpu.VMEM((nz, share, LANES), f32),
            pltpu.VMEM((share, LANES), f32),
            pltpu.VMEM((members, share, LANES), f32),
            dma((7 + sum(a.shape[1] // LANES for a in plans) + points // (2 * slab),)),
            dma(()), dma(()), dma(()), dma(()), dma(()), dma((nz,)), dma(()), dma(()),
            dma(()), dma(()), dma(()), dma(()), dma(()), dma(()), dma(()), dma(()), dma(()), dma(()),
        ],
        compiler_params=pltpu.CompilerParams(
            collective_id=0, has_side_effects=True, vmem_limit_bytes=VMEM_LIMIT
        ),
    )(
        rows, wt, target, area_weight.reshape(points // LANES, LANES), var_weight.reshape(1, variables),
        edge_owner.T, edge_row.T, edge_weight.T, jnp.asarray(packed),
    )
    grad_weight, mesh_grad = pl.pallas_call(
        finish_kernel,
        in_specs=[vmem] * 3,
        out_specs=[vmem] * 2,
        out_shape=[
            jax.ShapeDtypeStruct((members * share, variables), f32),
            jax.ShapeDtypeStruct((mesh_rows, latent), bf16),
        ],
        compiler_params=pltpu.CompilerParams(vmem_limit_bytes=VMEM_LIMIT),
    )(gw, mesh_sum, wt)
    return grad_weight, mesh_grad[None]


def solution(mesh):
    return jax.shard_map(
        per_device,
        mesh=mesh,
        in_specs=(
            P("ens", "grid", None),
            P(),
            P(None, "grid"),
            P("grid"),
            P(),
            P("grid", None),
            P("grid", None),
            P("grid", None),
        ),
        out_specs=(P("grid", None), P("ens", "grid", None)),
        check_vma=False,
    )
```

```python
import functools
import math

import jax
import jax.numpy as jnp
from jax import lax
from jax.experimental import pallas as pl
from jax.experimental.pallas import tpu as pltpu
from jax.sharding import PartitionSpec as P

smooth_width = 0.1
LANES = 128
STEPS = 32000.0
VMEM_LIMIT = 62 * 1024 * 1024


def softened_sign(difference):
    return difference * lax.rsqrt(difference * difference + smooth_width * smooth_width)


def round_up(n, m):
    return (n + m - 1) // m * m


def score_block(x, t, scale):
    n = len(x)
    total = [None] * n
    for i in range(n):
        for j in range(i + 1, n):
            a = softened_sign(x[i] - x[j])
            total[i] = a if total[i] is None else total[i] + a
            total[j] = -a if total[j] is None else total[j] - a
    out = []
    for i in range(n):
        raw = softened_sign(x[i] - t) * (1.0 / n) - total[i] * (1.0 / (n * (n - 1)))
        out.append((scale * raw).astype(jnp.bfloat16))
    return out


def grid_shape(owners):
    return (owners // 16, 8, 2) if owners >= 16 else (owners // 4, 2, 2)


def place_slots(own_ref, row_ref, ew_ref, slot_s, x_s):
    owners, points = slot_s.shape
    neigh = own_ref.shape[0]
    tri = (
        lax.broadcasted_iota(jnp.int32, (LANES, LANES), 0)
        <= lax.broadcasted_iota(jnp.int32, (LANES, LANES), 1)
    ).astype(jnp.float32).astype(jnp.bfloat16)
    nx, nz, nc = grid_shape(owners)
    at = lax.broadcasted_iota(jnp.int32, (owners, LANES), 0)
    z_id = lax.shift_right_logical(at, int(math.log2(nx * nc)))
    x_id = jnp.bitwise_and(lax.shift_right_logical(at, int(math.log2(nc))), nx - 1)
    owner_id = (x_id * nz + z_id) * nc + jnp.bitwise_and(at, nc - 1)
    line = lax.broadcasted_iota(jnp.int32, (16, LANES), 0)
    blank = jnp.zeros((LANES - 16, LANES), jnp.float32)

    def block(i, carry):
        span = pl.ds(pl.multiple_of(i * LANES, LANES), LANES)
        hit = jnp.zeros((owners, LANES), jnp.float32)
        vals = jnp.zeros((16, LANES), jnp.float32)
        owns = jnp.zeros((16, LANES), jnp.float32)
        for k in range(neigh):
            own = own_ref[k : k + 1, span]
            hit = jnp.where(own == owner_id, 1.0, hit)
            rest = ew_ref[k : k + 1, span]
            for j in range(3):
                piece = rest.astype(jnp.bfloat16).astype(jnp.float32)
                vals = jnp.where(line == 4 * k + j, piece, vals)
                rest = rest - piece
            vals = jnp.where(line == 4 * k + 3, row_ref[k : k + 1, span].astype(jnp.float32), vals)
            owns = jnp.where((line >= 4 * k) & (line < 4 * k + 4), own.astype(jnp.float32), owns)
        count = carry + jnp.dot(hit.astype(jnp.bfloat16), tri, preferred_element_type=jnp.float32)
        slot_s[:, span] = jnp.where(hit > 0.0, count, 0.0)
        x_s[span, 0:LANES] = jnp.concatenate([vals, blank], axis=0).T.astype(jnp.bfloat16)
        x_s[span, LANES:] = jnp.concatenate([owns, blank], axis=0).T.astype(jnp.bfloat16)
        return jnp.broadcast_to(count[:, LANES - 1 : LANES], (owners, LANES))

    lax.fori_loop(0, points // LANES, block, jnp.zeros((owners, LANES), jnp.float32))


def bulk_wait(ref, sem):
    pltpu.make_async_copy(ref, ref, sem).wait()


def fused_kernel(
    cfg,
    hidden_hbm, wt_hbm, target_hbm, area_hbm, var_hbm, own_hbm, row_hbm, ew_hbm,
    gw_out, mesh_out,
    hid, wt_raw, target, area, var, own, row, ew,
    wt, w_col, x_send, x_recv, unit_s, t_s, g_send, g_recv,
    slot_s, x_s, a_s, sel_s, wb_s, gt_s, out_buf, in_buf,
    d_send, d_recv, gw_s, half_recv, y_send, y_recv, q_s, gq_s, q_recv, p_send, p_recv, r_send, r_recv,
    in_sem, x_ss, x_rs, g_ss, g_rs, m_ss, m_rs, d_ss, d_rs, h_ss, h_rs, y_ss, y_rs, q_ss, q_rs, p_ss, p_rs, r_ss, r_rs,
):
    variables, slots, share, normalizer = cfg
    members, grows, slab = g_send.shape
    owners, points = slot_s.shape
    latent = hid.shape[1]
    mesh_rows = d_send.shape[1]
    e, g = lax.axis_index("ens"), lax.axis_index("grid")
    nx, nz, nc = grid_shape(owners)
    nu = nx * nc
    z, core = lax.rem(g // nc, nz), lax.rem(g, nc)
    x_at = g // (nz * nc)
    u = x_at * nc + core

    def plane_peer(i):
        return ((i // nc) * nz + z) * nc + lax.rem(i, nc)

    def column_peer(i):
        return ((u // nc) * nz + i) * nc + lax.rem(u, nc)

    def remote(src, dst, ss, rs, to):
        pltpu.make_async_remote_copy(
            src_ref=src, dst_ref=dst, send_sem=ss, recv_sem=rs, device_id=to, device_id_type=pl.DeviceIdType.MESH
        ).start()

    def send(src, dst, ss, rs, to, here):
        @pl.when(jnp.logical_not(here))
        def _():
            remote(src, dst, ss, rs, to)

        @pl.when(here)
        def _():
            pltpu.make_async_copy(src, dst, rs).start()

    def around(n, me, put):
        def step(o, _):
            put(lax.rem(me + o, n), False)
            return 0

        lax.fori_loop(1, n, step, 0)
        put(me, True)

    def send_to_members(src, dst, ss, rs):
        def put(m, own):
            if own:
                pltpu.make_async_copy(src(m), dst, rs).start()
            else:
                remote(src(m), dst, ss, rs, (m, g))

        around(members, e, put)

    barrier = pltpu.get_barrier_semaphore()

    def greet_ens(i, _):
        pl.semaphore_signal(barrier, inc=1, device_id=(lax.rem(e + i, members), g), device_id_type=pl.DeviceIdType.MESH)
        return 0

    def greet_plane(i, _):
        pl.semaphore_signal(barrier, inc=1, device_id=(e, plane_peer(lax.rem(u + i, nu))), device_id_type=pl.DeviceIdType.MESH)
        return 0

    def greet_column(i, _):
        pl.semaphore_signal(barrier, inc=1, device_id=(e, column_peer(lax.rem(z + i, nz))), device_id_type=pl.DeviceIdType.MESH)
        return 0

    chunk = 2 * slab
    loads = [pltpu.make_async_copy(wt_hbm, wt_raw, in_sem.at[0])]
    chunks = points // chunk
    order = [lax.rem(e // 2 + chunks // 2 + o, chunks) for o in range(chunks)]
    for c in order:
        rows = pl.ds(pl.multiple_of(c * chunk, chunk), chunk)
        loads.append(pltpu.make_async_copy(hidden_hbm.at[rows], hid.at[rows], in_sem.at[1 + c]))
    n_hid = len(loads)
    loads.append(
        pltpu.make_async_copy(
            target_hbm.at[:, pl.ds(pl.multiple_of(e * slab, slab), slab)], target, in_sem.at[n_hid]
        )
    )
    for i, (s, d) in enumerate(((area_hbm, area), (var_hbm, var), (own_hbm, own), (row_hbm, row), (ew_hbm, ew))):
        loads.append(pltpu.make_async_copy(s, d, in_sem.at[n_hid + 1 + i]))
    for cp in loads:
        cp.start()
    lax.fori_loop(1, members, greet_ens, 0)
    lax.fori_loop(1, nu, greet_plane, 0)
    lax.fori_loop(1, nz, greet_column, 0)

    loads[0].wait()
    whole = variables // 16 * 16
    wt[0:whole, :] = wt_raw[0:whole, :]
    wt[whole : whole + 16, :] = jnp.concatenate(
        [wt_raw[whole:variables, :], jnp.zeros((whole + 16 - variables, latent), jnp.bfloat16)], axis=0
    )
    wt[whole + 16 :, :] = jnp.zeros((LANES - whole - 16, latent), jnp.bfloat16)

    def turn(i, _):
        span = pl.ds(pl.multiple_of(i * LANES, LANES), LANES)
        w_col[span, :] = wt[:, span].astype(jnp.float32).T.astype(jnp.bfloat16)
        return 0

    lax.fori_loop(0, latent // LANES, turn, 0)

    tail_row = lax.broadcasted_iota(jnp.int32, (8, slab), 0)
    zero_rows = jnp.zeros((8, slab), jnp.int32)

    def forecast(t, _):
        c = lax.rem(e // 2 + chunks // 2 + t, chunks)
        rows = pl.ds(pl.multiple_of(c * chunk, chunk), chunk)
        pltpu.make_async_copy(hidden_hbm.at[rows], hid.at[rows], in_sem.at[1 + c]).wait()
        part = jnp.dot(hid[rows, :], w_col[...], preferred_element_type=jnp.float32)
        for s in range(2):
            m = 2 * c + s
            block = part[s * slab : (s + 1) * slab, :].T[: whole + 8, :]
            top = jnp.max(jnp.abs(block), axis=0, keepdims=True)
            power = jnp.ceil(jnp.log2(jnp.maximum(top, 1e-30)))
            code = jnp.floor(block * (jnp.exp2(-power) * STEPS) + 0.5).astype(jnp.int32)
            tail = jnp.where(tail_row == variables - whole, power.astype(jnp.int32), code[whole:, :])
            x_send[m, 0:whole, :] = code[0:whole, :].astype(jnp.int16)
            x_send[m, whole : whole + 16, :] = jnp.concatenate([tail, zero_rows], axis=0).astype(jnp.int16)
        for s in range(2):
            m = 2 * c + s
            send(x_send.at[m], x_recv.at[e], x_ss, x_rs, (m, g), m == e)
        return 0

    pl.semaphore_wait(barrier, members + nu + nz - 3)
    lax.fori_loop(0, chunks, forecast, 0)

    for cp in loads[n_hid:]:
        cp.wait()
    place_slots(own, row, ew, slot_s, x_s)
    step = nu * slots
    both = min(2, nz)
    groups = nz // both
    want = lax.broadcasted_iota(jnp.int32, (slots, LANES), 0).astype(jnp.float32) + 1.0
    line = lax.broadcasted_iota(jnp.int32, (LANES, LANES), 0)
    lane = lax.broadcasted_iota(jnp.int32, (LANES, LANES), 1)
    spread = jnp.where((lax.rem(line, 4) == 3) == (lane == variables), 1.0, 0.0).astype(jnp.bfloat16)

    def one_hot(t, _):
        at = lax.rem((z // both + 1) * both + t, nz)
        base = pl.multiple_of(at * nu, nu)
        first = pl.multiple_of(at * step, step)

        def fill(j, _):
            slot = slot_s[pl.ds(base + j, 1), :]
            rows = pl.ds(pl.multiple_of(first + j * slots, slots), slots)
            for b in range(0, points, LANES):
                same = slot[:, b : b + LANES] == want
                a_s[rows, b : b + LANES] = jnp.where(same, 1.0, 0.0).astype(jnp.bfloat16)
            return 0

        lax.fori_loop(0, nu, fill, 0)
        rows = pl.ds(first, step)
        ext = jnp.dot(a_s[rows, :], x_s[...], preferred_element_type=jnp.float32)
        for j in range(nu):
            owner = ((j // nc) * nz + at) * nc + j % nc
            part = ext[j * slots : (j + 1) * slots, :]
            mine = part[:, LANES:] == owner.astype(jnp.float32)
            sel_s[j * slots : (j + 1) * slots, :] = jnp.where(mine, part[:, 0:LANES], 0.0).astype(jnp.bfloat16)
        wb_s[rows, :] = jnp.dot(sel_s[...], spread, preferred_element_type=jnp.float32)
        return 0

    lax.fori_loop(0, nz // 2, one_hot, 0)
    vcol = jnp.broadcast_to(
        jnp.concatenate([var[...], jnp.zeros((1, LANES - variables), jnp.float32)], axis=1), (LANES, LANES)
    ).T
    scale = vcol * area[pl.ds(e, 1), :]
    q_s[0:LANES, :] = scale

    bulk_wait(x_recv, x_rs)

    def wide_block(m, at):
        return x_recv[m, at, :].astype(jnp.int32).astype(jnp.float32)

    def unit(m, _):
        power = wide_block(m, pl.ds(whole, 16))[variables - whole : variables - whole + 1, :]
        unit_s[m] = jnp.broadcast_to(jnp.exp2(power) * (1.0 / STEPS), (16, slab))
        return 0

    lax.fori_loop(0, members, unit, 0)
    t_s[0:whole, :] = target[0:whole, :]
    t_s[whole:, :] = jnp.concatenate(
        [target[whole:variables, :], jnp.zeros((whole + 16 - variables, slab), jnp.float32)], axis=0
    )

    def score(i, _):
        at = pl.ds(pl.multiple_of(i * 16, 16), 16)
        got = score_block([wide_block(m, at) * unit_s[m] for m in range(members)], t_s[at, :], q_s[at, :])
        for m in range(members):
            g_send[m, at, :] = got[m]
        return 0

    lax.fori_loop(0, grows // 16, score, 0)
    send_to_members(lambda m: g_send.at[m], g_recv.at[e], g_ss, g_rs)
    lax.fori_loop(nz // 2, nz, one_hot, 0)

    bulk_wait(g_recv, g_rs)
    pad = jnp.zeros((LANES - grows, LANES), jnp.float32)

    def turn_back(m, _):
        block = jnp.concatenate([g_recv[m].astype(jnp.float32), pad], axis=0).T
        span = pl.ds(pl.multiple_of(m * LANES, LANES), LANES)
        gt_s[span, :] = jnp.where(lane == variables, 1.0, block).astype(jnp.bfloat16)
        return 0

    lax.fori_loop(0, members, turn_back, 0)

    wide = jnp.concatenate([g_recv[s] for s in range(members)], axis=1)
    pairs = LANES // (nc * members * share)

    def project(b, _):
        part = jnp.dot(
            wide, hid[:, pl.ds(pl.multiple_of(b * 2 * LANES, 2 * LANES), 2 * LANES)], preferred_element_type=jnp.float32
        )
        for c in range(2):
            block = jnp.concatenate([part[:, c * LANES : (c + 1) * LANES], pad], axis=0).T
            gw_s[pl.ds((2 * b + c) * pairs, pairs)] = block.reshape(pairs, nc, members * share, LANES)
        return 0

    half = pltpu.make_async_remote_copy(
        src_ref=gw_s.at[:, 1 - core], dst_ref=half_recv, send_sem=h_ss, recv_sem=h_rs,
        device_id=(e, g + 1 - 2 * core), device_id_type=pl.DeviceIdType.MESH,
    )

    def sum_cores():
        half.wait_recv()
        total = gw_s[:, core] + half_recv[...]
        for m in range(members):
            y_send[m] = total[:, m * share : (m + 1) * share, :]
        send_to_members(lambda m: y_send.at[m], y_recv.at[e], y_ss, y_rs)

    def messages(t, _):
        at = lax.rem(z // both + 1 + t, groups)

        def scaled(i, _):
            rows = pl.ds(pl.multiple_of((at * both + i) * step, step), step)
            picked = jnp.dot(a_s[rows, :], gt_s[...], preferred_element_type=jnp.float32)
            out_buf[at * both + i] = (picked * wb_s[rows, :]).astype(jnp.bfloat16).reshape(nu, slots, LANES)
            return 0

        lax.fori_loop(0, both, scaled, 0)
        zs = pl.ds(at * both, both)

        def put(j, own):
            if own:
                pltpu.make_async_copy(out_buf.at[zs, j], in_buf.at[zs, u], m_rs.at[at]).start()
            else:
                remote(out_buf.at[zs, j], in_buf.at[zs, u], m_ss, m_rs.at[at], (e, plane_peer(j)))

        around(nu, u, put)

        @pl.when(t == 0)
        def _():
            lax.fori_loop(0, latent // (2 * LANES), project, 0)
            half.start()

        @pl.when(t == min(1, groups - 1))
        def _():
            sum_cores()

        return 0

    lax.fori_loop(0, groups, messages, 0)

    pick = (lax.broadcasted_iota(jnp.int32, (16, LANES), 1) == variables).astype(jnp.float32).astype(jnp.bfloat16)
    ids = lax.broadcasted_iota(jnp.int32, (mesh_rows, step), 0).astype(jnp.float32)

    def sum_members():
        bulk_wait(y_recv, y_rs)
        total = y_recv[0]
        for m in range(1, members):
            total = total + y_recv[m]
        gq_s[...] = total.reshape(nx, nz, share, LANES)

        def put(j, own):
            if own:
                pltpu.make_async_copy(gq_s.at[j], q_recv.at[x_at], q_rs).start()
            else:
                remote(gq_s.at[j], q_recv.at[x_at], q_ss, q_rs, (e, plane_peer(j * nc + core)))

        around(nx, x_at, put)

    def sum_plane():
        bulk_wait(q_recv, q_rs)
        total = q_recv[0]
        for j in range(1, nx):
            total = total + q_recv[j]
        p_send[...] = total

        def put(j, own):
            if own:
                pltpu.make_async_copy(p_send.at[j], p_recv.at[z], p_rs).start()
            else:
                remote(p_send.at[j], p_recv.at[z], p_ss, p_rs, (e, column_peer(j)))

        around(nz, z, put)

    def mesh_part(t, _):
        at = lax.rem(z // both + 1 + t, groups)
        zs = pl.ds(at * both, both)
        bulk_wait(in_buf.at[zs], m_rs.at[at])

        def one(i, _):
            zi = at * both + i
            block = in_buf[zi].reshape(step, LANES)
            place = lax.dot_general(pick, block, (((1,), (1,)), ((), ())), preferred_element_type=jnp.float32)
            picker = jnp.where(place[0:1, :] == ids, 1.0, 0.0).astype(jnp.bfloat16)
            d_send[zi] = jnp.dot(picker, block, preferred_element_type=jnp.float32).astype(jnp.bfloat16)
            send(d_send.at[zi], d_recv.at[z], d_ss, d_rs, (e, column_peer(zi)), zi == z)
            return 0

        lax.fori_loop(0, both, one, 0)

        @pl.when(t == max(groups - 3, 0))
        def _():
            sum_members()

        @pl.when(t == max(groups - 2, 0))
        def _():
            sum_plane()

        return 0

    lax.fori_loop(0, groups, mesh_part, 0)

    bulk_wait(p_recv, p_rs)
    r_send[...] = jnp.sum(p_recv[...], axis=0) * normalizer
    send_to_members(lambda m: r_send, r_recv.at[e], r_ss, r_rs)
    bulk_wait(d_recv, d_rs)
    acc = d_recv[0].astype(jnp.float32)
    for j in range(1, nz):
        acc = acc + d_recv[j].astype(jnp.float32)
    mesh_out[...] = acc.astype(jnp.bfloat16)
    bulk_wait(r_recv, r_rs)
    for m in range(members):
        gw_out[share * m : share * (m + 1), :] = r_recv[m]

    bulk_wait(x_send.at[pl.ds(0, members - 1)], x_ss)
    bulk_wait(g_send.at[pl.ds(0, members - 1)], g_ss)
    bulk_wait(out_buf.at[:, pl.ds(0, nu - 1)], m_ss)
    bulk_wait(d_send.at[pl.ds(0, nz - 1)], d_ss)
    half.wait_send()
    bulk_wait(y_send.at[pl.ds(0, members - 1)], y_ss)
    bulk_wait(q_recv.at[pl.ds(0, nx - 1)], q_ss)
    bulk_wait(p_send.at[pl.ds(0, nz - 1)], p_ss)
    bulk_wait(r_recv.at[pl.ds(0, members - 1)], r_ss)


def finish_kernel(gw_ref, mesh_ref, wt_ref, gw_out, mesh_out):
    variables, latent = wt_ref.shape
    gw_out[...] = gw_ref[:, 0:variables]
    whole = variables // 16 * 16
    wide = jnp.concatenate(
        [wt_ref[whole:variables, :], jnp.zeros((whole + 16 - variables, latent), jnp.bfloat16)], axis=0
    )
    total = jnp.dot(mesh_ref[:, 0:whole], wt_ref[0:whole, :], preferred_element_type=jnp.float32)
    total = total + jnp.dot(mesh_ref[:, whole : whole + 16], wide, preferred_element_type=jnp.float32)
    mesh_out[...] = total.astype(jnp.bfloat16)


def per_device(hidden, weight, target, area_weight, var_weight, edge_owner, edge_row, edge_weight):
    rows = hidden[0]
    points, latent = rows.shape
    variables = weight.shape[1]
    neigh = edge_owner.shape[1]
    members = lax.axis_size("ens")
    owners = lax.axis_size("grid")
    mesh_rows = points // 8
    slab = points // members
    assert slab == LANES and variables < LANES
    capacity = max(2, (5 * points * neigh + 4 * owners - 1) // (4 * owners))
    slots = round_up(capacity, 16)
    grows = round_up(variables, 16)
    assert variables % 16 in range(1, 8)
    nx, nz, nc = grid_shape(owners)
    nu = nx * nc
    share = latent // (owners * members)
    normalizer = 1.0 / math.sqrt(float(points * owners * members))
    f32, bf16, i32 = jnp.float32, jnp.bfloat16, jnp.int32
    hbm = pl.BlockSpec(memory_space=pltpu.HBM)
    vmem = pl.BlockSpec(memory_space=pltpu.VMEM)
    dma = pltpu.SemaphoreType.DMA
    wt = weight.T
    gw, mesh_sum = pl.pallas_call(
        functools.partial(fused_kernel, (variables, slots, share, normalizer)),
        in_specs=[hbm] * 8,
        out_specs=[vmem] * 2,
        out_shape=[
            jax.ShapeDtypeStruct((members * share, LANES), f32),
            jax.ShapeDtypeStruct((mesh_rows, LANES), bf16),
        ],
        scratch_shapes=[
            pltpu.VMEM((points, latent), bf16),
            pltpu.VMEM((variables, latent), bf16),
            pltpu.VMEM((variables, slab), f32),
            pltpu.VMEM((points // LANES, LANES), f32),
            pltpu.VMEM((1, variables), f32),
            pltpu.VMEM((neigh, points), i32),
            pltpu.VMEM((neigh, points), i32),
            pltpu.VMEM((neigh, points), f32),
            pltpu.VMEM((LANES, latent), bf16),
            pltpu.VMEM((latent, LANES), bf16),
            pltpu.VMEM((members, grows, slab), jnp.int16),
            pltpu.VMEM((members, grows, slab), jnp.int16),
            pltpu.VMEM((members, 16, slab), f32),
            pltpu.VMEM((grows, slab), f32),
            pltpu.VMEM((members, grows, slab), bf16),
            pltpu.VMEM((members, grows, slab), bf16),
            pltpu.VMEM((owners, points), f32),
            pltpu.VMEM((points, 2 * LANES), bf16),
            pltpu.VMEM((owners * slots, points), bf16),
            pltpu.VMEM((nu * slots, LANES), bf16),
            pltpu.VMEM((owners * slots, LANES), f32),
            pltpu.VMEM((points, LANES), bf16),
            pltpu.VMEM((nz, nu, slots, LANES), bf16),
            pltpu.VMEM((nz, nu, slots, LANES), bf16),
            pltpu.VMEM((nz, mesh_rows, LANES), bf16),
            pltpu.VMEM((nz, mesh_rows, LANES), bf16),
            pltpu.VMEM((nx * nz, nc, members * share, LANES), f32),
            pltpu.VMEM((nx * nz, members * share, LANES), f32),
            pltpu.VMEM((members, nx * nz, share, LANES), f32),
            pltpu.VMEM((members, nx * nz, share, LANES), f32),
            pltpu.VMEM((LANES, LANES), f32),
            pltpu.VMEM((nx, nz, share, LANES), f32),
            pltpu.VMEM((nx, nz, share, LANES), f32),
            pltpu.VMEM((nz, share, LANES), f32),
            pltpu.VMEM((nz, share, LANES), f32),
            pltpu.VMEM((share, LANES), f32),
            pltpu.VMEM((members, share, LANES), f32),
            dma((7 + points // (2 * slab),)),
            dma(()), dma(()), dma(()), dma(()), dma(()), dma((nz,)), dma(()), dma(()),
            dma(()), dma(()), dma(()), dma(()), dma(()), dma(()), dma(()), dma(()), dma(()), dma(()),
        ],
        compiler_params=pltpu.CompilerParams(
            collective_id=0, has_side_effects=True, vmem_limit_bytes=VMEM_LIMIT
        ),
    )(
        rows, wt, target, area_weight.reshape(points // LANES, LANES), var_weight.reshape(1, variables),
        edge_owner.T, edge_row.T, edge_weight.T,
    )
    grad_weight, mesh_grad = pl.pallas_call(
        finish_kernel,
        in_specs=[vmem] * 3,
        out_specs=[vmem] * 2,
        out_shape=[
            jax.ShapeDtypeStruct((members * share, variables), f32),
            jax.ShapeDtypeStruct((mesh_rows, latent), bf16),
        ],
        compiler_params=pltpu.CompilerParams(vmem_limit_bytes=VMEM_LIMIT),
    )(gw, mesh_sum, wt)
    return grad_weight, mesh_grad[None]


def solution(mesh):
    return jax.shard_map(
        per_device,
        mesh=mesh,
        in_specs=(
            P("ens", "grid", None),
            P(),
            P(None, "grid"),
            P("grid"),
            P(),
            P("grid", None),
            P("grid", None),
            P("grid", None),
        ),
        out_specs=(P("grid", None), P("ens", "grid", None)),
        check_vma=False,
    )
```

```python
import functools
import math

import jax
import jax.numpy as jnp
from jax import lax
from jax.experimental import pallas as pl
from jax.experimental.pallas import tpu as pltpu
from jax.sharding import PartitionSpec as P

smooth_width = 0.1
LANES = 128
STEPS = 32000.0
VMEM_LIMIT = 62 * 1024 * 1024


def softened_sign(difference):
    return difference * lax.rsqrt(difference * difference + smooth_width * smooth_width)


def round_up(n, m):
    return (n + m - 1) // m * m


def score_block(x, t, scale):
    n = len(x)
    total = [None] * n
    for i in range(n):
        for j in range(i + 1, n):
            a = softened_sign(x[i] - x[j])
            total[i] = a if total[i] is None else total[i] + a
            total[j] = -a if total[j] is None else total[j] - a
    out = []
    for i in range(n):
        raw = softened_sign(x[i] - t) * (1.0 / n) - total[i] * (1.0 / (n * (n - 1)))
        out.append((scale * raw).astype(jnp.bfloat16))
    return out


def grid_shape(owners):
    return (owners // 16, 8, 2) if owners >= 16 else (owners // 4, 2, 2)


def place_slots(own_ref, row_ref, ew_ref, slot_s, x_s):
    owners, points = slot_s.shape
    neigh = own_ref.shape[0]
    tri = (
        lax.broadcasted_iota(jnp.int32, (LANES, LANES), 0)
        <= lax.broadcasted_iota(jnp.int32, (LANES, LANES), 1)
    ).astype(jnp.float32).astype(jnp.bfloat16)
    nx, nz, nc = grid_shape(owners)
    at = lax.broadcasted_iota(jnp.int32, (owners, LANES), 0)
    z_id = lax.shift_right_logical(at, int(math.log2(nx * nc)))
    x_id = jnp.bitwise_and(lax.shift_right_logical(at, int(math.log2(nc))), nx - 1)
    owner_id = (x_id * nz + z_id) * nc + jnp.bitwise_and(at, nc - 1)
    line = lax.broadcasted_iota(jnp.int32, (16, LANES), 0)
    blank = jnp.zeros((LANES - 16, LANES), jnp.float32)
    carry = jnp.zeros((owners, 1), jnp.float32)
    for b in range(0, points, LANES):
        hit = jnp.zeros((owners, LANES), jnp.float32)
        vals = jnp.zeros((16, LANES), jnp.float32)
        owns = jnp.zeros((16, LANES), jnp.float32)
        for k in range(neigh):
            own = own_ref[k : k + 1, b : b + LANES]
            hit = jnp.where(own == owner_id, 1.0, hit)
            rest = ew_ref[k : k + 1, b : b + LANES]
            for i in range(3):
                piece = rest.astype(jnp.bfloat16).astype(jnp.float32)
                vals = jnp.where(line == 4 * k + i, piece, vals)
                rest = rest - piece
            vals = jnp.where(line == 4 * k + 3, row_ref[k : k + 1, b : b + LANES].astype(jnp.float32), vals)
            owns = jnp.where((line >= 4 * k) & (line < 4 * k + 4), own.astype(jnp.float32), owns)
        count = carry + jnp.dot(hit.astype(jnp.bfloat16), tri, preferred_element_type=jnp.float32)
        slot_s[:, b : b + LANES] = jnp.where(hit > 0.0, count, 0.0)
        carry = count[:, LANES - 1 : LANES]
        x_s[b : b + LANES, 0:LANES] = jnp.concatenate([vals, blank], axis=0).T.astype(jnp.bfloat16)
        x_s[b : b + LANES, LANES:] = jnp.concatenate([owns, blank], axis=0).T.astype(jnp.bfloat16)


def far_first(n):
    return sorted(range(n), key=lambda o: -min(o, n - o))


def bulk_wait(ref, sem):
    pltpu.make_async_copy(ref, ref, sem).wait()


def fused_kernel(
    cfg,
    hidden_hbm, wt_hbm, target_hbm, area_hbm, var_hbm, own_hbm, row_hbm, ew_hbm,
    gw_out, mesh_out,
    hid, wt_raw, target, area, var, own, row, ew,
    wt, w_col, x_send, x_recv, unit_s, g_send, g_recv,
    slot_s, x_s, a_s, sel_s, wb_s, gt_s, out_buf, in_buf,
    d_send, d_recv, gw_s, half_recv, y_send, y_recv, q_s, gq_s, q_recv, p_send, p_recv, r_send, r_recv,
    in_sem, x_ss, x_rs, g_ss, g_rs, m_ss, m_rs, d_ss, d_rs, h_ss, h_rs, y_ss, y_rs, q_ss, q_rs, p_ss, p_rs, r_ss, r_rs,
):
    variables, slots, share, normalizer = cfg
    members, grows, slab = g_send.shape
    owners, points = slot_s.shape
    latent = hid.shape[1]
    mesh_rows = d_send.shape[1]
    e, g = lax.axis_index("ens"), lax.axis_index("grid")
    nx, nz, nc = grid_shape(owners)
    nu = nx * nc
    z, core = lax.rem(g // nc, nz), lax.rem(g, nc)
    x_at = g // (nz * nc)
    u = x_at * nc + core

    def plane_peer(i):
        return ((i // nc) * nz + z) * nc + lax.rem(i, nc)

    def column_peer(i):
        return ((u // nc) * nz + i) * nc + lax.rem(u, nc)

    def send_known(src, dst, ss, rs, to, own):
        if own:
            pltpu.make_async_copy(src, dst, rs).start()
        else:
            pltpu.make_async_remote_copy(
                src_ref=src, dst_ref=dst, send_sem=ss, recv_sem=rs, device_id=to, device_id_type=pl.DeviceIdType.MESH
            ).start()

    def send(src, dst, ss, rs, axis, peer, me):
        @pl.when(peer != me)
        def _():
            pltpu.make_async_remote_copy(
                src_ref=src, dst_ref=dst, send_sem=ss, recv_sem=rs,
                device_id={axis: peer}, device_id_type=pl.DeviceIdType.MESH,
            ).start()

        @pl.when(peer == me)
        def _():
            pltpu.make_async_copy(src, dst, rs).start()

    barrier = pltpu.get_barrier_semaphore()

    def greet_ens(i, _):
        pl.semaphore_signal(barrier, inc=1, device_id={"ens": lax.rem(e + i, members)}, device_id_type=pl.DeviceIdType.MESH)
        return 0

    def greet_plane(i, _):
        pl.semaphore_signal(barrier, inc=1, device_id={"grid": plane_peer(lax.rem(u + i, nu))}, device_id_type=pl.DeviceIdType.MESH)
        return 0

    def greet_column(i, _):
        pl.semaphore_signal(barrier, inc=1, device_id={"grid": column_peer(lax.rem(z + i, nz))}, device_id_type=pl.DeviceIdType.MESH)
        return 0

    chunk = 2 * slab
    loads = [pltpu.make_async_copy(wt_hbm, wt_raw, in_sem.at[0])]
    chunks = points // chunk
    order = [lax.rem(e // 2 + o, chunks) for o in far_first(chunks)]
    for c in order:
        rows = pl.ds(pl.multiple_of(c * chunk, chunk), chunk)
        loads.append(pltpu.make_async_copy(hidden_hbm.at[rows], hid.at[rows], in_sem.at[1 + c]))
    n_hid = len(loads)
    loads.append(
        pltpu.make_async_copy(
            target_hbm.at[:, pl.ds(pl.multiple_of(e * slab, slab), slab)], target, in_sem.at[n_hid]
        )
    )
    for i, (s, d) in enumerate(((area_hbm, area), (var_hbm, var), (own_hbm, own), (row_hbm, row), (ew_hbm, ew))):
        loads.append(pltpu.make_async_copy(s, d, in_sem.at[n_hid + 1 + i]))
    for cp in loads:
        cp.start()
    lax.fori_loop(1, members, greet_ens, 0)
    lax.fori_loop(1, nu, greet_plane, 0)
    lax.fori_loop(1, nz, greet_column, 0)

    loads[0].wait()
    whole = variables // 16 * 16
    wt[0:whole, :] = wt_raw[0:whole, :]
    wt[whole : whole + 16, :] = jnp.concatenate(
        [wt_raw[whole:variables, :], jnp.zeros((whole + 16 - variables, latent), jnp.bfloat16)], axis=0
    )
    wt[whole + 16 :, :] = jnp.zeros((LANES - whole - 16, latent), jnp.bfloat16)
    for b in range(0, latent, LANES):
        w_col[b : b + LANES, :] = wt[:, b : b + LANES].astype(jnp.float32).T.astype(jnp.bfloat16)

    tail_row = lax.broadcasted_iota(jnp.int32, (8, slab), 0)
    zero_rows = jnp.zeros((8, slab), jnp.int32)
    for t, c in enumerate(order):
        loads[1 + t].wait()
        rows = pl.ds(pl.multiple_of(c * chunk, chunk), chunk)
        part = jnp.dot(hid[rows, :], w_col[...], preferred_element_type=jnp.float32)
        for s in range(2):
            m = 2 * c + s
            block = part[s * slab : (s + 1) * slab, :].T[: whole + 8, :]
            top = jnp.max(jnp.abs(block), axis=0, keepdims=True)
            power = jnp.ceil(jnp.log2(jnp.maximum(top, 1e-30)))
            code = jnp.floor(block * (jnp.exp2(-power) * STEPS) + 0.5).astype(jnp.int32)
            tail = jnp.where(tail_row == variables - whole, power.astype(jnp.int32), code[whole:, :])
            x_send[m, 0:whole, :] = code[0:whole, :].astype(jnp.int16)
            x_send[m, whole : whole + 16, :] = jnp.concatenate([tail, zero_rows], axis=0).astype(jnp.int16)
        if t == 0:
            pl.semaphore_wait(barrier, members + nu + nz - 3)
        for s in range(2):
            m = 2 * c + s
            if t < chunks - 1:
                send_known(x_send.at[m], x_recv.at[e], x_ss, x_rs, (m, g), False)
            else:
                send(x_send.at[m], x_recv.at[e], x_ss, x_rs, "ens", m, e)

    for cp in loads[n_hid:]:
        cp.wait()
    place_slots(own, row, ew, slot_s, x_s)
    step = nu * slots
    both = min(2, nz)
    groups = nz // both
    want = lax.broadcasted_iota(jnp.int32, (slots, LANES), 0).astype(jnp.float32) + 1.0
    line = lax.broadcasted_iota(jnp.int32, (LANES, LANES), 0)
    lane = lax.broadcasted_iota(jnp.int32, (LANES, LANES), 1)
    spread = jnp.where((lax.rem(line, 4) == 3) == (lane == variables), 1.0, 0.0).astype(jnp.bfloat16)

    def one_hot(t, _):
        at = lax.rem(z // both + 1 + t, groups)
        base = pl.multiple_of(at * (both * nu), both * nu)
        slot_g = slot_s[pl.ds(base, both * nu), :]
        first = at * (both * step)
        for j in range(both * nu):
            rows = pl.ds(pl.multiple_of(first + j * slots, slots), slots)
            for b in range(0, points, LANES):
                same = slot_g[j : j + 1, b : b + LANES] == want
                a_s[rows, b : b + LANES] = jnp.where(same, 1.0, 0.0).astype(jnp.bfloat16)
        rows = pl.ds(pl.multiple_of(first, both * step), both * step)
        ext = jnp.dot(a_s[rows, :], x_s[...], preferred_element_type=jnp.float32)
        for j in range(both * nu):
            owner = (((j % nu) // nc) * nz + at * both + j // nu) * nc + j % nc
            part = ext[j * slots : (j + 1) * slots, :]
            mine = part[:, LANES:] == owner.astype(jnp.float32)
            sel_s[j * slots : (j + 1) * slots, :] = jnp.where(mine, part[:, 0:LANES], 0.0).astype(jnp.bfloat16)
        wb_s[rows, :] = jnp.dot(sel_s[...], spread, preferred_element_type=jnp.float32)
        return 0

    lax.fori_loop(0, 1, one_hot, 0)
    vcol = jnp.broadcast_to(
        jnp.concatenate([var[...], jnp.zeros((1, LANES - variables), jnp.float32)], axis=1), (LANES, LANES)
    ).T
    scale = vcol * area[pl.ds(e, 1), :]
    q_s[0:LANES, :] = scale

    bulk_wait(x_recv, x_rs)

    def wide_block(m, at):
        return x_recv[m, at, :].astype(jnp.int32).astype(jnp.float32)

    for m in range(members):
        power = wide_block(m, pl.ds(whole, 16))[variables - whole : variables - whole + 1, :]
        unit_s[m] = jnp.broadcast_to(jnp.exp2(power) * (1.0 / STEPS), (16, slab))

    def score(r, t):
        at = pl.ds(r, 16)
        got = score_block([wide_block(m, at) * unit_s[m] for m in range(members)], t, q_s[at, :])
        for m in range(members):
            g_send[m, at, :] = got[m]

    def score_step(i, _):
        r = pl.multiple_of(i * 16, 16)
        score(r, target[pl.ds(r, 16), :])
        return 0

    lax.fori_loop(0, variables // 16, score_step, 0)
    score(
        whole,
        jnp.concatenate(
            [target[whole:variables, :], jnp.zeros((whole + 16 - variables, slab), jnp.float32)], axis=0
        ),
    )
    for o in far_first(members):
        m = lax.rem(e + o, members)
        send_known(g_send.at[m], g_recv.at[e], g_ss, g_rs, (m, g), o == 0)

    early = max(1, groups // 2)
    lax.fori_loop(1, early, one_hot, 0)

    bulk_wait(g_recv, g_rs)
    pad = jnp.zeros((LANES - grows, LANES), jnp.float32)
    for s in range(members):
        block = jnp.concatenate([g_recv[s].astype(jnp.float32), pad], axis=0).T
        gt_s[s * LANES : (s + 1) * LANES, :] = jnp.where(lane == variables, 1.0, block).astype(jnp.bfloat16)
    def messages(t, _):
        at = lax.rem(z // both + 1 + t, groups)
        rows = pl.ds(pl.multiple_of(at * (both * step), both * step), both * step)
        picked = jnp.dot(a_s[rows, :], gt_s[...], preferred_element_type=jnp.float32)
        zs = pl.ds(at * both, both)
        out_buf[zs] = (picked * wb_s[rows, :]).astype(jnp.bfloat16).reshape(both, nu, slots, LANES)
        for o in far_first(nx):
            for c in range(nc):
                x_to, c_to = lax.rem(x_at + o, nx), lax.rem(core + 1 + c, nc)
                send_known(
                    out_buf.at[zs, x_to * nc + c_to], in_buf.at[zs, u], m_ss, m_rs.at[at],
                    (e, (x_to * nz + z) * nc + c_to), o == 0 and c == nc - 1,
                )
        return 0

    lax.fori_loop(0, early, messages, 0)

    wide = jnp.concatenate([g_recv[s] for s in range(members)], axis=1)
    for b in range(0, latent, 2 * LANES):
        part = jnp.dot(wide, hid[:, b : b + 2 * LANES], preferred_element_type=jnp.float32)
        for c in range(0, 2 * LANES, LANES):
            block = jnp.concatenate([part[:, c : c + LANES], pad], axis=0).T
            pairs = LANES // (nc * members * share)
            gw_s[(b + c) // LANES * pairs : ((b + c) // LANES + 1) * pairs] = block.reshape(
                pairs, nc, members * share, LANES
            )
    half = pltpu.make_async_remote_copy(
        src_ref=gw_s.at[:, 1 - core], dst_ref=half_recv, send_sem=h_ss, recv_sem=h_rs,
        device_id={"grid": g + 1 - 2 * core}, device_id_type=pl.DeviceIdType.MESH,
    )
    half.start()

    def late_messages(t, _):
        one_hot(t, 0)
        return messages(t, 0)

    middle = (early + groups) // 2
    lax.fori_loop(early, middle, late_messages, 0)

    half.wait_recv()
    total = gw_s[:, core] + half_recv[...]
    for m in range(members):
        y_send[m] = total[:, m * share : (m + 1) * share, :]
    for o in far_first(members):
        m = lax.rem(e + o, members)
        send_known(y_send.at[m], y_recv.at[e], y_ss, y_rs, (m, g), o == 0)

    lax.fori_loop(middle, groups, late_messages, 0)

    pick = (lax.broadcasted_iota(jnp.int32, (16, LANES), 1) == variables).astype(jnp.float32).astype(jnp.bfloat16)
    ids = lax.broadcasted_iota(jnp.int32, (mesh_rows, step), 0).astype(jnp.float32)

    def mesh_part(t, _):
        at = lax.rem(z // both + 1 + t, groups)
        zs = pl.ds(at * both, both)
        bulk_wait(in_buf.at[zs], m_rs.at[at])
        for i in range(both):
            zi = at * both + i
            block = in_buf[zi].reshape(step, LANES)
            place = lax.dot_general(pick, block, (((1,), (1,)), ((), ())), preferred_element_type=jnp.float32)
            picker = jnp.where(place[0:1, :] == ids, 1.0, 0.0).astype(jnp.bfloat16)
            d_send[zi] = jnp.dot(picker, block, preferred_element_type=jnp.float32).astype(jnp.bfloat16)
            send(d_send.at[zi], d_recv.at[z], d_ss, d_rs, "grid", column_peer(zi), g)
        return 0

    lax.fori_loop(0, groups // 2, mesh_part, 0)

    bulk_wait(y_recv, y_rs)
    total = y_recv[0]
    for m in range(1, members):
        total = total + y_recv[m]
    gq_s[...] = total.reshape(nx, nz, share, LANES)
    for o in far_first(nx):
        j = lax.rem(x_at + o, nx)
        send_known(gq_s.at[j], q_recv.at[x_at], q_ss, q_rs, (e, (j * nz + z) * nc + core), o == 0)

    lax.fori_loop(groups // 2, groups - 1, mesh_part, 0)

    bulk_wait(q_recv, q_rs)
    total = q_recv[0]
    for j in range(1, nx):
        total = total + q_recv[j]
    p_send[...] = total
    for o in far_first(nz):
        j = lax.rem(z + o, nz)
        send_known(p_send.at[j], p_recv.at[z], p_ss, p_rs, (e, (x_at * nz + j) * nc + core), o == 0)

    lax.fori_loop(groups - 1, groups, mesh_part, 0)

    bulk_wait(p_recv, p_rs)
    r_send[...] = jnp.sum(p_recv[...], axis=0) * normalizer
    for o in far_first(members):
        send_known(r_send, r_recv.at[e], r_ss, r_rs, (lax.rem(e + o, members), g), o == 0)
    bulk_wait(d_recv, d_rs)
    acc = d_recv[0].astype(jnp.float32)
    for j in range(1, nz):
        acc = acc + d_recv[j].astype(jnp.float32)
    mesh_out[...] = acc.astype(jnp.bfloat16)
    bulk_wait(r_recv, r_rs)
    for m in range(members):
        gw_out[share * m : share * (m + 1), :] = r_recv[m]

    bulk_wait(x_send.at[pl.ds(0, members - 1)], x_ss)
    bulk_wait(g_send.at[pl.ds(0, members - 1)], g_ss)
    bulk_wait(out_buf.at[:, pl.ds(0, nu - 1)], m_ss)
    bulk_wait(d_send.at[pl.ds(0, nz - 1)], d_ss)
    half.wait_send()
    bulk_wait(y_send.at[pl.ds(0, members - 1)], y_ss)
    bulk_wait(q_recv.at[pl.ds(0, nx - 1)], q_ss)
    bulk_wait(p_send.at[pl.ds(0, nz - 1)], p_ss)
    bulk_wait(r_recv.at[pl.ds(0, members - 1)], r_ss)


def finish_kernel(gw_ref, mesh_ref, wt_ref, gw_out, mesh_out):
    variables, latent = wt_ref.shape
    gw_out[...] = gw_ref[:, 0:variables]
    whole = variables // 16 * 16
    wide = jnp.concatenate(
        [wt_ref[whole:variables, :], jnp.zeros((whole + 16 - variables, latent), jnp.bfloat16)], axis=0
    )
    total = jnp.dot(mesh_ref[:, 0:whole], wt_ref[0:whole, :], preferred_element_type=jnp.float32)
    total = total + jnp.dot(mesh_ref[:, whole : whole + 16], wide, preferred_element_type=jnp.float32)
    mesh_out[...] = total.astype(jnp.bfloat16)


def per_device(hidden, weight, target, area_weight, var_weight, edge_owner, edge_row, edge_weight):
    rows = hidden[0]
    points, latent = rows.shape
    variables = weight.shape[1]
    neigh = edge_owner.shape[1]
    members = lax.axis_size("ens")
    owners = lax.axis_size("grid")
    mesh_rows = points // 8
    slab = points // members
    assert slab == LANES and variables < LANES
    capacity = max(2, (5 * points * neigh + 4 * owners - 1) // (4 * owners))
    slots = round_up(capacity, 16)
    grows = round_up(variables, 16)
    assert variables % 16 in range(1, 8)
    nx, nz, nc = grid_shape(owners)
    nu = nx * nc
    share = latent // (owners * members)
    normalizer = 1.0 / math.sqrt(float(points * owners * members))
    f32, bf16, i32 = jnp.float32, jnp.bfloat16, jnp.int32
    hbm = pl.BlockSpec(memory_space=pltpu.HBM)
    vmem = pl.BlockSpec(memory_space=pltpu.VMEM)
    dma = pltpu.SemaphoreType.DMA
    wt = weight.T
    gw, mesh_sum = pl.pallas_call(
        functools.partial(fused_kernel, (variables, slots, share, normalizer)),
        in_specs=[hbm] * 8,
        out_specs=[vmem] * 2,
        out_shape=[
            jax.ShapeDtypeStruct((members * share, LANES), f32),
            jax.ShapeDtypeStruct((mesh_rows, LANES), bf16),
        ],
        scratch_shapes=[
            pltpu.VMEM((points, latent), bf16),
            pltpu.VMEM((variables, latent), bf16),
            pltpu.VMEM((variables, slab), f32),
            pltpu.VMEM((points // LANES, LANES), f32),
            pltpu.VMEM((1, variables), f32),
            pltpu.VMEM((neigh, points), i32),
            pltpu.VMEM((neigh, points), i32),
            pltpu.VMEM((neigh, points), f32),
            pltpu.VMEM((LANES, latent), bf16),
            pltpu.VMEM((latent, LANES), bf16),
            pltpu.VMEM((members, grows, slab), jnp.int16),
            pltpu.VMEM((members, grows, slab), jnp.int16),
            pltpu.VMEM((members, 16, slab), f32),
            pltpu.VMEM((members, grows, slab), bf16),
            pltpu.VMEM((members, grows, slab), bf16),
            pltpu.VMEM((owners, points), f32),
            pltpu.VMEM((points, 2 * LANES), bf16),
            pltpu.VMEM((owners * slots, points), bf16),
            pltpu.VMEM((min(2, nz) * nu * slots, LANES), bf16),
            pltpu.VMEM((owners * slots, LANES), f32),
            pltpu.VMEM((points, LANES), bf16),
            pltpu.VMEM((nz, nu, slots, LANES), bf16),
            pltpu.VMEM((nz, nu, slots, LANES), bf16),
            pltpu.VMEM((nz, mesh_rows, LANES), bf16),
            pltpu.VMEM((nz, mesh_rows, LANES), bf16),
            pltpu.VMEM((nx * nz, nc, members * share, LANES), f32),
            pltpu.VMEM((nx * nz, members * share, LANES), f32),
            pltpu.VMEM((members, nx * nz, share, LANES), f32),
            pltpu.VMEM((members, nx * nz, share, LANES), f32),
            pltpu.VMEM((LANES, LANES), f32),
            pltpu.VMEM((nx, nz, share, LANES), f32),
            pltpu.VMEM((nx, nz, share, LANES), f32),
            pltpu.VMEM((nz, share, LANES), f32),
            pltpu.VMEM((nz, share, LANES), f32),
            pltpu.VMEM((share, LANES), f32),
            pltpu.VMEM((members, share, LANES), f32),
            dma((7 + points // (2 * slab),)),
            dma(()), dma(()), dma(()), dma(()), dma(()), dma((nz,)), dma(()), dma(()),
            dma(()), dma(()), dma(()), dma(()), dma(()), dma(()), dma(()), dma(()), dma(()), dma(()),
        ],
        compiler_params=pltpu.CompilerParams(
            collective_id=0, has_side_effects=True, vmem_limit_bytes=VMEM_LIMIT
        ),
    )(
        rows, wt, target, area_weight.reshape(points // LANES, LANES), var_weight.reshape(1, variables),
        edge_owner.T, edge_row.T, edge_weight.T,
    )
    grad_weight, mesh_grad = pl.pallas_call(
        finish_kernel,
        in_specs=[vmem] * 3,
        out_specs=[vmem] * 2,
        out_shape=[
            jax.ShapeDtypeStruct((members * share, variables), f32),
            jax.ShapeDtypeStruct((mesh_rows, latent), bf16),
        ],
        compiler_params=pltpu.CompilerParams(vmem_limit_bytes=VMEM_LIMIT),
    )(gw, mesh_sum, wt)
    return grad_weight, mesh_grad[None]


def solution(mesh):
    return jax.shard_map(
        per_device,
        mesh=mesh,
        in_specs=(
            P("ens", "grid", None),
            P(),
            P(None, "grid"),
            P("grid"),
            P(),
            P("grid", None),
            P("grid", None),
            P("grid", None),
        ),
        out_specs=(P("grid", None), P("ens", "grid", None)),
        check_vma=False,
    )
```
